512 devices in a mesh: gx: 8 (over x, core), gy: 8 (over z_lo), gz: 8 (over z_hi, y).
Axes of the slice: x: 4, y: 4, z: 16 (z_hi: 2, z_lo: 8; z = z_hi * 8 + z_lo), core: 2. Of those that a mesh axis runs over, the one named last changes fastest.
Arguments:
- checkpoint: float32 [2, 7, 32, 128, 1024], P(None, None, 'gx', 'gy', 'gz'), may hold values from 0.02 to 0.3
- cotangent: float32 [2, 7, 32, 128, 1024], P(None, None, 'gx', 'gy', 'gz'), may hold values from -6 to 6
- reaction_rate: float32 [32, 128, 1024], P('gx', 'gy', 'gz'), may hold values from 0.2 to 2
- relax_time: float32 [2, 32, 128, 1024], P(None, 'gx', 'gy', 'gz'), may hold values from 0.6 to 1.8
Outputs:
- adjoint_state: float32 [2, 7, 32, 128, 1024], P(None, None, 'gx', 'gy', 'gz')
- grad_rate: float32 [32, 128, 1024], P('gx', 'gy', 'gz')
- grad_relax: float32 [2, 32, 128, 1024], P(None, 'gx', 'gy', 'gz')
The draws below stay inside these ranges and needn't reach their ends.
All inputs are finite; a program needn't handle non-finite values.
Results may differ from the reference program's by a relative error of at most 0.00002.
Values sent between devices are 32-bit elements; how exact they have to be, the bound alone decides.
No kernel may reach another device: no remote copies, remote signals or barrier semaphores. Data moves between devices by JAX's collectives and lax.ppermute only.
A program may use at most 64 MiB of HBM per device.

```python
import math
import jax
import jax.numpy as jnp
from jax import lax

NX = 32
NY = 128
NZ = 1024


def block_levels(own_key, extent, split, least, high):
    loudness = 1.0
    for dim, blocks in split:
        heights = jax.random.uniform(jax.random.fold_in(jax.random.fold_in(own_key, 6), dim), (blocks,), jnp.float32, least / len(split), high / len(split))
        loudness = loudness * jnp.repeat(jnp.exp(heights), extent[dim] // blocks).reshape((-1,) + (1,) * (len(extent) - 1 - dim))
    return loudness


def centred(key, extent, width, limit, cuts=(), kind=jnp.bfloat16):
    values = jax.random.normal(key, extent, jnp.float32) * width
    if len(cuts) > 0:
        values = block_levels(key, extent, cuts, -0.22, 0.18) * values
    return jnp.clip(values, min=-limit, max=limit).astype(kind)


def setup_inputs(seed: int = 0) -> dict:
    key_list = jax.random.split(jax.random.key(seed), 5)
    checkpoint = jnp.clip(0.02 + 0.28 * jax.random.uniform(key_list[0], (2, 7, NX, NY, NZ), jnp.float32) ** block_levels(key_list[0], (2, 7, NX, NY, NZ), ((2, 8), (3, 8), (4, 8)), -0.2, 0.2), 0.02, 0.3)
    cotangent = centred(key_list[1], (2, 7, NX, NY, NZ), 1.0, 6.0, ((2, 8), (3, 8), (4, 8)), jnp.float32)
    reaction_rate = jnp.clip(jnp.exp(math.log(2.0) - 2.3025851 * jax.random.uniform(key_list[2], (NX, NY, NZ), jnp.float32) ** block_levels(key_list[2], (NX, NY, NZ), ((0, 8), (1, 8), (2, 8)), -0.2, 0.2)), 0.2, 2.0)
    relax_time = jnp.clip(jnp.exp(math.log(1.8) - 1.0986122 * jax.random.uniform(key_list[3], (2, NX, NY, NZ), jnp.float32) ** block_levels(key_list[3], (2, NX, NY, NZ), ((1, 8), (2, 8), (3, 8)), -0.2, 0.2)), 0.6, 1.8)
    return {"checkpoint": checkpoint, "cotangent": cotangent, "reaction_rate": reaction_rate, "relax_time": relax_time}


WEIGHTS = (0.25, 0.125, 0.125, 0.125, 0.125, 0.125, 0.125)
OFFSETS = ((0, 0, 0), (1, 0, 0), (-1, 0, 0), (0, 1, 0), (0, -1, 0), (0, 0, 1), (0, 0, -1))

def collide(state, reaction_rate, relax_time):
    weight_row = jnp.asarray(WEIGHTS, state.dtype).reshape(1, 7, 1, 1, 1)
    density = lax.optimization_barrier(jnp.sum(state, axis=1))
    reaction = reaction_rate * density[0] * density[1]
    source = jnp.stack([-reaction, reaction])
    inverse = 1.0 / relax_time
    balance = weight_row * density[:, None]
    return state - (state - balance) * inverse[:, None] + weight_row * source[:, None]

def stream(state):
    moved = []
    for member in range(7):
        offset = OFFSETS[member]
        moved.append(jnp.roll(state[:, member], offset, axis=(1, 2, 3)))
    return jnp.stack(moved, axis=1)

def forward(state, reaction_rate, relax_time):
    middle = stream(collide(state, reaction_rate, relax_time))
    return stream(collide(middle, reaction_rate, relax_time))

def reference(checkpoint, cotangent, reaction_rate, relax_time):
    finished, pullback = jax.vjp(forward, checkpoint, reaction_rate, relax_time)
    adjoint_state, grad_rate, grad_relax = pullback(cotangent)
    return (adjoint_state, grad_rate, grad_relax)
```

```python
import functools

import jax
import jax.numpy as jnp
from jax import lax
from jax.experimental import pallas as pl
from jax.experimental.pallas import tpu as pltpu
from jax.sharding import PartitionSpec as P

WEIGHTS = (0.25, 0.125, 0.125, 0.125, 0.125, 0.125, 0.125)
AXES = ("gx", "gy", "gz")


def partner(index, count, color):
    if color == 0:
        return index ^ 1
    return (index + 1) % count if index % 2 else (index - 1) % count


def axis_pairs(axis, color):
    count = lax.axis_size(axis)
    return [(i, partner(i, count, color)) for i in range(count)]


def cross_pairs(color):
    nx, ny, nz = (lax.axis_size(a) for a in AXES)
    pairs = []
    for x in range(nx):
        for y in range(ny):
            for z in range(nz):
                if x % 2 == 0:
                    to = (x * ny + partner(y, ny, color)) * nz + z
                else:
                    to = (x * ny + y) * nz + partner(z, nz, color)
                pairs.append(((x * ny + y) * nz + z, to))
    return pairs


def parities():
    return tuple(lax.rem(lax.axis_index(a), 2) == 0 for a in AXES)


def load(ref, *lead):
    return [ref[lead + (x,)] for x in range(ref.shape[len(lead)])]


def total(terms):
    out = terms[0]
    for t in terms[1:]:
        out = out + t
    return out


def collided(f_ref, r_ref, t_ref):
    nx = r_ref.shape[0]
    rate = load(r_ref)
    inverse = [[1.0 / t for t in load(t_ref, s)] for s in range(2)]
    f = [[load(f_ref, s, q) for q in range(7)] for s in range(2)]
    rho = [[total([f[s][q][x] for q in range(7)]) for x in range(nx)] for s in range(2)]
    c = [[[None] * nx for _ in range(7)] for _ in range(2)]
    for x in range(nx):
        reaction = rate[x] * rho[0][x] * rho[1][x]
        for s in range(2):
            source = reaction if s == 1 else -reaction
            for q in range(7):
                w = WEIGHTS[q]
                v = f[s][q][x]
                c[s][q][x] = v - (v - w * rho[s][x]) * inverse[s][x] + w * source
    return c, rho, inverse, rate


def pack_x(fields, last):
    return [v[-1] if last else v[0] for v in fields]


def pack_y(fields, last):
    rows = []
    for v in fields:
        for plane in v:
            n = plane.shape[0]
            rows.append(plane[n - 1 : n] if last else plane[0:1])
    return jnp.concatenate(rows, axis=0)


def pack_z(fields, last):
    lane = lax.broadcasted_iota(jnp.int32, (8, 128), 1)
    out = jnp.zeros((8, 128), jnp.float32)
    j = 0
    for v in fields:
        for plane in v:
            for h in range(plane.shape[0] // 8):
                part = plane[8 * h : 8 * h + 8]
                shift = (j + 1) % 128 if last else j
                moved = pltpu.roll(part, shift, axis=1) if shift else part
                out = jnp.where(lane == j, moved, out)
                j += 1
    return out


def faces(up, down, even):
    out = []
    for axis, pack in enumerate((pack_x, pack_y, pack_z)):
        a, b = pack(up[axis], True), pack(down[axis], False)
        if axis == 0:
            first = [jnp.where(even[0], u, d) for u, d in zip(a, b)]
            second = [jnp.where(even[0], d, u) for u, d in zip(a, b)]
        else:
            first, second = jnp.where(even[axis], a, b), jnp.where(even[axis], b, a)
        out.append((first, second))
    return out


def store_faces(packed, even, s_ref, own0_ref, own1_ref, x_ref):
    (x0, x1), (y0, y1), (z0, z1) = packed
    for k in range(len(x0)):
        s_ref[16 * k : 16 * k + 16] = x0[k]
        x_ref[16 * k : 16 * k + 16] = x1[k]
    base = 16 * len(x0)
    rows = y0.shape[0]
    if rows > 8:
        pad = jnp.zeros((rows - 8, 128), jnp.float32)
        z0, z1 = jnp.concatenate([z0, pad], axis=0), jnp.concatenate([z1, pad], axis=0)
    own0_ref[...] = jnp.where(even[0], y0, z0)
    own1_ref[...] = jnp.where(even[0], y1, z1)
    s_ref[base : base + rows] = jnp.where(even[0], z0, y0)
    s_ref[base + rows : base + 2 * rows] = jnp.where(even[0], z1, y1)


def load_faces(count, even, s_ref, x_ref, c0_ref, c1_ref, t_ref):
    rows = 4 * count
    x0 = [s_ref[16 * k : 16 * k + 16] for k in range(count)]
    x1 = [x_ref[16 * k : 16 * k + 16] for k in range(count)]
    mine0, mine1 = c0_ref[0:rows], c1_ref[0:rows]
    other0, other1 = t_ref[0:rows], t_ref[rows : 2 * rows]
    y0, y1 = jnp.where(even[0], mine0, other0), jnp.where(even[0], mine1, other1)
    z0 = jnp.where(even[0], other0[0:8], mine0[0:8])
    z1 = jnp.where(even[0], other1[0:8], mine1[0:8])
    above = [[jnp.where(even[0], u, d) for u, d in zip(x0, x1)]]
    below = [[jnp.where(even[0], d, u) for u, d in zip(x0, x1)]]
    for axis, (u, d) in ((1, (y0, y1)), (2, (z0, z1))):
        above.append(jnp.where(even[axis], u, d))
        below.append(jnp.where(even[axis], d, u))
    return above, below


def moved(v, axis, sign, halo, k):
    if axis == 0:
        return v[1:] + [halo[k]] if sign > 0 else [halo[k]] + v[:-1]
    nx, (n, lanes) = len(v), v[0].shape
    out = []
    for x in range(nx):
        plane = v[x]
        if axis == 1:
            row = lax.broadcasted_iota(jnp.int32, (n, lanes), 0)
            edge = halo[k * nx + x : k * nx + x + 1]
            rolled = pltpu.roll(plane, n - 1 if sign > 0 else 1, axis=0)
            out.append(jnp.where(row == (n - 1 if sign > 0 else 0), edge, rolled))
        else:
            lane = lax.broadcasted_iota(jnp.int32, (n, lanes), 1)
            parts = []
            for h in range(n // 8):
                j = (k * nx + x) * (n // 8) + h
                shift = (lanes - 1 - j) % lanes if sign > 0 else (lanes - j) % lanes
                parts.append(pltpu.roll(halo, shift, axis=1) if shift else halo)
            edge = jnp.concatenate(parts, axis=0)
            rolled = pltpu.roll(plane, lanes - 1 if sign > 0 else 1, axis=1)
            out.append(jnp.where(lane == (lanes - 1 if sign > 0 else 0), edge, rolled))
    return out


def first_kernel(f_ref, g_ref, r_ref, t_ref, s_ref, own0_ref, own1_ref, x_ref):
    even = parities()
    c, _, _, _ = collided(f_ref, r_ref, t_ref)
    up, down = [], []
    for axis in range(3):
        plus, minus = 1 + 2 * axis, 2 + 2 * axis
        up.append([load(g_ref, 0, minus), load(g_ref, 1, minus), c[0][plus], c[1][plus]])
        down.append([load(g_ref, 0, plus), load(g_ref, 1, plus), c[0][minus], c[1][minus]])
    store_faces(faces(up, down, even), even, s_ref, own0_ref, own1_ref, x_ref)


def adjoint(upstream, state, rho, inverse, rate):
    moments = [total([WEIGHTS[q] * upstream[s][q] for q in range(7)]) for s in range(2)]
    contrast = moments[1] - moments[0]
    scaled = rate * contrast
    earlier, relax = [], []
    for s in range(2):
        keep = 1.0 - inverse[s]
        add = moments[s] * inverse[s] + scaled * rho[1 - s]
        earlier.append([keep * upstream[s][q] + add for q in range(7)])
        part = total([upstream[s][q] * (state[s][q] - WEIGHTS[q] * rho[s]) for q in range(7)])
        relax.append(part * inverse[s] * inverse[s])
    return earlier, rho[0] * rho[1] * contrast, relax


def second_kernel(
    f_ref, g_ref, r_ref, t_ref, sr_ref, xr_ref, c0_ref, c1_ref, tr_ref,
    later_ref, rate_ref, relax_ref, s_ref, own0_ref, own1_ref, x_ref,
):
    even = parities()
    nx = r_ref.shape[0]
    c, _, inverse, rate = collided(f_ref, r_ref, t_ref)
    above, below = load_faces(4, even, sr_ref, xr_ref, c0_ref, c1_ref, tr_ref)
    upstream = [[load(g_ref, s, 0)] for s in range(2)]
    middle = [[c[s][0]] for s in range(2)]
    for s in range(2):
        for axis in range(3):
            plus, minus = 1 + 2 * axis, 2 + 2 * axis
            upstream[s].append(moved(load(g_ref, s, plus), axis, 1, above[axis], s))
            upstream[s].append(moved(load(g_ref, s, minus), axis, -1, below[axis], s))
            middle[s].append(moved(c[s][plus], axis, -1, below[axis], 2 + s))
            middle[s].append(moved(c[s][minus], axis, 1, above[axis], 2 + s))
    later = [[[None] * nx for _ in range(7)] for _ in range(2)]
    for x in range(nx):
        up = [[upstream[s][q][x] for q in range(7)] for s in range(2)]
        mid = [[middle[s][q][x] for q in range(7)] for s in range(2)]
        rho = [total(mid[s]) for s in range(2)]
        earlier, rate_part, relax_part = adjoint(up, mid, rho, [inverse[s][x] for s in range(2)], rate[x])
        rate_ref[x] = rate_part
        for s in range(2):
            relax_ref[s, x] = relax_part[s]
            for q in range(7):
                later[s][q][x] = earlier[s][q]
                later_ref[s, q, x] = earlier[s][q]
    up = [[later[s][2 + 2 * axis] for s in range(2)] for axis in range(3)]
    down = [[later[s][1 + 2 * axis] for s in range(2)] for axis in range(3)]
    store_faces(faces(up, down, even), even, s_ref, own0_ref, own1_ref, x_ref)


def third_kernel(
    f_ref, r_ref, t_ref, later_ref, rate_late_ref, relax_late_ref, sr_ref, xr_ref, c0_ref, c1_ref, tr_ref,
    state_ref, rate_ref, relax_ref,
):
    even = parities()
    nx = r_ref.shape[0]
    above, below = load_faces(2, even, sr_ref, xr_ref, c0_ref, c1_ref, tr_ref)
    upstream = [[load(later_ref, s, 0)] for s in range(2)]
    for s in range(2):
        for axis in range(3):
            upstream[s].append(moved(load(later_ref, s, 1 + 2 * axis), axis, 1, above[axis], s))
            upstream[s].append(moved(load(later_ref, s, 2 + 2 * axis), axis, -1, below[axis], s))
    for x in range(nx):
        up = [[upstream[s][q][x] for q in range(7)] for s in range(2)]
        state = [[f_ref[s, q, x] for q in range(7)] for s in range(2)]
        rho = [total(state[s]) for s in range(2)]
        inverse = [1.0 / t_ref[s, x] for s in range(2)]
        earlier, rate_part, relax_part = adjoint(up, state, rho, inverse, r_ref[x])
        rate_ref[x] = rate_late_ref[x] + rate_part
        for s in range(2):
            relax_ref[s, x] = relax_late_ref[s, x] + relax_part[s]
            for q in range(7):
                state_ref[s, q, x] = earlier[s][q]


def call(kernel, shapes, *args):
    return pl.pallas_call(
        kernel,
        out_shape=[jax.ShapeDtypeStruct(s, jnp.float32) for s in shapes],
        in_specs=[pl.BlockSpec(memory_space=pltpu.VMEM)] * len(args),
        out_specs=[pl.BlockSpec(memory_space=pltpu.VMEM)] * len(shapes),
        compiler_params=pltpu.CompilerParams(vmem_limit_bytes=32 * 1024 * 1024),
    )(*args)


def exchange(rows, s, own0, own1, x):
    base = s.shape[0] - 2 * rows
    s_in = lax.ppermute(s, "gx", axis_pairs("gx", 0))
    far = jnp.concatenate([own1, s_in[base + rows :]], axis=0)
    near = jnp.concatenate([own0, s_in[base : base + rows]], axis=0)
    far_in = lax.ppermute(far, AXES, cross_pairs(1))
    near_in = lax.ppermute(near, AXES, cross_pairs(0))
    x_in = lax.ppermute(x, "gx", axis_pairs("gx", 1))
    back = jnp.concatenate([near_in[rows:], far_in[rows:]], axis=0)
    back_in = lax.ppermute(back, "gx", axis_pairs("gx", 0))
    return s_in, x_in, near_in, far_in, back_in


def message_shapes(count):
    return [(16 * count + 8 * count, 128), (4 * count, 128), (4 * count, 128), (16 * count, 128)]


def on_device(checkpoint, cotangent, reaction_rate, relax_time):
    sent = call(first_kernel, message_shapes(4), checkpoint, cotangent, reaction_rate, relax_time)
    received = exchange(16, *sent)
    later, rate_late, relax_late, *sent = call(
        second_kernel,
        [checkpoint.shape, reaction_rate.shape, relax_time.shape] + message_shapes(2),
        checkpoint, cotangent, reaction_rate, relax_time, *received,
    )
    received = exchange(8, *sent)
    return tuple(
        call(
            third_kernel,
            [checkpoint.shape, reaction_rate.shape, relax_time.shape],
            checkpoint, reaction_rate, relax_time, later, rate_late, relax_late, *received,
        )
    )


def solution(mesh):
    placed = (
        P(None, None, "gx", "gy", "gz"),
        P(None, None, "gx", "gy", "gz"),
        P("gx", "gy", "gz"),
        P(None, "gx", "gy", "gz"),
    )
    return jax.shard_map(
        on_device,
        mesh=mesh,
        in_specs=placed,
        out_specs=(P(None, None, "gx", "gy", "gz"), P("gx", "gy", "gz"), P(None, "gx", "gy", "gz")),
        check_vma=False,
    )
```

```python
import functools

import jax
import jax.numpy as jnp
from jax import lax
from jax.experimental import pallas as pl
from jax.experimental.pallas import tpu as pltpu
from jax.sharding import PartitionSpec as P

WEIGHTS = (0.25, 0.125, 0.125, 0.125, 0.125, 0.125, 0.125)
AXES = ("gx", "gy", "gz")


def partner(index, count, color):
    if color == 0:
        return index ^ 1
    return (index + 1) % count if index % 2 else (index - 1) % count


def axis_pairs(axis, color):
    count = lax.axis_size(axis)
    return [(i, partner(i, count, color)) for i in range(count)]


def cross_pairs(color):
    nx, ny, nz = (lax.axis_size(a) for a in AXES)
    pairs = []
    for x in range(nx):
        for y in range(ny):
            for z in range(nz):
                if x % 2 == 0:
                    to = (x * ny + partner(y, ny, color)) * nz + z
                else:
                    to = (x * ny + y) * nz + partner(z, nz, color)
                pairs.append(((x * ny + y) * nz + z, to))
    return pairs


def parities():
    return tuple(lax.rem(lax.axis_index(a), 2) == 0 for a in AXES)


def load(ref, *lead):
    return [ref[lead + (x,)] for x in range(ref.shape[len(lead)])]


def total(terms):
    out = terms[0]
    for t in terms[1:]:
        out = out + t
    return out


def collided(f_ref, r_ref, t_ref):
    nx = r_ref.shape[0]
    rate = load(r_ref)
    inverse = [[1.0 / t for t in load(t_ref, s)] for s in range(2)]
    f = [[load(f_ref, s, q) for q in range(7)] for s in range(2)]
    rho = [[total([f[s][q][x] for q in range(7)]) for x in range(nx)] for s in range(2)]
    c = [[[None] * nx for _ in range(7)] for _ in range(2)]
    for x in range(nx):
        reaction = rate[x] * rho[0][x] * rho[1][x]
        for s in range(2):
            source = reaction if s == 1 else -reaction
            for q in range(7):
                w = WEIGHTS[q]
                v = f[s][q][x]
                c[s][q][x] = v - (v - w * rho[s][x]) * inverse[s][x] + w * source
    return c, rho, inverse, rate


def pack_x(fields, last):
    return [v[-1] if last else v[0] for v in fields]


def pack_y(fields, last):
    rows = []
    for v in fields:
        for plane in v:
            n = plane.shape[0]
            rows.append(plane[n - 1 : n] if last else plane[0:1])
    return jnp.concatenate(rows, axis=0)


def pack_z(fields, last):
    lane = lax.broadcasted_iota(jnp.int32, (8, 128), 1)
    out = jnp.zeros((8, 128), jnp.float32)
    j = 0
    for v in fields:
        for plane in v:
            for h in range(plane.shape[0] // 8):
                part = plane[8 * h : 8 * h + 8]
                shift = (j + 1) % 128 if last else j
                moved = pltpu.roll(part, shift, axis=1) if shift else part
                out = jnp.where(lane == j, moved, out)
                j += 1
    return out


def store_faces(up, down, even, up_ref, down_ref, own0_ref, own1_ref):
    count = len(up[0])
    for k, (u, d) in enumerate(zip(pack_x(up[0], True), pack_x(down[0], False))):
        up_ref[16 * k : 16 * k + 16] = u
        down_ref[16 * k : 16 * k + 16] = d
    (y0, y1), (z0, z1) = [
        (jnp.where(even[axis], a, b), jnp.where(even[axis], b, a))
        for axis, a, b in (
            (1, pack_y(up[1], True), pack_y(down[1], False)),
            (2, pack_z(up[2], True), pack_z(down[2], False)),
        )
    ]
    base, rows = 16 * count, y0.shape[0]
    if rows > 8:
        pad = jnp.zeros((rows - 8, 128), jnp.float32)
        z0, z1 = jnp.concatenate([z0, pad], axis=0), jnp.concatenate([z1, pad], axis=0)
    own0_ref[...] = jnp.where(even[0], y0, z0)
    own1_ref[...] = jnp.where(even[0], y1, z1)
    for ref in (up_ref, down_ref):
        ref[base : base + rows] = jnp.where(even[0], z0, y0)
        ref[base + rows : base + 2 * rows] = jnp.where(even[0], z1, y1)


def load_faces(count, even, below_ref, above_ref, c1_ref, c0_ref, t_ref):
    rows = 4 * count
    mine0, mine1 = c0_ref[0:rows], c1_ref[0:rows]
    other0, other1 = t_ref[0:rows], t_ref[rows : 2 * rows]
    y0, y1 = jnp.where(even[0], mine0, other0), jnp.where(even[0], mine1, other1)
    z0 = jnp.where(even[0], other0[0:8], mine0[0:8])
    z1 = jnp.where(even[0], other1[0:8], mine1[0:8])
    above = [[above_ref[16 * k : 16 * k + 16] for k in range(count)]]
    below = [[below_ref[16 * k : 16 * k + 16] for k in range(count)]]
    for axis, (u, d) in ((1, (y0, y1)), (2, (z0, z1))):
        above.append(jnp.where(even[axis], u, d))
        below.append(jnp.where(even[axis], d, u))
    return above, below


def forward_kernel(own0_ref, own1_ref, below_ref, above_ref, far_ref, near_ref):
    even = parities()
    rows = own0_ref.shape[0]
    base = above_ref.shape[0] - 2 * rows
    for own, out, at in ((own0_ref, near_ref, base), (own1_ref, far_ref, base + rows)):
        out[0:rows] = own[...]
        out[rows : 2 * rows] = jnp.where(even[0], above_ref[at : at + rows], below_ref[at : at + rows])


def back_kernel(far_ref, near_ref, out_ref):
    rows = near_ref.shape[0] // 2
    out_ref[0:rows] = near_ref[rows : 2 * rows]
    out_ref[rows : 2 * rows] = far_ref[rows : 2 * rows]


def moved(v, axis, sign, halo, k):
    if axis == 0:
        return v[1:] + [halo[k]] if sign > 0 else [halo[k]] + v[:-1]
    nx, (n, lanes) = len(v), v[0].shape
    out = []
    for x in range(nx):
        plane = v[x]
        if axis == 1:
            row = lax.broadcasted_iota(jnp.int32, (n, lanes), 0)
            edge = halo[k * nx + x : k * nx + x + 1]
            rolled = pltpu.roll(plane, n - 1 if sign > 0 else 1, axis=0)
            out.append(jnp.where(row == (n - 1 if sign > 0 else 0), edge, rolled))
        else:
            lane = lax.broadcasted_iota(jnp.int32, (n, lanes), 1)
            parts = []
            for h in range(n // 8):
                j = (k * nx + x) * (n // 8) + h
                shift = (lanes - 1 - j) % lanes if sign > 0 else (lanes - j) % lanes
                parts.append(pltpu.roll(halo, shift, axis=1) if shift else halo)
            edge = jnp.concatenate(parts, axis=0)
            rolled = pltpu.roll(plane, lanes - 1 if sign > 0 else 1, axis=1)
            out.append(jnp.where(lane == (lanes - 1 if sign > 0 else 0), edge, rolled))
    return out


def first_kernel(f_hbm, g_hbm, r_hbm, t_hbm, f_ref, g_ref, r_ref, t_ref, up_ref, down_ref, own0_ref, own1_ref, sems):
    copies = [
        pltpu.make_async_copy(a, b, sems.at[i])
        for i, (a, b) in enumerate(((f_hbm, f_ref), (g_hbm, g_ref), (r_hbm, r_ref), (t_hbm, t_ref)))
    ]
    for copy in copies:
        copy.start()
    for copy in copies:
        copy.wait()
    even = parities()
    c, _, _, _ = collided(f_ref, r_ref, t_ref)
    up, down = [], []
    for axis in range(3):
        plus, minus = 1 + 2 * axis, 2 + 2 * axis
        up.append([load(g_ref, 0, minus), load(g_ref, 1, minus), c[0][plus], c[1][plus]])
        down.append([load(g_ref, 0, plus), load(g_ref, 1, plus), c[0][minus], c[1][minus]])
    store_faces(up, down, even, up_ref, down_ref, own0_ref, own1_ref)


def adjoint(upstream, state, rho, inverse, rate):
    moments = [total([WEIGHTS[q] * upstream[s][q] for q in range(7)]) for s in range(2)]
    contrast = moments[1] - moments[0]
    scaled = rate * contrast
    earlier, relax = [], []
    for s in range(2):
        keep = 1.0 - inverse[s]
        add = moments[s] * inverse[s] + scaled * rho[1 - s]
        earlier.append([keep * upstream[s][q] + add for q in range(7)])
        part = total([upstream[s][q] * (state[s][q] - WEIGHTS[q] * rho[s]) for q in range(7)])
        relax.append(part * inverse[s] * inverse[s])
    return earlier, rho[0] * rho[1] * contrast, relax


def second_kernel(
    f_ref, g_ref, r_ref, t_ref, below_ref, above_ref, c1_ref, c0_ref, tr_ref,
    later_ref, rate_ref, relax_ref, up_ref, down_ref, own0_ref, own1_ref,
):
    even = parities()
    nx = r_ref.shape[0]
    c, _, inverse, rate = collided(f_ref, r_ref, t_ref)
    above, below = load_faces(4, even, below_ref, above_ref, c1_ref, c0_ref, tr_ref)
    upstream = [[load(g_ref, s, 0)] for s in range(2)]
    middle = [[c[s][0]] for s in range(2)]
    for s in range(2):
        for axis in range(3):
            plus, minus = 1 + 2 * axis, 2 + 2 * axis
            upstream[s].append(moved(load(g_ref, s, plus), axis, 1, above[axis], s))
            upstream[s].append(moved(load(g_ref, s, minus), axis, -1, below[axis], s))
            middle[s].append(moved(c[s][plus], axis, -1, below[axis], 2 + s))
            middle[s].append(moved(c[s][minus], axis, 1, above[axis], 2 + s))
    later = [[[None] * nx for _ in range(7)] for _ in range(2)]
    for x in range(nx):
        up = [[upstream[s][q][x] for q in range(7)] for s in range(2)]
        mid = [[middle[s][q][x] for q in range(7)] for s in range(2)]
        rho = [total(mid[s]) for s in range(2)]
        earlier, rate_part, relax_part = adjoint(up, mid, rho, [inverse[s][x] for s in range(2)], rate[x])
        rate_ref[x] = rate_part
        for s in range(2):
            relax_ref[s, x] = relax_part[s]
            for q in range(7):
                later[s][q][x] = earlier[s][q]
                later_ref[s, q, x] = earlier[s][q]
    up = [[later[s][2 + 2 * axis] for s in range(2)] for axis in range(3)]
    down = [[later[s][1 + 2 * axis] for s in range(2)] for axis in range(3)]
    store_faces(up, down, even, up_ref, down_ref, own0_ref, own1_ref)


def third_kernel(
    f_ref, r_ref, t_ref, later_ref, rate_late_ref, relax_late_ref, below_ref, above_ref, c1_ref, c0_ref, tr_ref,
    state_ref, rate_ref, relax_ref,
):
    even = parities()
    nx = r_ref.shape[0]
    above, below = load_faces(2, even, below_ref, above_ref, c1_ref, c0_ref, tr_ref)
    upstream = [[load(later_ref, s, 0)] for s in range(2)]
    for s in range(2):
        for axis in range(3):
            upstream[s].append(moved(load(later_ref, s, 1 + 2 * axis), axis, 1, above[axis], s))
            upstream[s].append(moved(load(later_ref, s, 2 + 2 * axis), axis, -1, below[axis], s))
    for x in range(nx):
        up = [[upstream[s][q][x] for q in range(7)] for s in range(2)]
        state = [[f_ref[s, q, x] for q in range(7)] for s in range(2)]
        rho = [total(state[s]) for s in range(2)]
        inverse = [1.0 / t_ref[s, x] for s in range(2)]
        earlier, rate_part, relax_part = adjoint(up, state, rho, inverse, r_ref[x])
        rate_ref[x] = rate_late_ref[x] + rate_part
        for s in range(2):
            relax_ref[s, x] = relax_late_ref[s, x] + relax_part[s]
            for q in range(7):
                state_ref[s, q, x] = earlier[s][q]


def call(kernel, shapes, *args, source=pltpu.VMEM, scratch=()):
    return pl.pallas_call(
        kernel,
        out_shape=[jax.ShapeDtypeStruct(s, jnp.float32) for s in shapes],
        in_specs=[pl.BlockSpec(memory_space=source)] * len(args),
        out_specs=[pl.BlockSpec(memory_space=pltpu.VMEM)] * len(shapes),
        scratch_shapes=list(scratch),
        compiler_params=pltpu.CompilerParams(vmem_limit_bytes=32 * 1024 * 1024),
    )(*args)


def shifts(axis):
    count = lax.axis_size(axis)
    up = [(i, (i + 1) % count) for i in range(count)]
    return up, [(j, i) for i, j in up]


def exchange(up, down, own0, own1):
    to_up, to_down = shifts("gx")
    below = lax.ppermute(up, "gx", to_up)
    above = lax.ppermute(down, "gx", to_down)
    both = (2 * own0.shape[0], 128)
    far, near = call(forward_kernel, [both, both], own0, own1, below, above)
    far_in = lax.ppermute(far, AXES, cross_pairs(1))
    near_in = lax.ppermute(near, AXES, cross_pairs(0))
    (back,) = call(back_kernel, [both], far_in, near_in)
    back_in = lax.ppermute(back, "gx", axis_pairs("gx", 0))
    return below, above, far_in, near_in, back_in


def message_shapes(count):
    return [(24 * count, 128), (24 * count, 128), (4 * count, 128), (4 * count, 128)]


def on_device(checkpoint, cotangent, reaction_rate, relax_time):
    inputs = (checkpoint, cotangent, reaction_rate, relax_time)
    f, g, r, t, *sent = call(
        first_kernel, [a.shape for a in inputs] + message_shapes(4),
        *(pltpu.with_memory_space_constraint(a, pltpu.HBM) for a in inputs),
        source=pltpu.HBM, scratch=[pltpu.SemaphoreType.DMA((4,))],
    )
    received = exchange(*sent)
    later, rate_late, relax_late, *sent = call(
        second_kernel, [f.shape, r.shape, t.shape] + message_shapes(2), f, g, r, t, *received
    )
    received = exchange(*sent)
    return tuple(
        call(third_kernel, [f.shape, r.shape, t.shape], f, r, t, later, rate_late, relax_late, *received)
    )


def solution(mesh):
    placed = (
        P(None, None, "gx", "gy", "gz"),
        P(None, None, "gx", "gy", "gz"),
        P("gx", "gy", "gz"),
        P(None, "gx", "gy", "gz"),
    )
    return jax.shard_map(
        on_device,
        mesh=mesh,
        in_specs=placed,
        out_specs=(P(None, None, "gx", "gy", "gz"), P("gx", "gy", "gz"), P(None, "gx", "gy", "gz")),
        check_vma=False,
    )
```

```python
import jax
import jax.numpy as jnp
from jax import lax
from jax.experimental import pallas as pl
from jax.experimental.pallas import tpu as pltpu
from jax.sharding import PartitionSpec as P

WEIGHTS = (0.25, 0.125, 0.125, 0.125, 0.125, 0.125, 0.125)
AXES = ("gx", "gy", "gz")


def partner(index, count, color):
    if color == 0:
        return index ^ 1
    return (index + 1) % count if index % 2 else (index - 1) % count


def axis_pairs(axis, color):
    count = lax.axis_size(axis)
    return [(i, partner(i, count, color)) for i in range(count)]


def parities():
    return tuple(lax.rem(lax.axis_index(a), 2) == 0 for a in AXES)


def load(ref, *lead):
    return [ref[lead + (x,)] for x in range(ref.shape[len(lead)])]


def total(terms):
    out = terms[0]
    for t in terms[1:]:
        out = out + t
    return out


def collided(f_ref, r_ref, t_ref):
    nx = r_ref.shape[0]
    rate = load(r_ref)
    inverse = [[1.0 / t for t in load(t_ref, s)] for s in range(2)]
    f = [[load(f_ref, s, q) for q in range(7)] for s in range(2)]
    rho = [[total([f[s][q][x] for q in range(7)]) for x in range(nx)] for s in range(2)]
    c = [[[None] * nx for _ in range(7)] for _ in range(2)]
    for x in range(nx):
        reaction = rate[x] * rho[0][x] * rho[1][x]
        for s in range(2):
            source = reaction if s == 1 else -reaction
            for q in range(7):
                w = WEIGHTS[q]
                v = f[s][q][x]
                c[s][q][x] = v - (v - w * rho[s][x]) * inverse[s][x] + w * source
    return c, rho, inverse, rate


def pack_x(fields, last):
    return [v[-1] if last else v[0] for v in fields]


def rows_of(v, i):
    return jnp.concatenate([plane[i : i + 1] for plane in v], axis=0)


def pack_y(fields, last):
    n = fields[0][0].shape[0]
    return jnp.concatenate([rows_of(v, n - 1 if last else 0) for v in fields], axis=0)


def pack_z(fields, last, start=0, out=None):
    lane = lax.broadcasted_iota(jnp.int32, (8, 128), 1)
    out = jnp.zeros((8, 128), jnp.float32) if out is None else out
    j = start
    for v in fields:
        for plane in v:
            for h in range(plane.shape[0] // 8):
                part = plane[8 * h : 8 * h + 8]
                shift = (j + 1) % 128 if last else j
                part = pltpu.roll(part, shift, axis=1) if shift else part
                out = jnp.where(lane == j, part, out)
                j += 1
    return out


def cut(v, axis, sign):
    if axis == 0:
        zero = jnp.zeros_like(v[0])
        return v[1:] + [zero] if sign > 0 else [zero] + v[:-1]
    out = []
    for plane in v:
        n = plane.shape[axis - 1]
        at = lax.broadcasted_iota(jnp.int32, plane.shape, axis - 1)
        rolled = pltpu.roll(plane, n - 1 if sign > 0 else 1, axis=axis - 1)
        out.append(jnp.where(at == (n - 1 if sign > 0 else 0), 0.0, rolled))
    return out


def plus(a, b):
    return [x + y for x, y in zip(a, b)]


def partial_sums(g, c, axes):
    moments, density = [], []
    for s in range(2):
        m = [WEIGHTS[1] * v for v in cut(g[s][1 + 2 * axes[0]], axes[0], 1)]
        d = plus(c[s][0], cut(c[s][1 + 2 * axes[0]], axes[0], -1))
        m = plus(m, [WEIGHTS[1] * v for v in cut(g[s][2 + 2 * axes[0]], axes[0], -1)])
        d = plus(d, cut(c[s][2 + 2 * axes[0]], axes[0], 1))
        m = plus(m, [WEIGHTS[1] * v for v in cut(g[s][1 + 2 * axes[1]], axes[1], 1)])
        d = plus(d, cut(c[s][1 + 2 * axes[1]], axes[1], -1))
        m = plus(m, [WEIGHTS[1] * v for v in cut(g[s][2 + 2 * axes[1]], axes[1], -1)])
        d = plus(d, cut(c[s][2 + 2 * axes[1]], axes[1], 1))
        moments.append(plus(m, [WEIGHTS[0] * v for v in g[s][0]]))
        density.append(d)
    return moments, density


def face_fields(g, c, moments, density, inverse, rate, axis, last):
    out_q, in_q = (1 + 2 * axis, 2 + 2 * axis) if last else (2 + 2 * axis, 1 + 2 * axis)
    sign = -1 if last else 1
    inner = [cut(g[s][in_q], axis, sign) for s in range(2)]
    m = [plus(moments[s], [WEIGHTS[1] * v for v in inner[s]]) for s in range(2)]
    d = [plus(density[s], cut(c[s][out_q], axis, sign)) for s in range(2)]
    return [*inner, *m, *d, *inverse, rate]


def edge_fields(g, c, axis):
    p, m = 1 + 2 * axis, 2 + 2 * axis
    return [(g[0][p], g[0][m]), (g[1][p], g[1][m]), (c[0][m], c[0][p]), (c[1][m], c[1][p])]


def first_kernel(
    f_hbm, g_hbm, r_hbm, t_hbm, f_ref, g_ref, r_ref, t_ref, up_ref, down_ref, own0_ref, own1_ref, diag_ref, raw_ref, sems
):
    copies = [
        pltpu.make_async_copy(a, b, sems.at[i])
        for i, (a, b) in enumerate(((f_hbm, f_ref), (g_hbm, g_ref), (r_hbm, r_ref), (t_hbm, t_ref)))
    ]
    for copy in copies:
        copy.start()
    for copy in copies:
        copy.wait()
    even = parities()
    c, _, inverse, rate = collided(f_ref, r_ref, t_ref)
    g = [[load(g_ref, s, q) for q in range(7)] for s in range(2)]
    up, down = [], []
    for axis in range(3):
        p, m = 1 + 2 * axis, 2 + 2 * axis
        up.append([g[0][m], g[1][m], c[0][p], c[1][p]])
        down.append([g[0][p], g[1][p], c[0][m], c[1][m]])
    for k, (u, d) in enumerate(zip(pack_x(up[0], True), pack_x(down[0], False))):
        up_ref[16 * k : 16 * k + 16] = u
        down_ref[16 * k : 16 * k + 16] = d
    nx, n = len(rate), rate[0].shape[0]
    lane = lax.broadcasted_iota(jnp.int32, (nx, 128), 1)
    row = lax.broadcasted_iota(jnp.int32, (n, 128), 0)
    x_edge, y_edge, z_edge = (edge_fields(g, c, axis) for axis in range(3))
    y_faces, z_faces = [], []
    y_sums, z_sums = partial_sums(g, c, (0, 2)), partial_sums(g, c, (0, 1))
    for last in (False, True):
        i = n - 1 if last else 0
        raw = pack_y((up if last else down)[1], last)
        deep = pack_y(face_fields(g, c, *y_sums, inverse, rate, 1, last), last)
        x_lines = [line for a, b in x_edge for line in (a[0][i : i + 1], b[-1][i : i + 1])]
        x_lines.append(jnp.zeros((28 - 4 * len(rate) - len(x_lines), 128), jnp.float32))
        z_lines = [jnp.where(lane < 64, rows_of(a, i), rows_of(b, i)) for a, b in z_edge]
        y_faces.append((raw, jnp.concatenate([raw, deep, *x_lines], axis=0), jnp.concatenate(z_lines, axis=0)))
        raw = pack_z((up if last else down)[2], last)
        deep = pack_z(face_fields(g, c, *z_sums, inverse, rate, 2, last), last, 32, raw)
        y_lines = [[jnp.where(row < 8, u, v) for u, v in zip(a, b)] for a, b in y_edge]
        x_lines = [a[:-1] + b[-1:] for a, b in x_edge]
        z_faces.append((raw, deep, pack_z(y_lines + x_lines, last)))
    y1, y2 = jnp.where(even[1], y_faces[1][0], y_faces[0][0]), jnp.where(even[1], y_faces[0][0], y_faces[1][0])
    z1, z2 = jnp.where(even[2], z_faces[1][0], z_faces[0][0]), jnp.where(even[2], z_faces[0][0], z_faces[1][0])
    y_deep = jnp.where(even[1], y_faces[0][1], y_faces[1][1])
    y_lines = jnp.where(even[1], y_faces[0][2], y_faces[1][2])
    z_deep = jnp.where(even[2], z_faces[0][1], z_faces[1][1])
    z_lines = jnp.where(even[2], z_faces[0][2], z_faces[1][2])
    raw_ref[0:16] = y2
    raw_ref[16:24] = z2
    diag_ref[0:16] = y_lines
    diag_ref[16:24] = z_lines
    z1 = jnp.concatenate([z1, jnp.zeros_like(z1)], axis=0)
    y_all = jnp.concatenate([y_deep, y_lines], axis=0)
    z_all = jnp.concatenate([z_deep, z_lines, jnp.zeros((y_all.shape[0] - 16, 128), jnp.float32)], axis=0)
    own0_ref[...] = jnp.where(even[0], y1, z1)
    own1_ref[...] = jnp.where(even[0], y_all, z_all)
    for ref in (up_ref, down_ref):
        ref[64:80] = jnp.where(even[0], z1, y1)
        ref[80:160] = jnp.where(even[0], z_all, y_all)


def forward_kernel(own0_ref, own1_ref, below_ref, above_ref, y_ref, z_ref, near_ref):
    even = parities()
    near_ref[0:16] = own0_ref[...]
    near_ref[16:32] = jnp.where(even[0], above_ref[64:80], below_ref[64:80])
    share = jnp.where(even[0], above_ref[80:160], below_ref[80:160])
    y_ref[0:80] = own1_ref[...]
    y_ref[80:160] = share
    z_ref[0:16] = own1_ref[0:16]
    z_ref[16:32] = share[0:16]


def back_kernel(y_ref, z_ref, near_ref, out_ref):
    even = parities()
    out_ref[0:16] = near_ref[16:32]
    out_ref[16:32] = jnp.where(even[0], y_ref[80:96], z_ref[16:32])
    out_ref[32:96] = y_ref[96:160]


def moved(v, axis, sign, halo, k):
    if axis == 0:
        return v[1:] + [halo[k]] if sign > 0 else [halo[k]] + v[:-1]
    nx, (n, lanes) = len(v), v[0].shape
    out = []
    for x in range(nx):
        plane = v[x]
        if axis == 1:
            row = lax.broadcasted_iota(jnp.int32, (n, lanes), 0)
            edge = halo[k * nx + x : k * nx + x + 1]
            rolled = pltpu.roll(plane, n - 1 if sign > 0 else 1, axis=0)
            out.append(jnp.where(row == (n - 1 if sign > 0 else 0), edge, rolled))
        else:
            lane = lax.broadcasted_iota(jnp.int32, (n, lanes), 1)
            parts = []
            for h in range(n // 8):
                j = (k * nx + x) * (n // 8) + h
                shift = (lanes - 1 - j) % lanes if sign > 0 else (lanes - j) % lanes
                parts.append(pltpu.roll(halo, shift, axis=1) if shift else halo)
            edge = jnp.concatenate(parts, axis=0)
            rolled = pltpu.roll(plane, lanes - 1 if sign > 0 else 1, axis=1)
            out.append(jnp.where(lane == (lanes - 1 if sign > 0 else 0), edge, rolled))
    return out


def adjoint(upstream, state, rho, inverse, rate):
    moments = [total([WEIGHTS[q] * upstream[s][q] for q in range(7)]) for s in range(2)]
    contrast = moments[1] - moments[0]
    scaled = rate * contrast
    earlier, relax = [], []
    for s in range(2):
        keep = 1.0 - inverse[s]
        add = moments[s] * inverse[s] + scaled * rho[1 - s]
        earlier.append([keep * upstream[s][q] + add for q in range(7)])
        part = total([upstream[s][q] * (state[s][q] - WEIGHTS[q] * rho[s]) for q in range(7)])
        relax.append(part * inverse[s] * inverse[s])
    return earlier, rho[0] * rho[1] * contrast, relax


def second_kernel(
    f_ref, g_ref, r_ref, t_ref, below_ref, above_ref, y_ref, z_ref, near_ref, back_ref,
    later_ref, rate_ref, relax_ref, deep_ref, up_ref, down_ref, y1_ref, y2_ref, z1_ref, z2_ref,
):
    even = parities()
    nx = r_ref.shape[0]
    c, _, inverse, rate = collided(f_ref, r_ref, t_ref)
    y1 = jnp.where(even[0], near_ref[0:16], back_ref[0:16])
    z1 = jnp.where(even[0], back_ref[0:8], near_ref[0:8])
    y2 = jnp.where(even[0], y_ref[0:80], back_ref[16:96])
    z2 = jnp.where(even[0], back_ref[16:32], z_ref[0:16])
    deep_ref[0:80] = y2
    deep_ref[80:96] = z2
    above = [[above_ref[16 * k : 16 * k + 16] for k in range(4)]]
    below = [[below_ref[16 * k : 16 * k + 16] for k in range(4)]]
    for axis, a, b in ((1, y1, y2[0:16]), (2, z1, z2[0:8])):
        above.append(jnp.where(even[axis], a, b))
        below.append(jnp.where(even[axis], b, a))
    upstream = [[load(g_ref, s, 0)] for s in range(2)]
    middle = [[c[s][0]] for s in range(2)]
    for s in range(2):
        for axis in range(3):
            p, m = 1 + 2 * axis, 2 + 2 * axis
            upstream[s].append(moved(load(g_ref, s, p), axis, 1, above[axis], s))
            upstream[s].append(moved(load(g_ref, s, m), axis, -1, below[axis], s))
            middle[s].append(moved(c[s][p], axis, -1, below[axis], 2 + s))
            middle[s].append(moved(c[s][m], axis, 1, above[axis], 2 + s))
    later = [[[None] * nx for _ in range(7)] for _ in range(2)]
    for x in range(nx):
        up = [[upstream[s][q][x] for q in range(7)] for s in range(2)]
        mid = [[middle[s][q][x] for q in range(7)] for s in range(2)]
        rho = [total(mid[s]) for s in range(2)]
        earlier, rate_part, relax_part = adjoint(up, mid, rho, [inverse[s][x] for s in range(2)], rate[x])
        rate_ref[x] = rate_part
        for s in range(2):
            relax_ref[s, x] = relax_part[s]
            for q in range(7):
                later[s][q][x] = earlier[s][q]
                later_ref[s, q, x] = earlier[s][q]
    for ref, last in ((up_ref, True), (down_ref, False)):
        for s, face in enumerate(pack_x([later[s][2 if last else 1] for s in range(2)], last)):
            ref[16 * s : 16 * s + 16] = face
        ref[32:40] = y2[52:60]
        ref[40:48] = z2[8:16]
    for axis, pack, first, second in ((1, pack_y, y1_ref, y2_ref), (2, pack_z, z1_ref, z2_ref)):
        a = pack([later[s][2 + 2 * axis] for s in range(2)], True)
        b = pack([later[s][1 + 2 * axis] for s in range(2)], False)
        first[0:8] = jnp.where(even[axis], a, b)
        second[0:8] = jnp.where(even[axis], b, a)
    for ref in (y1_ref, y2_ref):
        ref[8:16] = z2[8:16]
    for ref in (z1_ref, z2_ref):
        ref[8:24] = y2[64:80]


def later_beyond(inner, moments, density, inverse, rate):
    scaled = rate * (moments[1] - moments[0])
    return [(1.0 - inverse[s]) * inner[s] + moments[s] * inverse[s] + scaled * density[1 - s] for s in range(2)]


def beyond_y(deep, own, x_above, x_below, z_above, z_below):
    nx = 4
    field = lambda k: deep[16 + nx * k : 16 + nx * k + nx]
    lane = lax.broadcasted_iota(jnp.int32, (nx, 128), 1)
    added = []
    for k in range(4):
        zero = jnp.zeros((nx - 2, 128), jnp.float32)
        x_part = jnp.concatenate([x_below[2 * k + 1 : 2 * k + 2], zero, x_above[2 * k : 2 * k + 1]], axis=0)
        high = pltpu.roll(z_above[nx * k : nx * k + nx], 127, axis=1)
        low = pltpu.roll(z_below[nx * k : nx * k + nx], 1, axis=1)
        z_part = jnp.where(lane == 127, high, jnp.where(lane == 0, low, 0.0))
        added.append(own[nx * k : nx * k + nx] + x_part + z_part)
    moments = [field(2 + s) + WEIGHTS[1] * added[s] for s in range(2)]
    density = [field(4 + s) + added[2 + s] for s in range(2)]
    out = later_beyond([field(0), field(1)], moments, density, [field(6), field(7)], field(8))
    return jnp.concatenate(out, axis=0)


def beyond_z(deep, own, x_above, x_below, y_above, y_below):
    lane = lax.broadcasted_iota(jnp.int32, (8, 128), 1)
    row = lax.broadcasted_iota(jnp.int32, (8, 128), 0)

    def at(v, shift):
        shift = shift % 128
        return pltpu.roll(v, shift, axis=1) if shift else v

    field = lambda k: at(deep, -32 - 8 * k)
    odd = lax.rem(lane, 2) == 1
    y_high, y_low = pltpu.roll(y_above, 7, axis=0), pltpu.roll(y_below, 1, axis=0)
    added = []
    for k in range(4):
        x_part = jnp.where(lane >= 6, at(x_above, 6 - 32 - 8 * k), 0.0)
        x_part = jnp.where(lane < 2, at(x_below, -6 - 32 - 8 * k), x_part)
        y_part = jnp.where((row == 7) & odd, at(y_high, 1 - 8 * k), 0.0)
        y_part = jnp.where((row == 0) & ~odd, at(y_low, -1 - 8 * k), y_part)
        added.append(at(own, -8 * k) + x_part + y_part)
    moments = [field(2 + s) + WEIGHTS[1] * added[s] for s in range(2)]
    density = [field(4 + s) + added[2 + s] for s in range(2)]
    out = later_beyond([field(0), field(1)], moments, density, [field(6), field(7)], field(8))
    return jnp.where(lane < 8, out[0], pltpu.roll(out[1], 8, axis=1))


def third_kernel(
    f_ref, r_ref, t_ref, later_ref, rate_late_ref, relax_late_ref, deep_ref, raw_ref, diag_ref,
    below_ref, above_ref, y1_ref, y2_ref, z1_ref, z2_ref, state_ref, rate_ref, relax_ref,
):
    even = parities()
    nx = r_ref.shape[0]
    far_y = far_along_y(lax.axis_index("gy"), lax.axis_size("gy"))
    far_z = far_along_z(lax.axis_index("gz"), lax.axis_size("gz"))
    lines1, lines2 = z1_ref[8:24], jnp.where(far_z, diag_ref[0:16], z2_ref[8:24])
    y2 = beyond_y(
        deep_ref[0:80], raw_ref[0:16], above_ref[32:40], below_ref[32:40],
        jnp.where(even[2], lines1, lines2), jnp.where(even[2], lines2, lines1),
    )
    lines1, lines2 = y1_ref[8:16], jnp.where(far_y, diag_ref[16:24], y2_ref[8:16])
    z2 = beyond_z(
        deep_ref[80:88], raw_ref[16:24], above_ref[40:48], below_ref[40:48],
        jnp.where(even[1], lines1, lines2), jnp.where(even[1], lines2, lines1),
    )
    y2 = jnp.where(far_y, y2, y2_ref[0:8])
    z2 = jnp.where(far_z, z2, z2_ref[0:8])
    above = [[above_ref[16 * k : 16 * k + 16] for k in range(2)]]
    below = [[below_ref[16 * k : 16 * k + 16] for k in range(2)]]
    for axis, a, b in ((1, y1_ref[0:8], y2), (2, z1_ref[0:8], z2)):
        above.append(jnp.where(even[axis], a, b))
        below.append(jnp.where(even[axis], b, a))
    upstream = [[load(later_ref, s, 0)] for s in range(2)]
    for s in range(2):
        for axis in range(3):
            upstream[s].append(moved(load(later_ref, s, 1 + 2 * axis), axis, 1, above[axis], s))
            upstream[s].append(moved(load(later_ref, s, 2 + 2 * axis), axis, -1, below[axis], s))
    for x in range(nx):
        up = [[upstream[s][q][x] for q in range(7)] for s in range(2)]
        state = [[f_ref[s, q, x] for q in range(7)] for s in range(2)]
        rho = [total(state[s]) for s in range(2)]
        inverse = [1.0 / t_ref[s, x] for s in range(2)]
        earlier, rate_part, relax_part = adjoint(up, state, rho, inverse, r_ref[x])
        rate_ref[x] = rate_late_ref[x] + rate_part
        for s in range(2):
            relax_ref[s, x] = relax_late_ref[s, x] + relax_part[s]
            for q in range(7):
                state_ref[s, q, x] = earlier[s][q]


def call(kernel, shapes, *args, source=pltpu.VMEM, scratch=()):
    return pl.pallas_call(
        kernel,
        out_shape=[jax.ShapeDtypeStruct(s, jnp.float32) for s in shapes],
        in_specs=[pl.BlockSpec(memory_space=source)] * len(args),
        out_specs=[pl.BlockSpec(memory_space=pltpu.VMEM)] * len(shapes),
        scratch_shapes=list(scratch),
        compiler_params=pltpu.CompilerParams(vmem_limit_bytes=32 * 1024 * 1024),
    )(*args)


def shifts(axis):
    count = lax.axis_size(axis)
    up = [(i, (i + 1) % count) for i in range(count)]
    return up, [(j, i) for i, j in up]


def far_along_y(index, count):
    return (index == 0) | (index == count - 1)


def far_along_z(index, count):
    half = count // 2
    return (index % half == 0) | (index % half == half - 1)


def grid_pairs(move):
    counts = tuple(lax.axis_size(a) for a in AXES)
    nx, ny, nz = counts
    pairs = []
    for x in range(nx):
        for y in range(ny):
            for z in range(nz):
                to = move(x, y, z, counts)
                if to is not None:
                    pairs.append(((x * ny + y) * nz + z, (to[0] * ny + to[1]) * nz + to[2]))
    return pairs


def near_move(x, y, z, counts):
    return (x, partner(y, counts[1], 0), z) if x % 2 == 0 else (x, y, partner(z, counts[2], 0))


def second_y_move(x, y, z, counts):
    return (x, partner(y, counts[1], 1), z) if x % 2 == 0 else None


def second_z_move(x, y, z, counts):
    return (x, y, partner(z, counts[2], 1)) if x % 2 == 1 else None


def diagonal_move(x, y, z, counts):
    if far_along_y(y, counts[1]) and far_along_z(z, counts[2]):
        return (x, partner(y, counts[1], 1), partner(z, counts[2], 1))
    return None


def first_exchange(up, down, own0, own1, diag):
    to_up, to_down = shifts("gx")
    below = lax.ppermute(up, "gx", to_up)
    above = lax.ppermute(down, "gx", to_down)
    y, z, near = call(forward_kernel, [(160, 128), (32, 128), (32, 128)], own0, own1, below, above)
    y_in = lax.ppermute(y, AXES, grid_pairs(second_y_move))
    z_in = lax.ppermute(z, AXES, grid_pairs(second_z_move))
    diag_in = lax.ppermute(diag, AXES, grid_pairs(diagonal_move))
    near_in = lax.ppermute(near, AXES, grid_pairs(near_move))
    (back,) = call(back_kernel, [(96, 128)], y_in, z_in, near_in)
    back_in = lax.ppermute(back, "gx", axis_pairs("gx", 0))
    return (below, above, y_in, z_in, near_in, back_in), diag_in


def second_exchange(up, down, y1, y2, z1, z2):
    to_up, to_down = shifts("gx")
    below = lax.ppermute(up, "gx", to_up)
    above = lax.ppermute(down, "gx", to_down)
    received = [below, above]
    for axis, far, a, b in (("gy", far_along_y, y1, y2), ("gz", far_along_z, z1, z2)):
        count = lax.axis_size(axis)
        received.append(lax.ppermute(a, axis, axis_pairs(axis, 0)))
        near = [(i, j) for i, j in axis_pairs(axis, 1) if not far(i, count)]
        received.append(lax.ppermute(b, axis, near))
    return received


def on_device(checkpoint, cotangent, reaction_rate, relax_time):
    inputs = (checkpoint, cotangent, reaction_rate, relax_time)
    messages = [(160, 128), (160, 128), (16, 128), (80, 128), (24, 128), (24, 128)]
    f, g, r, t, *sent, raw = call(
        first_kernel, [a.shape for a in inputs] + messages,
        *(pltpu.with_memory_space_constraint(a, pltpu.HBM) for a in inputs),
        source=pltpu.HBM, scratch=[pltpu.SemaphoreType.DMA((4,))],
    )
    received, diag_in = first_exchange(*sent)
    messages = [(96, 128), (48, 128), (48, 128), (16, 128), (16, 128), (24, 128), (24, 128)]
    later, rate_late, relax_late, deep, *sent = call(
        second_kernel, [f.shape, r.shape, t.shape] + messages, f, g, r, t, *received
    )
    received = second_exchange(*sent)
    return tuple(
        call(
            third_kernel, [f.shape, r.shape, t.shape],
            f, r, t, later, rate_late, relax_late, deep, raw, diag_in, *received,
        )
    )


def solution(mesh):
    placed = (
        P(None, None, "gx", "gy", "gz"),
        P(None, None, "gx", "gy", "gz"),
        P("gx", "gy", "gz"),
        P(None, "gx", "gy", "gz"),
    )
    return jax.shard_map(
        on_device,
        mesh=mesh,
        in_specs=placed,
        out_specs=(P(None, None, "gx", "gy", "gz"), P("gx", "gy", "gz"), P(None, "gx", "gy", "gz")),
        check_vma=False,
    )
```

```python
import jax
import jax.numpy as jnp
from jax import lax
from jax.experimental import pallas as pl
from jax.experimental.pallas import tpu as pltpu
from jax.sharding import PartitionSpec as P

WEIGHTS = (0.25, 0.125, 0.125, 0.125, 0.125, 0.125, 0.125)
AXES = ("gx", "gy", "gz")


def partner(index, count, color):
    if color == 0:
        return index ^ 1
    return (index + 1) % count if index % 2 else (index - 1) % count


def axis_pairs(axis, color):
    count = lax.axis_size(axis)
    return [(i, partner(i, count, color)) for i in range(count)]


def parities():
    return tuple(lax.rem(lax.axis_index(a), 2) == 0 for a in AXES)


def load(ref, *lead):
    return [ref[lead + (x,)] for x in range(ref.shape[len(lead)])]


def total(terms):
    out = terms[0]
    for t in terms[1:]:
        out = out + t
    return out


def collided(f_ref, r_ref, t_ref):
    nx = r_ref.shape[0]
    rate = load(r_ref)
    inverse = [[1.0 / t for t in load(t_ref, s)] for s in range(2)]
    f = [[load(f_ref, s, q) for q in range(7)] for s in range(2)]
    rho = [[total([f[s][q][x] for q in range(7)]) for x in range(nx)] for s in range(2)]
    c = [[[None] * nx for _ in range(7)] for _ in range(2)]
    for x in range(nx):
        reaction = rate[x] * rho[0][x] * rho[1][x]
        for s in range(2):
            source = reaction if s == 1 else -reaction
            for q in range(7):
                w = WEIGHTS[q]
                v = f[s][q][x]
                c[s][q][x] = v - (v - w * rho[s][x]) * inverse[s][x] + w * source
    return c, rho, inverse, rate


def pack_x(fields, last):
    return [v[-1] if last else v[0] for v in fields]


def rows_of(v, i):
    return jnp.concatenate([plane[i : i + 1] for plane in v], axis=0)


def pack_y(fields, last):
    n = fields[0][0].shape[0]
    return jnp.concatenate([rows_of(v, n - 1 if last else 0) for v in fields], axis=0)


def pack_z(fields, last, start=0, out=None):
    lane = lax.broadcasted_iota(jnp.int32, (8, 128), 1)
    out = jnp.zeros((8, 128), jnp.float32) if out is None else out
    j = start
    for v in fields:
        for plane in v:
            for h in range(plane.shape[0] // 8):
                part = plane[8 * h : 8 * h + 8]
                shift = (j + 1) % 128 if last else j
                part = pltpu.roll(part, shift, axis=1) if shift else part
                out = jnp.where(lane == j, part, out)
                j += 1
    return out


def cut(v, axis, sign):
    if axis == 0:
        zero = jnp.zeros_like(v[0])
        return v[1:] + [zero] if sign > 0 else [zero] + v[:-1]
    out = []
    for plane in v:
        n = plane.shape[axis - 1]
        at = lax.broadcasted_iota(jnp.int32, plane.shape, axis - 1)
        rolled = pltpu.roll(plane, n - 1 if sign > 0 else 1, axis=axis - 1)
        out.append(jnp.where(at == (n - 1 if sign > 0 else 0), 0.0, rolled))
    return out


def plus(a, b):
    return [x + y for x, y in zip(a, b)]


def partial_sums(g, c, axes):
    moments, density = [], []
    for s in range(2):
        m = [WEIGHTS[1] * v for v in cut(g[s][1 + 2 * axes[0]], axes[0], 1)]
        d = plus(c[s][0], cut(c[s][1 + 2 * axes[0]], axes[0], -1))
        m = plus(m, [WEIGHTS[1] * v for v in cut(g[s][2 + 2 * axes[0]], axes[0], -1)])
        d = plus(d, cut(c[s][2 + 2 * axes[0]], axes[0], 1))
        m = plus(m, [WEIGHTS[1] * v for v in cut(g[s][1 + 2 * axes[1]], axes[1], 1)])
        d = plus(d, cut(c[s][1 + 2 * axes[1]], axes[1], -1))
        m = plus(m, [WEIGHTS[1] * v for v in cut(g[s][2 + 2 * axes[1]], axes[1], -1)])
        d = plus(d, cut(c[s][2 + 2 * axes[1]], axes[1], 1))
        moments.append(plus(m, [WEIGHTS[0] * v for v in g[s][0]]))
        density.append(d)
    return moments, density


def face_fields(g, c, moments, density, inverse, rate, axis, last):
    out_q, in_q = (1 + 2 * axis, 2 + 2 * axis) if last else (2 + 2 * axis, 1 + 2 * axis)
    sign = -1 if last else 1
    inner = [cut(g[s][in_q], axis, sign) for s in range(2)]
    m = [plus(moments[s], [WEIGHTS[1] * v for v in inner[s]]) for s in range(2)]
    d = [plus(density[s], cut(c[s][out_q], axis, sign)) for s in range(2)]
    return [*inner, *m, *d, *inverse, rate]


def edge_fields(g, c, axis):
    p, m = 1 + 2 * axis, 2 + 2 * axis
    return [(g[0][p], g[0][m]), (g[1][p], g[1][m]), (c[0][m], c[0][p]), (c[1][m], c[1][p])]


def first_kernel(
    f_hbm, g_hbm, r_hbm, t_hbm, f_ref, g_ref, r_ref, t_ref, up_ref, down_ref, own0_ref, own1_ref, diag_ref, raw_ref, sems
):
    copies = [
        pltpu.make_async_copy(a, b, sems.at[i])
        for i, (a, b) in enumerate(((f_hbm, f_ref), (g_hbm, g_ref), (r_hbm, r_ref), (t_hbm, t_ref)))
    ]
    for copy in copies:
        copy.start()
    for copy in copies:
        copy.wait()
    even = parities()
    c, _, inverse, rate = collided(f_ref, r_ref, t_ref)
    g = [[load(g_ref, s, q) for q in range(7)] for s in range(2)]
    up, down = [], []
    for axis in range(3):
        p, m = 1 + 2 * axis, 2 + 2 * axis
        up.append([g[0][m], g[1][m], c[0][p], c[1][p]])
        down.append([g[0][p], g[1][p], c[0][m], c[1][m]])
    for k, (u, d) in enumerate(zip(pack_x(up[0], True), pack_x(down[0], False))):
        up_ref[16 * k : 16 * k + 16] = u
        down_ref[16 * k : 16 * k + 16] = d
    nx, n = len(rate), rate[0].shape[0]
    lane = lax.broadcasted_iota(jnp.int32, (nx, 128), 1)
    row = lax.broadcasted_iota(jnp.int32, (n, 128), 0)
    x_edge, y_edge, z_edge = (edge_fields(g, c, axis) for axis in range(3))
    y_faces, z_faces = [], []
    y_sums, z_sums = partial_sums(g, c, (0, 2)), partial_sums(g, c, (0, 1))
    for last in (False, True):
        i = n - 1 if last else 0
        raw = pack_y((up if last else down)[1], last)
        deep = pack_y(face_fields(g, c, *y_sums, inverse, rate, 1, last), last)
        x_lines = [line for a, b in x_edge for line in (a[0][i : i + 1], b[-1][i : i + 1])]
        x_lines.append(jnp.zeros((28 - 4 * len(rate) - len(x_lines), 128), jnp.float32))
        z_lines = [jnp.where(lane < 64, rows_of(a, i), rows_of(b, i)) for a, b in z_edge]
        y_faces.append((raw, jnp.concatenate([raw, deep, *x_lines], axis=0), jnp.concatenate(z_lines, axis=0)))
        raw = pack_z((up if last else down)[2], last)
        deep = pack_z(face_fields(g, c, *z_sums, inverse, rate, 2, last), last, 32, raw)
        y_lines = [[jnp.where(row < 8, u, v) for u, v in zip(a, b)] for a, b in y_edge]
        x_lines = [a[:-1] + b[-1:] for a, b in x_edge]
        z_faces.append((raw, deep, pack_z(y_lines + x_lines, last)))
    y1, y2 = jnp.where(even[1], y_faces[1][0], y_faces[0][0]), jnp.where(even[1], y_faces[0][0], y_faces[1][0])
    z1, z2 = jnp.where(even[2], z_faces[1][0], z_faces[0][0]), jnp.where(even[2], z_faces[0][0], z_faces[1][0])
    y_deep = jnp.where(even[1], y_faces[0][1], y_faces[1][1])
    y_lines = jnp.where(even[1], y_faces[0][2], y_faces[1][2])
    z_deep = jnp.where(even[2], z_faces[0][1], z_faces[1][1])
    z_lines = jnp.where(even[2], z_faces[0][2], z_faces[1][2])
    raw_ref[0:16] = y2
    raw_ref[16:24] = z2
    diag_ref[0:16] = y_lines
    diag_ref[16:24] = z_lines
    diag_ref[24:40] = jnp.zeros((16, 128), jnp.float32)
    z1 = jnp.concatenate([z1, jnp.zeros_like(z1)], axis=0)
    y_all = jnp.concatenate([y_deep, y_lines], axis=0)
    z_all = jnp.concatenate([z_deep, z_lines, jnp.zeros((y_all.shape[0] - 16, 128), jnp.float32)], axis=0)
    own0_ref[...] = jnp.where(even[0], y1, z1)
    own1_ref[...] = jnp.where(even[0], y_all, z_all)
    for ref in (up_ref, down_ref):
        ref[64:80] = jnp.where(even[0], z1, y1)
        ref[80:160] = jnp.where(even[0], z_all, y_all)


def forward_kernel(own0_ref, own1_ref, below_ref, above_ref, y_ref, z_ref, near_ref):
    even = parities()
    near_ref[0:16] = own0_ref[...]
    near_ref[16:32] = jnp.where(even[0], above_ref[64:80], below_ref[64:80])
    share = jnp.where(even[0], above_ref[80:160], below_ref[80:160])
    y_ref[0:80] = own1_ref[...]
    y_ref[80:160] = share
    z_ref[0:16] = own1_ref[0:16]
    z_ref[16:32] = share[0:16]
    z_ref[32:48] = share[0:16]


def back_kernel(z_ref, y_ref, diag_ref, near_ref, out_ref, lines_ref):
    even = parities()
    lines_ref[...] = diag_ref[...]
    out_ref[0:16] = near_ref[16:32]
    out_ref[16:32] = jnp.where(even[0], y_ref[80:96], z_ref[16:32])
    out_ref[32:96] = y_ref[96:160]


def moved(v, axis, sign, halo, k):
    if axis == 0:
        return v[1:] + [halo[k]] if sign > 0 else [halo[k]] + v[:-1]
    nx, (n, lanes) = len(v), v[0].shape
    out = []
    for x in range(nx):
        plane = v[x]
        if axis == 1:
            row = lax.broadcasted_iota(jnp.int32, (n, lanes), 0)
            edge = halo[k * nx + x : k * nx + x + 1]
            rolled = pltpu.roll(plane, n - 1 if sign > 0 else 1, axis=0)
            out.append(jnp.where(row == (n - 1 if sign > 0 else 0), edge, rolled))
        else:
            lane = lax.broadcasted_iota(jnp.int32, (n, lanes), 1)
            parts = []
            for h in range(n // 8):
                j = (k * nx + x) * (n // 8) + h
                shift = (lanes - 1 - j) % lanes if sign > 0 else (lanes - j) % lanes
                parts.append(pltpu.roll(halo, shift, axis=1) if shift else halo)
            edge = jnp.concatenate(parts, axis=0)
            rolled = pltpu.roll(plane, lanes - 1 if sign > 0 else 1, axis=1)
            out.append(jnp.where(lane == (lanes - 1 if sign > 0 else 0), edge, rolled))
    return out


def adjoint(upstream, state, rho, inverse, rate):
    moments = [total([WEIGHTS[q] * upstream[s][q] for q in range(7)]) for s in range(2)]
    contrast = moments[1] - moments[0]
    scaled = rate * contrast
    earlier, relax = [], []
    for s in range(2):
        keep = 1.0 - inverse[s]
        add = moments[s] * inverse[s] + scaled * rho[1 - s]
        earlier.append([keep * upstream[s][q] + add for q in range(7)])
        part = total([upstream[s][q] * (state[s][q] - WEIGHTS[q] * rho[s]) for q in range(7)])
        relax.append(part * inverse[s] * inverse[s])
    return earlier, rho[0] * rho[1] * contrast, relax


def second_kernel(
    f_ref, g_ref, r_ref, t_ref, below_ref, above_ref, z_ref, y_ref, near_ref, back_ref,
    later_ref, rate_ref, relax_ref, deep_ref, up_ref, down_ref, y1_ref, y2_ref, z1_ref, z2_ref,
):
    even = parities()
    nx = r_ref.shape[0]
    c, _, inverse, rate = collided(f_ref, r_ref, t_ref)
    y1 = jnp.where(even[0], near_ref[0:16], back_ref[0:16])
    z1 = jnp.where(even[0], back_ref[0:8], near_ref[0:8])
    y2 = jnp.where(even[0], y_ref[0:80], back_ref[16:96])
    z2 = jnp.where(even[0], back_ref[16:32], z_ref[0:16])
    deep_ref[0:80] = y2
    deep_ref[80:96] = z2
    above = [[above_ref[16 * k : 16 * k + 16] for k in range(4)]]
    below = [[below_ref[16 * k : 16 * k + 16] for k in range(4)]]
    for axis, a, b in ((1, y1, y2[0:16]), (2, z1, z2[0:8])):
        above.append(jnp.where(even[axis], a, b))
        below.append(jnp.where(even[axis], b, a))
    upstream = [[load(g_ref, s, 0)] for s in range(2)]
    middle = [[c[s][0]] for s in range(2)]
    for s in range(2):
        for axis in range(3):
            p, m = 1 + 2 * axis, 2 + 2 * axis
            upstream[s].append(moved(load(g_ref, s, p), axis, 1, above[axis], s))
            upstream[s].append(moved(load(g_ref, s, m), axis, -1, below[axis], s))
            middle[s].append(moved(c[s][p], axis, -1, below[axis], 2 + s))
            middle[s].append(moved(c[s][m], axis, 1, above[axis], 2 + s))
    later = [[[None] * nx for _ in range(7)] for _ in range(2)]
    for x in range(nx):
        up = [[upstream[s][q][x] for q in range(7)] for s in range(2)]
        mid = [[middle[s][q][x] for q in range(7)] for s in range(2)]
        rho = [total(mid[s]) for s in range(2)]
        earlier, rate_part, relax_part = adjoint(up, mid, rho, [inverse[s][x] for s in range(2)], rate[x])
        rate_ref[x] = rate_part
        for s in range(2):
            relax_ref[s, x] = relax_part[s]
            for q in range(7):
                later[s][q][x] = earlier[s][q]
                later_ref[s, q, x] = earlier[s][q]
    for ref, last in ((up_ref, True), (down_ref, False)):
        for s, face in enumerate(pack_x([later[s][2 if last else 1] for s in range(2)], last)):
            ref[16 * s : 16 * s + 16] = face
        ref[32:40] = y2[52:60]
        ref[40:48] = z2[8:16]
    for axis, pack, first, second in ((1, pack_y, y1_ref, y2_ref), (2, pack_z, z1_ref, z2_ref)):
        a = pack([later[s][2 + 2 * axis] for s in range(2)], True)
        b = pack([later[s][1 + 2 * axis] for s in range(2)], False)
        first[0:8] = jnp.where(even[axis], a, b)
        second[0:8] = jnp.where(even[axis], b, a)
    for ref in (y1_ref, y2_ref):
        ref[8:16] = z2[8:16]
    for ref in (z1_ref, z2_ref):
        ref[8:24] = y2[64:80]


def later_beyond(inner, moments, density, inverse, rate):
    scaled = rate * (moments[1] - moments[0])
    return [(1.0 - inverse[s]) * inner[s] + moments[s] * inverse[s] + scaled * density[1 - s] for s in range(2)]


def beyond_y(deep, own, x_above, x_below, z_above, z_below):
    nx = 4
    field = lambda k: deep[16 + nx * k : 16 + nx * k + nx]
    lane = lax.broadcasted_iota(jnp.int32, (nx, 128), 1)
    added = []
    for k in range(4):
        zero = jnp.zeros((nx - 2, 128), jnp.float32)
        x_part = jnp.concatenate([x_below[2 * k + 1 : 2 * k + 2], zero, x_above[2 * k : 2 * k + 1]], axis=0)
        high = pltpu.roll(z_above[nx * k : nx * k + nx], 127, axis=1)
        low = pltpu.roll(z_below[nx * k : nx * k + nx], 1, axis=1)
        z_part = jnp.where(lane == 127, high, jnp.where(lane == 0, low, 0.0))
        added.append(own[nx * k : nx * k + nx] + x_part + z_part)
    moments = [field(2 + s) + WEIGHTS[1] * added[s] for s in range(2)]
    density = [field(4 + s) + added[2 + s] for s in range(2)]
    out = later_beyond([field(0), field(1)], moments, density, [field(6), field(7)], field(8))
    return jnp.concatenate(out, axis=0)


def beyond_z(deep, own, x_above, x_below, y_above, y_below):
    lane = lax.broadcasted_iota(jnp.int32, (8, 128), 1)
    row = lax.broadcasted_iota(jnp.int32, (8, 128), 0)

    def at(v, shift):
        shift = shift % 128
        return pltpu.roll(v, shift, axis=1) if shift else v

    field = lambda k: at(deep, -32 - 8 * k)
    odd = lax.rem(lane, 2) == 1
    y_high, y_low = pltpu.roll(y_above, 7, axis=0), pltpu.roll(y_below, 1, axis=0)
    added = []
    for k in range(4):
        x_part = jnp.where(lane >= 6, at(x_above, 6 - 32 - 8 * k), 0.0)
        x_part = jnp.where(lane < 2, at(x_below, -6 - 32 - 8 * k), x_part)
        y_part = jnp.where((row == 7) & odd, at(y_high, 1 - 8 * k), 0.0)
        y_part = jnp.where((row == 0) & ~odd, at(y_low, -1 - 8 * k), y_part)
        added.append(at(own, -8 * k) + x_part + y_part)
    moments = [field(2 + s) + WEIGHTS[1] * added[s] for s in range(2)]
    density = [field(4 + s) + added[2 + s] for s in range(2)]
    out = later_beyond([field(0), field(1)], moments, density, [field(6), field(7)], field(8))
    return jnp.where(lane < 8, out[0], pltpu.roll(out[1], 8, axis=1))


def third_kernel(
    f_ref, r_ref, t_ref, later_ref, rate_late_ref, relax_late_ref, deep_ref, raw_ref, diag_ref,
    below_ref, above_ref, y1_ref, y2_ref, z1_ref, z2_ref, state_ref, rate_ref, relax_ref,
):
    even = parities()
    nx = r_ref.shape[0]
    far_y = far_along_y(lax.axis_index("gy"), lax.axis_size("gy"))
    far_z = far_along_z(lax.axis_index("gz"), lax.axis_size("gz"))
    lines1, lines2 = z1_ref[8:24], jnp.where(far_z, diag_ref[0:16], z2_ref[8:24])
    y2 = beyond_y(
        deep_ref[0:80], raw_ref[0:16], above_ref[32:40], below_ref[32:40],
        jnp.where(even[2], lines1, lines2), jnp.where(even[2], lines2, lines1),
    )
    lines1, lines2 = y1_ref[8:16], jnp.where(far_y, diag_ref[16:24], y2_ref[8:16])
    z2 = beyond_z(
        deep_ref[80:88], raw_ref[16:24], above_ref[40:48], below_ref[40:48],
        jnp.where(even[1], lines1, lines2), jnp.where(even[1], lines2, lines1),
    )
    y2 = jnp.where(far_y, y2, y2_ref[0:8])
    z2 = jnp.where(far_z, z2, z2_ref[0:8])
    above = [[above_ref[16 * k : 16 * k + 16] for k in range(2)]]
    below = [[below_ref[16 * k : 16 * k + 16] for k in range(2)]]
    for axis, a, b in ((1, y1_ref[0:8], y2), (2, z1_ref[0:8], z2)):
        above.append(jnp.where(even[axis], a, b))
        below.append(jnp.where(even[axis], b, a))
    upstream = [[load(later_ref, s, 0)] for s in range(2)]
    for s in range(2):
        for axis in range(3):
            upstream[s].append(moved(load(later_ref, s, 1 + 2 * axis), axis, 1, above[axis], s))
            upstream[s].append(moved(load(later_ref, s, 2 + 2 * axis), axis, -1, below[axis], s))
    for x in range(nx):
        up = [[upstream[s][q][x] for q in range(7)] for s in range(2)]
        state = [[f_ref[s, q, x] for q in range(7)] for s in range(2)]
        rho = [total(state[s]) for s in range(2)]
        inverse = [1.0 / t_ref[s, x] for s in range(2)]
        earlier, rate_part, relax_part = adjoint(up, state, rho, inverse, r_ref[x])
        rate_ref[x] = rate_late_ref[x] + rate_part
        for s in range(2):
            relax_ref[s, x] = relax_late_ref[s, x] + relax_part[s]
            for q in range(7):
                state_ref[s, q, x] = earlier[s][q]


def call(kernel, shapes, *args, source=pltpu.VMEM, scratch=()):
    return pl.pallas_call(
        kernel,
        out_shape=[jax.ShapeDtypeStruct(s, jnp.float32) for s in shapes],
        in_specs=[pl.BlockSpec(memory_space=source)] * len(args),
        out_specs=[pl.BlockSpec(memory_space=pltpu.VMEM)] * len(shapes),
        scratch_shapes=list(scratch),
        compiler_params=pltpu.CompilerParams(vmem_limit_bytes=32 * 1024 * 1024),
    )(*args)


def shifts(axis):
    count = lax.axis_size(axis)
    up = [(i, (i + 1) % count) for i in range(count)]
    return up, [(j, i) for i, j in up]


def far_along_y(index, count):
    return (index == 0) | (index == count - 1)


def far_along_z(index, count):
    half = count // 2
    return (index % half == 0) | (index % half == half - 1)


def grid_pairs(move):
    counts = tuple(lax.axis_size(a) for a in AXES)
    nx, ny, nz = counts
    pairs = []
    for x in range(nx):
        for y in range(ny):
            for z in range(nz):
                to = move(x, y, z, counts)
                if to is not None:
                    pairs.append(((x * ny + y) * nz + z, (to[0] * ny + to[1]) * nz + to[2]))
    return pairs


def near_move(x, y, z, counts):
    return (x, partner(y, counts[1], 0), z) if x % 2 == 0 else (x, y, partner(z, counts[2], 0))


def second_y_move(x, y, z, counts):
    return (x, partner(y, counts[1], 1), z) if x % 2 == 0 else None


def second_z_move(x, y, z, counts):
    return (x, y, partner(z, counts[2], 1)) if x % 2 == 1 else None


def diagonal_move(x, y, z, counts):
    if far_along_y(y, counts[1]) and far_along_z(z, counts[2]):
        return (x, partner(y, counts[1], 1), partner(z, counts[2], 1))
    return None


def first_exchange(up, down, own0, own1, diag):
    to_up, to_down = shifts("gx")
    below = lax.ppermute(up, "gx", to_up)
    above = lax.ppermute(down, "gx", to_down)
    y, z, near = call(forward_kernel, [(160, 128), (48, 128), (32, 128)], own0, own1, below, above)
    z_in = lax.ppermute(z, AXES, grid_pairs(second_z_move))
    y_in = lax.ppermute(y, AXES, grid_pairs(second_y_move))
    diag_in = lax.ppermute(diag, AXES, grid_pairs(diagonal_move))
    near_in = lax.ppermute(near, AXES, grid_pairs(near_move))
    back, lines = call(back_kernel, [(96, 128), diag.shape], z_in, y_in, diag_in, near_in)
    back_in = lax.ppermute(back, "gx", axis_pairs("gx", 0))
    return (below, above, z_in, y_in, near_in, back_in), lines


def second_exchange(up, down, y1, y2, z1, z2):
    to_up, to_down = shifts("gx")
    below = lax.ppermute(up, "gx", to_up)
    above = lax.ppermute(down, "gx", to_down)
    received = [below, above]
    for axis, far, a, b in (("gy", far_along_y, y1, y2), ("gz", far_along_z, z1, z2)):
        count = lax.axis_size(axis)
        received.append(lax.ppermute(a, axis, axis_pairs(axis, 0)))
        near = [(i, j) for i, j in axis_pairs(axis, 1) if not far(i, count)]
        received.append(lax.ppermute(b, axis, near))
    return received


def on_device(checkpoint, cotangent, reaction_rate, relax_time):
    inputs = (checkpoint, cotangent, reaction_rate, relax_time)
    messages = [(160, 128), (160, 128), (16, 128), (80, 128), (40, 128), (24, 128)]
    f, g, r, t, *sent, raw = call(
        first_kernel, [a.shape for a in inputs] + messages,
        *(pltpu.with_memory_space_constraint(a, pltpu.HBM) for a in inputs),
        source=pltpu.HBM, scratch=[pltpu.SemaphoreType.DMA((4,))],
    )
    received, diag_in = first_exchange(*sent)
    messages = [(96, 128), (48, 128), (48, 128), (16, 128), (16, 128), (24, 128), (24, 128)]
    later, rate_late, relax_late, deep, *sent = call(
        second_kernel, [f.shape, r.shape, t.shape] + messages, f, g, r, t, *received
    )
    received = second_exchange(*sent)
    return tuple(
        call(
            third_kernel, [f.shape, r.shape, t.shape],
            f, r, t, later, rate_late, relax_late, deep, raw, diag_in, *received,
        )
    )


def solution(mesh):
    placed = (
        P(None, None, "gx", "gy", "gz"),
        P(None, None, "gx", "gy", "gz"),
        P("gx", "gy", "gz"),
        P(None, "gx", "gy", "gz"),
    )
    return jax.shard_map(
        on_device,
        mesh=mesh,
        in_specs=placed,
        out_specs=(P(None, None, "gx", "gy", "gz"), P("gx", "gy", "gz"), P(None, "gx", "gy", "gz")),
        check_vma=False,
    )
```

```python
import jax
import jax.numpy as jnp
from jax import lax
from jax.experimental import pallas as pl
from jax.experimental.pallas import tpu as pltpu
from jax.sharding import PartitionSpec as P

WEIGHTS = (0.25, 0.125, 0.125, 0.125, 0.125, 0.125, 0.125)
AXES = ("gx", "gy", "gz")


def partner(index, count, color):
    if color == 0:
        return index ^ 1
    return (index + 1) % count if index % 2 else (index - 1) % count


def axis_pairs(axis, color):
    count = lax.axis_size(axis)
    return [(i, partner(i, count, color)) for i in range(count)]


def parities():
    return tuple(lax.rem(lax.axis_index(a), 2) == 0 for a in AXES)


def load(ref, *lead):
    return [ref[lead + (x,)] for x in range(ref.shape[len(lead)])]


def total(terms):
    out = terms[0]
    for t in terms[1:]:
        out = out + t
    return out


def collided(f_ref, r_ref, t_ref):
    nx = r_ref.shape[0]
    rate = load(r_ref)
    inverse = [[1.0 / t for t in load(t_ref, s)] for s in range(2)]
    f = [[load(f_ref, s, q) for q in range(7)] for s in range(2)]
    rho = [[total([f[s][q][x] for q in range(7)]) for x in range(nx)] for s in range(2)]
    c = [[[None] * nx for _ in range(7)] for _ in range(2)]
    for x in range(nx):
        reaction = rate[x] * rho[0][x] * rho[1][x]
        for s in range(2):
            source = reaction if s == 1 else -reaction
            for q in range(7):
                w = WEIGHTS[q]
                v = f[s][q][x]
                c[s][q][x] = v - (v - w * rho[s][x]) * inverse[s][x] + w * source
    return c, rho, inverse, rate


def pack_x(fields, last):
    return [v[-1] if last else v[0] for v in fields]


def rows_of(v, i):
    return jnp.concatenate([plane[i : i + 1] for plane in v], axis=0)


def pack_y(fields, last):
    n = fields[0][0].shape[0]
    return jnp.concatenate([rows_of(v, n - 1 if last else 0) for v in fields], axis=0)


def pack_z(fields, last, start=0, out=None):
    lane = lax.broadcasted_iota(jnp.int32, (8, 128), 1)
    out = jnp.zeros((8, 128), jnp.float32) if out is None else out
    j = start
    for v in fields:
        for plane in v:
            for h in range(plane.shape[0] // 8):
                part = plane[8 * h : 8 * h + 8]
                shift = (j + 1) % 128 if last else j
                part = pltpu.roll(part, shift, axis=1) if shift else part
                out = jnp.where(lane == j, part, out)
                j += 1
    return out


def cut(v, axis, sign):
    if axis == 0:
        zero = jnp.zeros_like(v[0])
        return v[1:] + [zero] if sign > 0 else [zero] + v[:-1]
    out = []
    for plane in v:
        n = plane.shape[axis - 1]
        at = lax.broadcasted_iota(jnp.int32, plane.shape, axis - 1)
        rolled = pltpu.roll(plane, n - 1 if sign > 0 else 1, axis=axis - 1)
        out.append(jnp.where(at == (n - 1 if sign > 0 else 0), 0.0, rolled))
    return out


def plus(a, b):
    return [x + y for x, y in zip(a, b)]


def partial_sums(g, c, axes):
    moments, density = [], []
    for s in range(2):
        m = [WEIGHTS[1] * v for v in cut(g[s][1 + 2 * axes[0]], axes[0], 1)]
        d = plus(c[s][0], cut(c[s][1 + 2 * axes[0]], axes[0], -1))
        m = plus(m, [WEIGHTS[1] * v for v in cut(g[s][2 + 2 * axes[0]], axes[0], -1)])
        d = plus(d, cut(c[s][2 + 2 * axes[0]], axes[0], 1))
        m = plus(m, [WEIGHTS[1] * v for v in cut(g[s][1 + 2 * axes[1]], axes[1], 1)])
        d = plus(d, cut(c[s][1 + 2 * axes[1]], axes[1], -1))
        m = plus(m, [WEIGHTS[1] * v for v in cut(g[s][2 + 2 * axes[1]], axes[1], -1)])
        d = plus(d, cut(c[s][2 + 2 * axes[1]], axes[1], 1))
        moments.append(plus(m, [WEIGHTS[0] * v for v in g[s][0]]))
        density.append(d)
    return moments, density


def face_fields(g, c, moments, density, inverse, rate, axis, last):
    out_q, in_q = (1 + 2 * axis, 2 + 2 * axis) if last else (2 + 2 * axis, 1 + 2 * axis)
    sign = -1 if last else 1
    inner = [cut(g[s][in_q], axis, sign) for s in range(2)]
    m = [plus(moments[s], [WEIGHTS[1] * v for v in inner[s]]) for s in range(2)]
    d = [plus(density[s], cut(c[s][out_q], axis, sign)) for s in range(2)]
    return [*inner, *m, *d, *inverse, rate]


def edge_fields(g, c, axis):
    p, m = 1 + 2 * axis, 2 + 2 * axis
    return [(g[0][p], g[0][m]), (g[1][p], g[1][m]), (c[0][m], c[0][p]), (c[1][m], c[1][p])]


def first_kernel(
    f_hbm, g_hbm, r_hbm, t_hbm, f_ref, g_ref, r_ref, t_ref, up_ref, down_ref, own0_ref, own1_ref, diag_ref, raw_ref, sems
):
    copies = [
        pltpu.make_async_copy(a, b, sems.at[i])
        for i, (a, b) in enumerate(((f_hbm, f_ref), (g_hbm, g_ref), (r_hbm, r_ref), (t_hbm, t_ref)))
    ]
    for copy in copies:
        copy.start()
    for copy in copies:
        copy.wait()
    even = parities()
    c, _, inverse, rate = collided(f_ref, r_ref, t_ref)
    g = [[load(g_ref, s, q) for q in range(7)] for s in range(2)]
    up, down = [], []
    for axis in range(3):
        p, m = 1 + 2 * axis, 2 + 2 * axis
        up.append([g[0][m], g[1][m], c[0][p], c[1][p]])
        down.append([g[0][p], g[1][p], c[0][m], c[1][m]])
    for k, (u, d) in enumerate(zip(pack_x(up[0], True), pack_x(down[0], False))):
        up_ref[16 * k : 16 * k + 16] = u
        down_ref[16 * k : 16 * k + 16] = d
    nx, n = len(rate), rate[0].shape[0]
    lane = lax.broadcasted_iota(jnp.int32, (nx, 128), 1)
    row = lax.broadcasted_iota(jnp.int32, (n, 128), 0)
    x_edge, y_edge, z_edge = (edge_fields(g, c, axis) for axis in range(3))
    y_faces, z_faces = [], []
    y_sums, z_sums = partial_sums(g, c, (0, 2)), partial_sums(g, c, (0, 1))
    for last in (False, True):
        i = n - 1 if last else 0
        raw = pack_y((up if last else down)[1], last)
        deep = pack_y(face_fields(g, c, *y_sums, inverse, rate, 1, last), last)
        x_lines = [line for a, b in x_edge for line in (a[0][i : i + 1], b[-1][i : i + 1])]
        x_lines.append(jnp.zeros((28 - 4 * len(rate) - len(x_lines), 128), jnp.float32))
        z_lines = [jnp.where(lane < 64, rows_of(a, i), rows_of(b, i)) for a, b in z_edge]
        y_faces.append((raw, jnp.concatenate([raw, deep, *x_lines], axis=0), jnp.concatenate(z_lines, axis=0)))
        raw = pack_z((up if last else down)[2], last)
        deep = pack_z(face_fields(g, c, *z_sums, inverse, rate, 2, last), last, 32, raw)
        y_lines = [[jnp.where(row < 8, u, v) for u, v in zip(a, b)] for a, b in y_edge]
        x_lines = [a[:-1] + b[-1:] for a, b in x_edge]
        z_faces.append((raw, deep, pack_z(y_lines + x_lines, last)))
    y1, y2 = jnp.where(even[1], y_faces[1][0], y_faces[0][0]), jnp.where(even[1], y_faces[0][0], y_faces[1][0])
    z1, z2 = jnp.where(even[2], z_faces[1][0], z_faces[0][0]), jnp.where(even[2], z_faces[0][0], z_faces[1][0])
    y_deep = jnp.where(even[1], y_faces[0][1], y_faces[1][1])
    y_lines = jnp.where(even[1], y_faces[0][2], y_faces[1][2])
    z_deep = jnp.where(even[2], z_faces[0][1], z_faces[1][1])
    z_lines = jnp.where(even[2], z_faces[0][2], z_faces[1][2])
    raw_ref[0:16] = y2
    raw_ref[16:24] = z2
    diag_ref[0:16] = y_lines
    diag_ref[16:24] = z_lines
    diag_ref[24:40] = jnp.zeros((16, 128), jnp.float32)
    z1 = jnp.concatenate([z1, jnp.zeros_like(z1)], axis=0)
    y_all = jnp.concatenate([y_deep, y_lines], axis=0)
    z_all = jnp.concatenate([z_deep, z_lines, jnp.zeros((y_all.shape[0] - 16, 128), jnp.float32)], axis=0)
    own0_ref[...] = jnp.where(even[0], y1, z1)
    own1_ref[...] = jnp.where(even[0], y_all, z_all)
    for ref in (up_ref, down_ref):
        ref[64:80] = jnp.where(even[0], z1, y1)
        ref[80:160] = jnp.where(even[0], z_all, y_all)


def forward_kernel(own0_ref, own1_ref, below_ref, above_ref, y_ref, z_ref, near_ref):
    even = parities()
    near_ref[0:16] = own0_ref[...]
    near_ref[16:32] = jnp.where(even[0], above_ref[64:80], below_ref[64:80])
    share = jnp.where(even[0], above_ref[80:160], below_ref[80:160])
    y_ref[0:80] = own1_ref[...]
    y_ref[80:160] = share
    z_ref[0:16] = own1_ref[0:16]
    z_ref[16:32] = share[0:16]
    z_ref[32:48] = share[0:16]


def back_kernel(z_ref, y_ref, diag_ref, near_ref, out_ref, lines_ref):
    even = parities()
    lines_ref[...] = diag_ref[0:24]
    out_ref[0:16] = near_ref[16:32]
    out_ref[16:32] = jnp.where(even[0], y_ref[80:96], z_ref[16:32])
    out_ref[32:96] = y_ref[96:160]


def moved(v, axis, sign, halo, k):
    if axis == 0:
        return v[1:] + [halo[k]] if sign > 0 else [halo[k]] + v[:-1]
    nx, (n, lanes) = len(v), v[0].shape
    out = []
    for x in range(nx):
        plane = v[x]
        if axis == 1:
            row = lax.broadcasted_iota(jnp.int32, (n, lanes), 0)
            edge = halo[k * nx + x : k * nx + x + 1]
            rolled = pltpu.roll(plane, n - 1 if sign > 0 else 1, axis=0)
            out.append(jnp.where(row == (n - 1 if sign > 0 else 0), edge, rolled))
        else:
            lane = lax.broadcasted_iota(jnp.int32, (n, lanes), 1)
            parts = []
            for h in range(n // 8):
                j = (k * nx + x) * (n // 8) + h
                shift = (lanes - 1 - j) % lanes if sign > 0 else (lanes - j) % lanes
                parts.append(pltpu.roll(halo, shift, axis=1) if shift else halo)
            edge = jnp.concatenate(parts, axis=0)
            rolled = pltpu.roll(plane, lanes - 1 if sign > 0 else 1, axis=1)
            out.append(jnp.where(lane == (lanes - 1 if sign > 0 else 0), edge, rolled))
    return out


def adjoint(upstream, state, rho, inverse, rate):
    moments = [total([WEIGHTS[q] * upstream[s][q] for q in range(7)]) for s in range(2)]
    contrast = moments[1] - moments[0]
    scaled = rate * contrast
    earlier, relax = [], []
    for s in range(2):
        keep = 1.0 - inverse[s]
        add = moments[s] * inverse[s] + scaled * rho[1 - s]
        earlier.append([keep * upstream[s][q] + add for q in range(7)])
        part = total([upstream[s][q] * (state[s][q] - WEIGHTS[q] * rho[s]) for q in range(7)])
        relax.append(part * inverse[s] * inverse[s])
    return earlier, rho[0] * rho[1] * contrast, relax


def second_kernel(
    f_ref, g_ref, r_ref, t_ref, below_ref, above_ref, z_ref, y_ref, near_ref, back_ref,
    later_ref, rate_ref, relax_ref, deep_ref, up_ref, down_ref, y1_ref, z1_ref, relay_ref,
):
    even = parities()
    nx = r_ref.shape[0]
    c, _, inverse, rate = collided(f_ref, r_ref, t_ref)
    y1 = jnp.where(even[0], near_ref[0:16], back_ref[0:16])
    z1 = jnp.where(even[0], back_ref[0:8], near_ref[0:8])
    y2 = jnp.where(even[0], y_ref[0:80], back_ref[16:96])
    z2 = jnp.where(even[0], back_ref[16:32], z_ref[0:16])
    deep_ref[0:80] = y2
    deep_ref[80:96] = z2
    above = [[above_ref[16 * k : 16 * k + 16] for k in range(4)]]
    below = [[below_ref[16 * k : 16 * k + 16] for k in range(4)]]
    for axis, a, b in ((1, y1, y2[0:16]), (2, z1, z2[0:8])):
        above.append(jnp.where(even[axis], a, b))
        below.append(jnp.where(even[axis], b, a))
    upstream = [[load(g_ref, s, 0)] for s in range(2)]
    middle = [[c[s][0]] for s in range(2)]
    for s in range(2):
        for axis in range(3):
            p, m = 1 + 2 * axis, 2 + 2 * axis
            upstream[s].append(moved(load(g_ref, s, p), axis, 1, above[axis], s))
            upstream[s].append(moved(load(g_ref, s, m), axis, -1, below[axis], s))
            middle[s].append(moved(c[s][p], axis, -1, below[axis], 2 + s))
            middle[s].append(moved(c[s][m], axis, 1, above[axis], 2 + s))
    later = [[[None] * nx for _ in range(7)] for _ in range(2)]
    for x in range(nx):
        up = [[upstream[s][q][x] for q in range(7)] for s in range(2)]
        mid = [[middle[s][q][x] for q in range(7)] for s in range(2)]
        rho = [total(mid[s]) for s in range(2)]
        earlier, rate_part, relax_part = adjoint(up, mid, rho, [inverse[s][x] for s in range(2)], rate[x])
        rate_ref[x] = rate_part
        for s in range(2):
            relax_ref[s, x] = relax_part[s]
            for q in range(7):
                later[s][q][x] = earlier[s][q]
                later_ref[s, q, x] = earlier[s][q]
    for ref, last in ((up_ref, True), (down_ref, False)):
        for s, face in enumerate(pack_x([later[s][2 if last else 1] for s in range(2)], last)):
            ref[16 * s : 16 * s + 16] = face
        ref[32:40] = y2[52:60]
        ref[40:48] = z2[8:16]
    for axis, pack, ref in ((1, pack_y, y1_ref), (2, pack_z, z1_ref)):
        a = pack([later[s][2 + 2 * axis] for s in range(2)], True)
        b = pack([later[s][1 + 2 * axis] for s in range(2)], False)
        ref[0:8] = jnp.where(even[axis], a, b)
    y1_ref[8:16] = z2[8:16]
    z1_ref[8:24] = y2[64:80]
    relay_ref[0:16] = y2[64:80]
    relay_ref[16:24] = z2[8:16]
    relay_ref[24:40] = y2[0:16]
    relay_ref[40:48] = z2[0:8]


def later_beyond(inner, moments, density, inverse, rate):
    scaled = rate * (moments[1] - moments[0])
    return [(1.0 - inverse[s]) * inner[s] + moments[s] * inverse[s] + scaled * density[1 - s] for s in range(2)]


def beyond_y(deep, own, x_above, x_below, z_above, z_below):
    nx = 4
    field = lambda k: deep[16 + nx * k : 16 + nx * k + nx]
    lane = lax.broadcasted_iota(jnp.int32, (nx, 128), 1)
    added = []
    for k in range(4):
        zero = jnp.zeros((nx - 2, 128), jnp.float32)
        x_part = jnp.concatenate([x_below[2 * k + 1 : 2 * k + 2], zero, x_above[2 * k : 2 * k + 1]], axis=0)
        high = pltpu.roll(z_above[nx * k : nx * k + nx], 127, axis=1)
        low = pltpu.roll(z_below[nx * k : nx * k + nx], 1, axis=1)
        z_part = jnp.where(lane == 127, high, jnp.where(lane == 0, low, 0.0))
        added.append(own[nx * k : nx * k + nx] + x_part + z_part)
    moments = [field(2 + s) + WEIGHTS[1] * added[s] for s in range(2)]
    density = [field(4 + s) + added[2 + s] for s in range(2)]
    out = later_beyond([field(0), field(1)], moments, density, [field(6), field(7)], field(8))
    return jnp.concatenate(out, axis=0)


def beyond_z(deep, own, x_above, x_below, y_above, y_below):
    lane = lax.broadcasted_iota(jnp.int32, (8, 128), 1)
    row = lax.broadcasted_iota(jnp.int32, (8, 128), 0)

    def at(v, shift):
        shift = shift % 128
        return pltpu.roll(v, shift, axis=1) if shift else v

    field = lambda k: at(deep, -32 - 8 * k)
    odd = lax.rem(lane, 2) == 1
    y_high, y_low = pltpu.roll(y_above, 7, axis=0), pltpu.roll(y_below, 1, axis=0)
    added = []
    for k in range(4):
        x_part = jnp.where(lane >= 6, at(x_above, 6 - 32 - 8 * k), 0.0)
        x_part = jnp.where(lane < 2, at(x_below, -6 - 32 - 8 * k), x_part)
        y_part = jnp.where((row == 7) & odd, at(y_high, 1 - 8 * k), 0.0)
        y_part = jnp.where((row == 0) & ~odd, at(y_low, -1 - 8 * k), y_part)
        added.append(at(own, -8 * k) + x_part + y_part)
    moments = [field(2 + s) + WEIGHTS[1] * added[s] for s in range(2)]
    density = [field(4 + s) + added[2 + s] for s in range(2)]
    out = later_beyond([field(0), field(1)], moments, density, [field(6), field(7)], field(8))
    return jnp.where(lane < 8, out[0], pltpu.roll(out[1], 8, axis=1))


def z_lines_of(packed, last):
    row, lane = (lax.broadcasted_iota(jnp.int32, (16, 128), d) for d in (0, 1))
    edge = jnp.where(last, packed[7:8], packed[0:1])
    wanted = lane == 2 * row + jnp.where(last, 1, 0)
    return jnp.broadcast_to(jnp.sum(jnp.where(wanted, edge, 0.0), axis=1, keepdims=True), (16, 128))


def y_lines_of(rows, last):
    row, lane = (lax.broadcasted_iota(jnp.int32, (16, 128), d) for d in (0, 1))
    wanted = lane == jnp.where(last, 127, 0)
    edge = jnp.sum(jnp.where(wanted, rows, 0.0), axis=1, keepdims=True)
    return jnp.broadcast_to(jnp.sum(jnp.where(lane // 2 == row, edge, 0.0), axis=0, keepdims=True), (8, 128))


def third_kernel(
    f_ref, r_ref, t_ref, later_ref, rate_late_ref, relax_late_ref, deep_ref, raw_ref, diag_ref,
    below_ref, above_ref, y1_ref, z1_ref, relay_ref, state_ref, rate_ref, relax_ref,
):
    even = parities()
    nx = r_ref.shape[0]
    far_y = far_along_y(lax.axis_index("gy"), lax.axis_size("gy"))
    far_z = far_along_z(lax.axis_index("gz"), lax.axis_size("gz"))
    alike = far_y == far_z
    lines1 = z1_ref[8:24]
    lines2 = jnp.where(far_y, relay_ref[0:16], z_lines_of(relay_ref[40:48], even[1]))
    lines2 = jnp.where(alike, diag_ref[0:16], lines2)
    y2 = beyond_y(
        deep_ref[0:80], raw_ref[0:16], above_ref[32:40], below_ref[32:40],
        jnp.where(even[2], lines1, lines2), jnp.where(even[2], lines2, lines1),
    )
    lines1 = y1_ref[8:16]
    lines2 = jnp.where(far_z, relay_ref[16:24], y_lines_of(relay_ref[24:40], even[2]))
    lines2 = jnp.where(alike, diag_ref[16:24], lines2)
    z2 = beyond_z(
        deep_ref[80:88], raw_ref[16:24], above_ref[40:48], below_ref[40:48],
        jnp.where(even[1], lines1, lines2), jnp.where(even[1], lines2, lines1),
    )
    above = [[above_ref[16 * k : 16 * k + 16] for k in range(2)]]
    below = [[below_ref[16 * k : 16 * k + 16] for k in range(2)]]
    for axis, a, b in ((1, y1_ref[0:8], y2), (2, z1_ref[0:8], z2)):
        above.append(jnp.where(even[axis], a, b))
        below.append(jnp.where(even[axis], b, a))
    upstream = [[load(later_ref, s, 0)] for s in range(2)]
    for s in range(2):
        for axis in range(3):
            upstream[s].append(moved(load(later_ref, s, 1 + 2 * axis), axis, 1, above[axis], s))
            upstream[s].append(moved(load(later_ref, s, 2 + 2 * axis), axis, -1, below[axis], s))
    for x in range(nx):
        up = [[upstream[s][q][x] for q in range(7)] for s in range(2)]
        state = [[f_ref[s, q, x] for q in range(7)] for s in range(2)]
        rho = [total(state[s]) for s in range(2)]
        inverse = [1.0 / t_ref[s, x] for s in range(2)]
        earlier, rate_part, relax_part = adjoint(up, state, rho, inverse, r_ref[x])
        rate_ref[x] = rate_late_ref[x] + rate_part
        for s in range(2):
            relax_ref[s, x] = relax_late_ref[s, x] + relax_part[s]
            for q in range(7):
                state_ref[s, q, x] = earlier[s][q]


def call(kernel, shapes, *args, source=pltpu.VMEM, scratch=()):
    return pl.pallas_call(
        kernel,
        out_shape=[jax.ShapeDtypeStruct(s, jnp.float32) for s in shapes],
        in_specs=[pl.BlockSpec(memory_space=source)] * len(args),
        out_specs=[pl.BlockSpec(memory_space=pltpu.VMEM)] * len(shapes),
        scratch_shapes=list(scratch),
        compiler_params=pltpu.CompilerParams(vmem_limit_bytes=32 * 1024 * 1024),
    )(*args)


def shifts(axis):
    count = lax.axis_size(axis)
    up = [(i, (i + 1) % count) for i in range(count)]
    return up, [(j, i) for i, j in up]


def far_along_y(index, count):
    return (index == 0) | (index == count - 1)


def far_along_z(index, count):
    half = count // 2
    return (index % half == 0) | (index % half == half - 1)


def grid_pairs(move):
    counts = tuple(lax.axis_size(a) for a in AXES)
    nx, ny, nz = counts
    pairs = []
    for x in range(nx):
        for y in range(ny):
            for z in range(nz):
                to = move(x, y, z, counts)
                if to is not None:
                    pairs.append(((x * ny + y) * nz + z, (to[0] * ny + to[1]) * nz + to[2]))
    return pairs


def near_move(x, y, z, counts):
    return (x, partner(y, counts[1], 0), z) if x % 2 == 0 else (x, y, partner(z, counts[2], 0))


def second_y_move(x, y, z, counts):
    return (x, partner(y, counts[1], 1), z) if x % 2 == 0 else None


def second_z_move(x, y, z, counts):
    return (x, y, partner(z, counts[2], 1)) if x % 2 == 1 else None


def diagonal_move(x, y, z, counts):
    if far_along_y(y, counts[1]) == far_along_z(z, counts[2]):
        return (x, partner(y, counts[1], 1), partner(z, counts[2], 1))
    return None


def relay_move(x, y, z, counts):
    far_y, far_z = far_along_y(y, counts[1]), far_along_z(z, counts[2])
    if far_y and not far_z:
        return (x, y, partner(z, counts[2], 1))
    return (x, partner(y, counts[1], 1), z) if far_z and not far_y else None


def first_exchange(up, down, own0, own1, diag):
    to_up, to_down = shifts("gx")
    below = lax.ppermute(up, "gx", to_up)
    above = lax.ppermute(down, "gx", to_down)
    y, z, near = call(forward_kernel, [(160, 128), (48, 128), (32, 128)], own0, own1, below, above)
    z_in = lax.ppermute(z, AXES, grid_pairs(second_z_move))
    y_in = lax.ppermute(y, AXES, grid_pairs(second_y_move))
    diag_in = lax.ppermute(diag, AXES, grid_pairs(diagonal_move))
    near_in = lax.ppermute(near, AXES, grid_pairs(near_move))
    back, lines = call(back_kernel, [(96, 128), (24, 128)], z_in, y_in, diag_in, near_in)
    back_in = lax.ppermute(back, "gx", axis_pairs("gx", 0))
    return (below, above, z_in, y_in, near_in, back_in), lines


def second_exchange(up, down, y1, z1, relay):
    to_up, to_down = shifts("gx")
    return (
        lax.ppermute(up, "gx", to_up),
        lax.ppermute(down, "gx", to_down),
        lax.ppermute(y1, "gy", axis_pairs("gy", 0)),
        lax.ppermute(z1, "gz", axis_pairs("gz", 0)),
        lax.ppermute(relay, AXES, grid_pairs(relay_move)),
    )


def on_device(checkpoint, cotangent, reaction_rate, relax_time):
    inputs = (checkpoint, cotangent, reaction_rate, relax_time)
    messages = [(160, 128), (160, 128), (16, 128), (80, 128), (40, 128), (24, 128)]
    f, g, r, t, *sent, raw = call(
        first_kernel, [a.shape for a in inputs] + messages,
        *(pltpu.with_memory_space_constraint(a, pltpu.HBM) for a in inputs),
        source=pltpu.HBM, scratch=[pltpu.SemaphoreType.DMA((4,))],
    )
    received, diag_in = first_exchange(*sent)
    messages = [(96, 128), (48, 128), (48, 128), (16, 128), (24, 128), (48, 128)]
    later, rate_late, relax_late, deep, *sent = call(
        second_kernel, [f.shape, r.shape, t.shape] + messages, f, g, r, t, *received
    )
    received = second_exchange(*sent)
    return tuple(
        call(
            third_kernel, [f.shape, r.shape, t.shape],
            f, r, t, later, rate_late, relax_late, deep, raw, diag_in, *received,
        )
    )


def solution(mesh):
    placed = (
        P(None, None, "gx", "gy", "gz"),
        P(None, None, "gx", "gy", "gz"),
        P("gx", "gy", "gz"),
        P(None, "gx", "gy", "gz"),
    )
    return jax.shard_map(
        on_device,
        mesh=mesh,
        in_specs=placed,
        out_specs=(P(None, None, "gx", "gy", "gz"), P("gx", "gy", "gz"), P(None, "gx", "gy", "gz")),
        check_vma=False,
    )
```

```python
import jax
import jax.numpy as jnp
from jax import lax
from jax.experimental import pallas as pl
from jax.experimental.pallas import tpu as pltpu
from jax.sharding import PartitionSpec as P

WEIGHTS = (0.25, 0.125, 0.125, 0.125, 0.125, 0.125, 0.125)
AXES = ("gx", "gy", "gz")


def partner(index, count, color):
    if color == 0:
        return index ^ 1
    return (index + 1) % count if index % 2 else (index - 1) % count


def axis_pairs(axis, color):
    count = lax.axis_size(axis)
    return [(i, partner(i, count, color)) for i in range(count)]


def parities():
    return tuple(lax.rem(lax.axis_index(a), 2) == 0 for a in AXES)


def load(ref, *lead):
    return [ref[lead + (x,)] for x in range(ref.shape[len(lead)])]


def total(terms):
    out = terms[0]
    for t in terms[1:]:
        out = out + t
    return out


def collided(f_ref, r_ref, t_ref):
    nx = r_ref.shape[0]
    rate = load(r_ref)
    inverse = [[1.0 / t for t in load(t_ref, s)] for s in range(2)]
    f = [[load(f_ref, s, q) for q in range(7)] for s in range(2)]
    rho = [[total([f[s][q][x] for q in range(7)]) for x in range(nx)] for s in range(2)]
    c = [[[None] * nx for _ in range(7)] for _ in range(2)]
    for x in range(nx):
        reaction = rate[x] * rho[0][x] * rho[1][x]
        for s in range(2):
            source = reaction if s == 1 else -reaction
            for q in range(7):
                w = WEIGHTS[q]
                v = f[s][q][x]
                c[s][q][x] = v - (v - w * rho[s][x]) * inverse[s][x] + w * source
    return c, rho, inverse, rate


def pack_x(fields, last):
    return [v[-1] if last else v[0] for v in fields]


def rows_of(v, i):
    return jnp.concatenate([plane[i : i + 1] for plane in v], axis=0)


def pack_y(fields, last):
    n = fields[0][0].shape[0]
    return jnp.concatenate([rows_of(v, n - 1 if last else 0) for v in fields], axis=0)


def pack_z(fields, last, start=0, out=None):
    lane = lax.broadcasted_iota(jnp.int32, (8, 128), 1)
    out = jnp.zeros((8, 128), jnp.float32) if out is None else out
    j = start
    for v in fields:
        for plane in v:
            for h in range(plane.shape[0] // 8):
                part = plane[8 * h : 8 * h + 8]
                shift = (j + 1) % 128 if last else j
                part = pltpu.roll(part, shift, axis=1) if shift else part
                out = jnp.where(lane == j, part, out)
                j += 1
    return out


def cut(v, axis, sign):
    if axis == 0:
        zero = jnp.zeros_like(v[0])
        return v[1:] + [zero] if sign > 0 else [zero] + v[:-1]
    out = []
    for plane in v:
        n = plane.shape[axis - 1]
        at = lax.broadcasted_iota(jnp.int32, plane.shape, axis - 1)
        rolled = pltpu.roll(plane, n - 1 if sign > 0 else 1, axis=axis - 1)
        out.append(jnp.where(at == (n - 1 if sign > 0 else 0), 0.0, rolled))
    return out


def plus(a, b):
    return [x + y for x, y in zip(a, b)]


def partial_sums(g, c, axes):
    moments, density = [], []
    for s in range(2):
        m = [WEIGHTS[1] * v for v in cut(g[s][1 + 2 * axes[0]], axes[0], 1)]
        d = plus(c[s][0], cut(c[s][1 + 2 * axes[0]], axes[0], -1))
        m = plus(m, [WEIGHTS[1] * v for v in cut(g[s][2 + 2 * axes[0]], axes[0], -1)])
        d = plus(d, cut(c[s][2 + 2 * axes[0]], axes[0], 1))
        m = plus(m, [WEIGHTS[1] * v for v in cut(g[s][1 + 2 * axes[1]], axes[1], 1)])
        d = plus(d, cut(c[s][1 + 2 * axes[1]], axes[1], -1))
        m = plus(m, [WEIGHTS[1] * v for v in cut(g[s][2 + 2 * axes[1]], axes[1], -1)])
        d = plus(d, cut(c[s][2 + 2 * axes[1]], axes[1], 1))
        moments.append(plus(m, [WEIGHTS[0] * v for v in g[s][0]]))
        density.append(d)
    return moments, density


def face_fields(g, c, moments, density, inverse, rate, axis, last):
    out_q, in_q = (1 + 2 * axis, 2 + 2 * axis) if last else (2 + 2 * axis, 1 + 2 * axis)
    sign = -1 if last else 1
    inner = [cut(g[s][in_q], axis, sign) for s in range(2)]
    m = [plus(moments[s], [WEIGHTS[1] * v for v in inner[s]]) for s in range(2)]
    d = [plus(density[s], cut(c[s][out_q], axis, sign)) for s in range(2)]
    return [*inner, *m, *d, *inverse, rate]


def edge_fields(g, c, axis):
    p, m = 1 + 2 * axis, 2 + 2 * axis
    return [(g[0][p], g[0][m]), (g[1][p], g[1][m]), (c[0][m], c[0][p]), (c[1][m], c[1][p])]


def first_kernel(
    f_hbm, g_hbm, r_hbm, t_hbm, f_ref, g_ref, r_ref, t_ref, up_ref, down_ref, own0_ref, own1_ref, diag_ref, raw_ref, sems
):
    copies = [
        pltpu.make_async_copy(a, b, sems.at[i])
        for i, (a, b) in enumerate(((f_hbm, f_ref), (g_hbm, g_ref), (r_hbm, r_ref), (t_hbm, t_ref)))
    ]
    for copy in copies:
        copy.start()
    for copy in copies:
        copy.wait()
    even = parities()
    c, _, inverse, rate = collided(f_ref, r_ref, t_ref)
    g = [[load(g_ref, s, q) for q in range(7)] for s in range(2)]
    up, down = [], []
    for axis in range(3):
        p, m = 1 + 2 * axis, 2 + 2 * axis
        up.append([g[0][m], g[1][m], c[0][p], c[1][p]])
        down.append([g[0][p], g[1][p], c[0][m], c[1][m]])
    for k, (u, d) in enumerate(zip(pack_x(up[0], True), pack_x(down[0], False))):
        up_ref[16 * k : 16 * k + 16] = u
        down_ref[16 * k : 16 * k + 16] = d
    nx, n = len(rate), rate[0].shape[0]
    lane = lax.broadcasted_iota(jnp.int32, (nx, 128), 1)
    row = lax.broadcasted_iota(jnp.int32, (n, 128), 0)
    x_edge, y_edge, z_edge = (edge_fields(g, c, axis) for axis in range(3))
    y_faces, z_faces = [], []
    y_sums, z_sums = partial_sums(g, c, (0, 2)), partial_sums(g, c, (0, 1))
    for last in (False, True):
        i = n - 1 if last else 0
        raw = pack_y((up if last else down)[1], last)
        deep = pack_y(face_fields(g, c, *y_sums, inverse, rate, 1, last), last)
        x_lines = [line for a, b in x_edge for line in (a[0][i : i + 1], b[-1][i : i + 1])]
        x_lines.append(jnp.zeros((28 - 4 * len(rate) - len(x_lines), 128), jnp.float32))
        z_lines = [jnp.where(lane < 64, rows_of(a, i), rows_of(b, i)) for a, b in z_edge]
        y_faces.append((raw, jnp.concatenate([raw, deep, *x_lines], axis=0), jnp.concatenate(z_lines, axis=0)))
        raw = pack_z((up if last else down)[2], last)
        deep = pack_z(face_fields(g, c, *z_sums, inverse, rate, 2, last), last, 32, raw)
        y_lines = [[jnp.where(row < 8, u, v) for u, v in zip(a, b)] for a, b in y_edge]
        x_lines = [a[:-1] + b[-1:] for a, b in x_edge]
        z_faces.append((raw, deep, pack_z(y_lines + x_lines, last)))
    y1, y2 = jnp.where(even[1], y_faces[1][0], y_faces[0][0]), jnp.where(even[1], y_faces[0][0], y_faces[1][0])
    z1, z2 = jnp.where(even[2], z_faces[1][0], z_faces[0][0]), jnp.where(even[2], z_faces[0][0], z_faces[1][0])
    y_deep = jnp.where(even[1], y_faces[0][1], y_faces[1][1])
    y_lines = jnp.where(even[1], y_faces[0][2], y_faces[1][2])
    z_deep = jnp.where(even[2], z_faces[0][1], z_faces[1][1])
    z_lines = jnp.where(even[2], z_faces[0][2], z_faces[1][2])
    raw_ref[0:16] = y2
    raw_ref[16:24] = z2
    diag_ref[0:16] = y_lines
    diag_ref[16:24] = z_lines
    rest = diag_ref.shape[0] - 24
    diag_ref[24:] = jnp.zeros((rest, 128), jnp.float32)
    z1 = jnp.concatenate([z1, jnp.zeros_like(z1)], axis=0)
    y_all = jnp.concatenate([y_deep, y_lines], axis=0)
    z_all = jnp.concatenate([z_deep, z_lines, jnp.zeros((y_all.shape[0] - 16, 128), jnp.float32)], axis=0)
    own0_ref[...] = jnp.where(even[0], y1, z1)
    own1_ref[...] = jnp.where(even[0], y_all, z_all)
    for ref in (up_ref, down_ref):
        ref[64:80] = jnp.where(even[0], z1, y1)
        ref[80:160] = jnp.where(even[0], z_all, y_all)


def forward_kernel(own0_ref, own1_ref, below_ref, above_ref, y_ref, z_ref, near_ref):
    even = parities()
    near_ref[0:16] = own0_ref[...]
    near_ref[16:32] = jnp.where(even[0], above_ref[64:80], below_ref[64:80])
    share = jnp.where(even[0], above_ref[80:160], below_ref[80:160])
    y_ref[0:80] = own1_ref[...]
    y_ref[80:160] = share
    z_ref[0:16] = own1_ref[0:16]
    z_ref[16:32] = share[0:16]
    z_ref[32:48] = share[0:16]


def back_kernel(z_ref, y_ref, near_ref, out_ref):
    even = parities()
    out_ref[0:16] = near_ref[16:32]
    out_ref[16:32] = jnp.where(even[0], y_ref[80:96], z_ref[16:32])
    out_ref[32:96] = y_ref[96:160]


def moved(v, axis, sign, halo, k):
    if axis == 0:
        return v[1:] + [halo[k]] if sign > 0 else [halo[k]] + v[:-1]
    nx, (n, lanes) = len(v), v[0].shape
    out = []
    for x in range(nx):
        plane = v[x]
        if axis == 1:
            row = lax.broadcasted_iota(jnp.int32, (n, lanes), 0)
            edge = halo[k * nx + x : k * nx + x + 1]
            rolled = pltpu.roll(plane, n - 1 if sign > 0 else 1, axis=0)
            out.append(jnp.where(row == (n - 1 if sign > 0 else 0), edge, rolled))
        else:
            lane = lax.broadcasted_iota(jnp.int32, (n, lanes), 1)
            parts = []
            for h in range(n // 8):
                j = (k * nx + x) * (n // 8) + h
                shift = (lanes - 1 - j) % lanes if sign > 0 else (lanes - j) % lanes
                parts.append(pltpu.roll(halo, shift, axis=1) if shift else halo)
            edge = jnp.concatenate(parts, axis=0)
            rolled = pltpu.roll(plane, lanes - 1 if sign > 0 else 1, axis=1)
            out.append(jnp.where(lane == (lanes - 1 if sign > 0 else 0), edge, rolled))
    return out


def adjoint(upstream, state, rho, inverse, rate):
    moments = [total([WEIGHTS[q] * upstream[s][q] for q in range(7)]) for s in range(2)]
    contrast = moments[1] - moments[0]
    scaled = rate * contrast
    earlier, relax = [], []
    for s in range(2):
        keep = 1.0 - inverse[s]
        add = moments[s] * inverse[s] + scaled * rho[1 - s]
        earlier.append([keep * upstream[s][q] + add for q in range(7)])
        part = total([upstream[s][q] * (state[s][q] - WEIGHTS[q] * rho[s]) for q in range(7)])
        relax.append(part * inverse[s] * inverse[s])
    return earlier, rho[0] * rho[1] * contrast, relax


def second_kernel(
    f_ref, g_ref, r_ref, t_ref, below_ref, above_ref, z_ref, y_ref, near_ref, back_ref,
    later_ref, rate_ref, relax_ref, deep_ref, up_ref, down_ref, y1_ref, z1_ref, relay_ref,
):
    even = parities()
    nx = r_ref.shape[0]
    c, _, inverse, rate = collided(f_ref, r_ref, t_ref)
    y1 = jnp.where(even[0], near_ref[0:16], back_ref[0:16])
    z1 = jnp.where(even[0], back_ref[0:8], near_ref[0:8])
    y2 = jnp.where(even[0], y_ref[0:80], back_ref[16:96])
    z2 = jnp.where(even[0], back_ref[16:32], z_ref[0:16])
    deep_ref[0:80] = y2
    deep_ref[80:96] = z2
    above = [[above_ref[16 * k : 16 * k + 16] for k in range(4)]]
    below = [[below_ref[16 * k : 16 * k + 16] for k in range(4)]]
    for axis, a, b in ((1, y1, y2[0:16]), (2, z1, z2[0:8])):
        above.append(jnp.where(even[axis], a, b))
        below.append(jnp.where(even[axis], b, a))
    upstream = [[load(g_ref, s, 0)] for s in range(2)]
    middle = [[c[s][0]] for s in range(2)]
    for s in range(2):
        for axis in range(3):
            p, m = 1 + 2 * axis, 2 + 2 * axis
            upstream[s].append(moved(load(g_ref, s, p), axis, 1, above[axis], s))
            upstream[s].append(moved(load(g_ref, s, m), axis, -1, below[axis], s))
            middle[s].append(moved(c[s][p], axis, -1, below[axis], 2 + s))
            middle[s].append(moved(c[s][m], axis, 1, above[axis], 2 + s))
    later = [[[None] * nx for _ in range(7)] for _ in range(2)]
    for x in range(nx):
        up = [[upstream[s][q][x] for q in range(7)] for s in range(2)]
        mid = [[middle[s][q][x] for q in range(7)] for s in range(2)]
        rho = [total(mid[s]) for s in range(2)]
        earlier, rate_part, relax_part = adjoint(up, mid, rho, [inverse[s][x] for s in range(2)], rate[x])
        rate_ref[x] = rate_part
        for s in range(2):
            relax_ref[s, x] = relax_part[s]
            for q in range(7):
                later[s][q][x] = earlier[s][q]
                later_ref[s, q, x] = earlier[s][q]
    for ref, last in ((up_ref, True), (down_ref, False)):
        for s, face in enumerate(pack_x([later[s][2 if last else 1] for s in range(2)], last)):
            ref[16 * s : 16 * s + 16] = face
        ref[32:40] = y2[52:60]
        ref[40:48] = z2[8:16]
    for axis, pack, ref in ((1, pack_y, y1_ref), (2, pack_z, z1_ref)):
        a = pack([later[s][2 + 2 * axis] for s in range(2)], True)
        b = pack([later[s][1 + 2 * axis] for s in range(2)], False)
        ref[0:8] = jnp.where(even[axis], a, b)
    y1_ref[8:16] = z2[8:16]
    z1_ref[8:24] = y2[64:80]
    relay_ref[0:16] = y2[64:80]
    relay_ref[16:24] = z2[8:16]
    relay_ref[24:40] = y2[0:16]
    relay_ref[40:48] = z2[0:8]


def later_beyond(inner, moments, density, inverse, rate):
    scaled = rate * (moments[1] - moments[0])
    return [(1.0 - inverse[s]) * inner[s] + moments[s] * inverse[s] + scaled * density[1 - s] for s in range(2)]


def beyond_y(deep, own, x_above, x_below, z_above, z_below):
    nx = 4
    field = lambda k: deep[16 + nx * k : 16 + nx * k + nx]
    lane = lax.broadcasted_iota(jnp.int32, (nx, 128), 1)
    added = []
    for k in range(4):
        zero = jnp.zeros((nx - 2, 128), jnp.float32)
        x_part = jnp.concatenate([x_below[2 * k + 1 : 2 * k + 2], zero, x_above[2 * k : 2 * k + 1]], axis=0)
        high = pltpu.roll(z_above[nx * k : nx * k + nx], 127, axis=1)
        low = pltpu.roll(z_below[nx * k : nx * k + nx], 1, axis=1)
        z_part = jnp.where(lane == 127, high, jnp.where(lane == 0, low, 0.0))
        added.append(own[nx * k : nx * k + nx] + x_part + z_part)
    moments = [field(2 + s) + WEIGHTS[1] * added[s] for s in range(2)]
    density = [field(4 + s) + added[2 + s] for s in range(2)]
    out = later_beyond([field(0), field(1)], moments, density, [field(6), field(7)], field(8))
    return jnp.concatenate(out, axis=0)


def beyond_z(deep, own, x_above, x_below, y_above, y_below):
    lane = lax.broadcasted_iota(jnp.int32, (8, 128), 1)
    row = lax.broadcasted_iota(jnp.int32, (8, 128), 0)

    def at(v, shift):
        shift = shift % 128
        return pltpu.roll(v, shift, axis=1) if shift else v

    field = lambda k: at(deep, -32 - 8 * k)
    odd = lax.rem(lane, 2) == 1
    y_high, y_low = pltpu.roll(y_above, 7, axis=0), pltpu.roll(y_below, 1, axis=0)
    added = []
    for k in range(4):
        x_part = jnp.where(lane >= 6, at(x_above, 6 - 32 - 8 * k), 0.0)
        x_part = jnp.where(lane < 2, at(x_below, -6 - 32 - 8 * k), x_part)
        y_part = jnp.where((row == 7) & odd, at(y_high, 1 - 8 * k), 0.0)
        y_part = jnp.where((row == 0) & ~odd, at(y_low, -1 - 8 * k), y_part)
        added.append(at(own, -8 * k) + x_part + y_part)
    moments = [field(2 + s) + WEIGHTS[1] * added[s] for s in range(2)]
    density = [field(4 + s) + added[2 + s] for s in range(2)]
    out = later_beyond([field(0), field(1)], moments, density, [field(6), field(7)], field(8))
    return jnp.where(lane < 8, out[0], pltpu.roll(out[1], 8, axis=1))


def z_lines_of(packed, last):
    row, lane = (lax.broadcasted_iota(jnp.int32, (16, 128), d) for d in (0, 1))
    edge = jnp.where(last, packed[7:8], packed[0:1])
    wanted = lane == 2 * row + jnp.where(last, 1, 0)
    return jnp.broadcast_to(jnp.sum(jnp.where(wanted, edge, 0.0), axis=1, keepdims=True), (16, 128))


def y_lines_of(rows, last):
    row, lane = (lax.broadcasted_iota(jnp.int32, (16, 128), d) for d in (0, 1))
    wanted = lane == jnp.where(last, 127, 0)
    edge = jnp.sum(jnp.where(wanted, rows, 0.0), axis=1, keepdims=True)
    return jnp.broadcast_to(jnp.sum(jnp.where(lane // 2 == row, edge, 0.0), axis=0, keepdims=True), (8, 128))


def third_kernel(
    f_ref, r_ref, t_ref, later_ref, rate_late_ref, relax_late_ref, deep_ref, raw_ref, diag_ref,
    below_ref, above_ref, y1_ref, z1_ref, relay_ref, state_ref, rate_ref, relax_ref,
):
    even = parities()
    nx = r_ref.shape[0]
    far_y = far_along_y(lax.axis_index("gy"), lax.axis_size("gy"))
    far_z = far_along_z(lax.axis_index("gz"), lax.axis_size("gz"))
    alike = far_y == far_z
    lines1 = z1_ref[8:24]
    lines2 = jnp.where(far_y, relay_ref[0:16], z_lines_of(relay_ref[40:48], even[1]))
    lines2 = jnp.where(alike, diag_ref[0:16], lines2)
    y2 = beyond_y(
        deep_ref[0:80], raw_ref[0:16], above_ref[32:40], below_ref[32:40],
        jnp.where(even[2], lines1, lines2), jnp.where(even[2], lines2, lines1),
    )
    lines1 = y1_ref[8:16]
    lines2 = jnp.where(far_z, relay_ref[16:24], y_lines_of(relay_ref[24:40], even[2]))
    lines2 = jnp.where(alike, diag_ref[16:24], lines2)
    z2 = beyond_z(
        deep_ref[80:88], raw_ref[16:24], above_ref[40:48], below_ref[40:48],
        jnp.where(even[1], lines1, lines2), jnp.where(even[1], lines2, lines1),
    )
    above = [[above_ref[16 * k : 16 * k + 16] for k in range(2)]]
    below = [[below_ref[16 * k : 16 * k + 16] for k in range(2)]]
    for axis, a, b in ((1, y1_ref[0:8], y2), (2, z1_ref[0:8], z2)):
        above.append(jnp.where(even[axis], a, b))
        below.append(jnp.where(even[axis], b, a))
    upstream = [[load(later_ref, s, 0)] for s in range(2)]
    for s in range(2):
        for axis in range(3):
            upstream[s].append(moved(load(later_ref, s, 1 + 2 * axis), axis, 1, above[axis], s))
            upstream[s].append(moved(load(later_ref, s, 2 + 2 * axis), axis, -1, below[axis], s))
    for x in range(nx):
        up = [[upstream[s][q][x] for q in range(7)] for s in range(2)]
        state = [[f_ref[s, q, x] for q in range(7)] for s in range(2)]
        rho = [total(state[s]) for s in range(2)]
        inverse = [1.0 / t_ref[s, x] for s in range(2)]
        earlier, rate_part, relax_part = adjoint(up, state, rho, inverse, r_ref[x])
        rate_ref[x] = rate_late_ref[x] + rate_part
        for s in range(2):
            relax_ref[s, x] = relax_late_ref[s, x] + relax_part[s]
            for q in range(7):
                state_ref[s, q, x] = earlier[s][q]


def call(kernel, shapes, *args, source=pltpu.VMEM, scratch=()):
    return pl.pallas_call(
        kernel,
        out_shape=[jax.ShapeDtypeStruct(s, jnp.float32) for s in shapes],
        in_specs=[pl.BlockSpec(memory_space=source)] * len(args),
        out_specs=[pl.BlockSpec(memory_space=pltpu.VMEM)] * len(shapes),
        scratch_shapes=list(scratch),
        compiler_params=pltpu.CompilerParams(vmem_limit_bytes=32 * 1024 * 1024),
    )(*args)


def shifts(axis):
    count = lax.axis_size(axis)
    up = [(i, (i + 1) % count) for i in range(count)]
    return up, [(j, i) for i, j in up]


def far_along_y(index, count):
    return (index == 0) | (index == count - 1)


def far_along_z(index, count):
    half = count // 2
    return (index % half == 0) | (index % half == half - 1)


def grid_pairs(move):
    counts = tuple(lax.axis_size(a) for a in AXES)
    nx, ny, nz = counts
    pairs = []
    for x in range(nx):
        for y in range(ny):
            for z in range(nz):
                to = move(x, y, z, counts)
                if to is not None:
                    pairs.append(((x * ny + y) * nz + z, (to[0] * ny + to[1]) * nz + to[2]))
    return pairs


def near_move(x, y, z, counts):
    return (x, partner(y, counts[1], 0), z) if x % 2 == 0 else (x, y, partner(z, counts[2], 0))


def second_y_move(x, y, z, counts):
    return (x, partner(y, counts[1], 1), z) if x % 2 == 0 else None


def second_z_move(x, y, z, counts):
    return (x, y, partner(z, counts[2], 1)) if x % 2 == 1 else None


def diagonal_move(x, y, z, counts):
    if far_along_y(y, counts[1]) == far_along_z(z, counts[2]):
        return (x, partner(y, counts[1], 1), partner(z, counts[2], 1))
    return None


def relay_move(x, y, z, counts):
    far_y, far_z = far_along_y(y, counts[1]), far_along_z(z, counts[2])
    if far_y and not far_z:
        return (x, y, partner(z, counts[2], 1))
    return (x, partner(y, counts[1], 1), z) if far_z and not far_y else None


def first_exchange(up, down, own0, own1, diag):
    to_up, to_down = shifts("gx")
    below = lax.ppermute(up, "gx", to_up)
    above = lax.ppermute(down, "gx", to_down)
    y, z, near = call(forward_kernel, [(160, 128), (48, 128), (32, 128)], own0, own1, below, above)
    z_in = lax.ppermute(z, AXES, grid_pairs(second_z_move))
    y_in = lax.ppermute(y, AXES, grid_pairs(second_y_move))
    diag_in = lax.ppermute(diag, AXES, grid_pairs(diagonal_move))
    near_in = lax.ppermute(near, AXES, grid_pairs(near_move))
    (back,) = call(back_kernel, [(96, 128)], z_in, y_in, near_in)
    back_in = lax.ppermute(back, "gx", axis_pairs("gx", 0))
    return (below, above, z_in, y_in, near_in, back_in), diag_in


def second_exchange(up, down, y1, z1, relay):
    to_up, to_down = shifts("gx")
    return (
        lax.ppermute(up, "gx", to_up),
        lax.ppermute(down, "gx", to_down),
        lax.ppermute(y1, "gy", axis_pairs("gy", 0)),
        lax.ppermute(z1, "gz", axis_pairs("gz", 0)),
        lax.ppermute(relay, AXES, grid_pairs(relay_move)),
    )


def on_device(checkpoint, cotangent, reaction_rate, relax_time):
    inputs = (checkpoint, cotangent, reaction_rate, relax_time)
    messages = [(160, 128), (160, 128), (16, 128), (80, 128), (152, 128), (24, 128)]
    f, g, r, t, *sent, raw = call(
        first_kernel, [a.shape for a in inputs] + messages,
        *(pltpu.with_memory_space_constraint(a, pltpu.HBM) for a in inputs),
        source=pltpu.HBM, scratch=[pltpu.SemaphoreType.DMA((4,))],
    )
    received, diag_in = first_exchange(*sent)
    messages = [(96, 128), (48, 128), (48, 128), (16, 128), (24, 128), (48, 128)]
    later, rate_late, relax_late, deep, *sent = call(
        second_kernel, [f.shape, r.shape, t.shape] + messages, f, g, r, t, *received
    )
    received = second_exchange(*sent)
    return tuple(
        call(
            third_kernel, [f.shape, r.shape, t.shape],
            f, r, t, later, rate_late, relax_late, deep, raw, diag_in, *received,
        )
    )


def solution(mesh):
    placed = (
        P(None, None, "gx", "gy", "gz"),
        P(None, None, "gx", "gy", "gz"),
        P("gx", "gy", "gz"),
        P(None, "gx", "gy", "gz"),
    )
    return jax.shard_map(
        on_device,
        mesh=mesh,
        in_specs=placed,
        out_specs=(P(None, None, "gx", "gy", "gz"), P("gx", "gy", "gz"), P(None, "gx", "gy", "gz")),
        check_vma=False,
    )
```

```python
import jax
import jax.numpy as jnp
from jax import lax
from jax.experimental import pallas as pl
from jax.experimental.pallas import tpu as pltpu
from jax.sharding import PartitionSpec as P

WEIGHTS = (0.25, 0.125, 0.125, 0.125, 0.125, 0.125, 0.125)
AXES = ("gx", "gy", "gz")


def partner(index, count, color):
    if color == 0:
        return index ^ 1
    return (index + 1) % count if index % 2 else (index - 1) % count


def axis_pairs(axis, color):
    count = lax.axis_size(axis)
    return [(i, partner(i, count, color)) for i in range(count)]


def parities():
    return tuple(lax.rem(lax.axis_index(a), 2) == 0 for a in AXES)


def load(ref, *lead):
    return [ref[lead + (x,)] for x in range(ref.shape[len(lead)])]


def total(terms):
    out = terms[0]
    for t in terms[1:]:
        out = out + t
    return out


def collided(f_ref, r_ref, t_ref):
    nx = r_ref.shape[0]
    rate = load(r_ref)
    inverse = [[1.0 / t for t in load(t_ref, s)] for s in range(2)]
    f = [[load(f_ref, s, q) for q in range(7)] for s in range(2)]
    rho = [[total([f[s][q][x] for q in range(7)]) for x in range(nx)] for s in range(2)]
    c = [[[None] * nx for _ in range(7)] for _ in range(2)]
    for x in range(nx):
        reaction = rate[x] * rho[0][x] * rho[1][x]
        for s in range(2):
            source = reaction if s == 1 else -reaction
            for q in range(7):
                w = WEIGHTS[q]
                v = f[s][q][x]
                c[s][q][x] = v - (v - w * rho[s][x]) * inverse[s][x] + w * source
    return c, rho, inverse, rate


def pack_x(fields, last):
    return [v[-1] if last else v[0] for v in fields]


def rows_of(v, i):
    return jnp.concatenate([plane[i : i + 1] for plane in v], axis=0)


def pack_y(fields, last):
    n = fields[0][0].shape[0]
    return jnp.concatenate([rows_of(v, n - 1 if last else 0) for v in fields], axis=0)


def pack_z(fields, last, start=0, out=None):
    lane = lax.broadcasted_iota(jnp.int32, (8, 128), 1)
    out = jnp.zeros((8, 128), jnp.float32) if out is None else out
    j = start
    for v in fields:
        for plane in v:
            for h in range(plane.shape[0] // 8):
                part = plane[8 * h : 8 * h + 8]
                shift = (j + 1) % 128 if last else j
                part = pltpu.roll(part, shift, axis=1) if shift else part
                out = jnp.where(lane == j, part, out)
                j += 1
    return out


def cut(v, axis, sign):
    if axis == 0:
        zero = jnp.zeros_like(v[0])
        return v[1:] + [zero] if sign > 0 else [zero] + v[:-1]
    out = []
    for plane in v:
        n = plane.shape[axis - 1]
        at = lax.broadcasted_iota(jnp.int32, plane.shape, axis - 1)
        rolled = pltpu.roll(plane, n - 1 if sign > 0 else 1, axis=axis - 1)
        out.append(jnp.where(at == (n - 1 if sign > 0 else 0), 0.0, rolled))
    return out


def plus(a, b):
    return [x + y for x, y in zip(a, b)]


def partial_sums(g, c, axes):
    moments, density = [], []
    for s in range(2):
        m = [WEIGHTS[1] * v for v in cut(g[s][1 + 2 * axes[0]], axes[0], 1)]
        d = plus(c[s][0], cut(c[s][1 + 2 * axes[0]], axes[0], -1))
        m = plus(m, [WEIGHTS[1] * v for v in cut(g[s][2 + 2 * axes[0]], axes[0], -1)])
        d = plus(d, cut(c[s][2 + 2 * axes[0]], axes[0], 1))
        m = plus(m, [WEIGHTS[1] * v for v in cut(g[s][1 + 2 * axes[1]], axes[1], 1)])
        d = plus(d, cut(c[s][1 + 2 * axes[1]], axes[1], -1))
        m = plus(m, [WEIGHTS[1] * v for v in cut(g[s][2 + 2 * axes[1]], axes[1], -1)])
        d = plus(d, cut(c[s][2 + 2 * axes[1]], axes[1], 1))
        moments.append(plus(m, [WEIGHTS[0] * v for v in g[s][0]]))
        density.append(d)
    return moments, density


def face_fields(g, c, moments, density, inverse, rate, axis, last):
    out_q, in_q = (1 + 2 * axis, 2 + 2 * axis) if last else (2 + 2 * axis, 1 + 2 * axis)
    sign = -1 if last else 1
    inner = [cut(g[s][in_q], axis, sign) for s in range(2)]
    m = [plus(moments[s], [WEIGHTS[1] * v for v in inner[s]]) for s in range(2)]
    d = [plus(density[s], cut(c[s][out_q], axis, sign)) for s in range(2)]
    return [*inner, *m, *d, *inverse, rate]


def edge_fields(g, c, axis):
    p, m = 1 + 2 * axis, 2 + 2 * axis
    return [(g[0][p], g[0][m]), (g[1][p], g[1][m]), (c[0][m], c[0][p]), (c[1][m], c[1][p])]


def first_kernel(
    f_hbm, g_hbm, r_hbm, t_hbm, f_ref, g_ref, r_ref, t_ref, up_ref, down_ref, own0_ref, own1_ref, diag_ref, raw_ref, sems
):
    copies = [
        pltpu.make_async_copy(a, b, sems.at[i])
        for i, (a, b) in enumerate(((f_hbm, f_ref), (g_hbm, g_ref), (r_hbm, r_ref), (t_hbm, t_ref)))
    ]
    for copy in copies:
        copy.start()
    for copy in copies:
        copy.wait()
    even = parities()
    c, _, inverse, rate = collided(f_ref, r_ref, t_ref)
    g = [[load(g_ref, s, q) for q in range(7)] for s in range(2)]
    up, down = [], []
    for axis in range(3):
        p, m = 1 + 2 * axis, 2 + 2 * axis
        up.append([g[0][m], g[1][m], c[0][p], c[1][p]])
        down.append([g[0][p], g[1][p], c[0][m], c[1][m]])
    for k, (u, d) in enumerate(zip(pack_x(up[0], True), pack_x(down[0], False))):
        up_ref[16 * k : 16 * k + 16] = u
        down_ref[16 * k : 16 * k + 16] = d
    nx, n = len(rate), rate[0].shape[0]
    lane = lax.broadcasted_iota(jnp.int32, (nx, 128), 1)
    row = lax.broadcasted_iota(jnp.int32, (n, 128), 0)
    x_edge, y_edge, z_edge = (edge_fields(g, c, axis) for axis in range(3))
    y_faces, z_faces = [], []
    y_sums, z_sums = partial_sums(g, c, (0, 2)), partial_sums(g, c, (0, 1))
    for last in (False, True):
        i = n - 1 if last else 0
        raw = pack_y((up if last else down)[1], last)
        deep = pack_y(face_fields(g, c, *y_sums, inverse, rate, 1, last), last)
        x_lines = [line for a, b in x_edge for line in (a[0][i : i + 1], b[-1][i : i + 1])]
        x_lines.append(jnp.zeros((28 - 4 * len(rate) - len(x_lines), 128), jnp.float32))
        z_lines = [jnp.where(lane < 64, rows_of(a, i), rows_of(b, i)) for a, b in z_edge]
        y_faces.append((raw, jnp.concatenate([raw, deep, *x_lines], axis=0), jnp.concatenate(z_lines, axis=0)))
        raw = pack_z((up if last else down)[2], last)
        deep = pack_z(face_fields(g, c, *z_sums, inverse, rate, 2, last), last, 32, raw)
        y_lines = [[jnp.where(row < 8, u, v) for u, v in zip(a, b)] for a, b in y_edge]
        x_lines = [a[:-1] + b[-1:] for a, b in x_edge]
        z_faces.append((raw, deep, pack_z(y_lines + x_lines, last)))
    y1, y2 = jnp.where(even[1], y_faces[1][0], y_faces[0][0]), jnp.where(even[1], y_faces[0][0], y_faces[1][0])
    z1, z2 = jnp.where(even[2], z_faces[1][0], z_faces[0][0]), jnp.where(even[2], z_faces[0][0], z_faces[1][0])
    y_deep = jnp.where(even[1], y_faces[0][1], y_faces[1][1])
    y_lines = jnp.where(even[1], y_faces[0][2], y_faces[1][2])
    z_deep = jnp.where(even[2], z_faces[0][1], z_faces[1][1])
    z_lines = jnp.where(even[2], z_faces[0][2], z_faces[1][2])
    raw_ref[0:16] = y2
    raw_ref[16:24] = z2
    diag_ref[0:16] = y_lines
    diag_ref[16:24] = z_lines
    rest = diag_ref.shape[0] - 24
    diag_ref[24:] = jnp.zeros((rest, 128), jnp.float32)
    z1 = jnp.concatenate([z1, jnp.zeros_like(z1)], axis=0)
    y_all = jnp.concatenate([y_deep, y_lines], axis=0)
    z_all = jnp.concatenate([z_deep, z_lines, jnp.zeros((y_all.shape[0] - 16, 128), jnp.float32)], axis=0)
    own0_ref[...] = jnp.where(even[0], y1, z1)
    own1_ref[...] = jnp.where(even[0], y_all, z_all)
    up_ref[64:80] = z1
    up_ref[80:96] = z_all[0:16]
    down_ref[64:80] = y1
    down_ref[80:160] = y_all


def forward_kernel(own0_ref, own1_ref, above_ref, below_ref, y_ref, near_ref, z_ref):
    even = parities()
    near_ref[0:16] = own0_ref[...]
    near_ref[16:32] = jnp.where(even[0], above_ref[64:80], below_ref[64:80])
    near_ref[32:40] = jnp.zeros((8, 128), jnp.float32)
    y_ref[0:80] = own1_ref[...]
    y_ref[80:160] = above_ref[80:160]
    z_ref[0:16] = own1_ref[0:16]
    z_ref[16:32] = below_ref[80:96]


def back_kernel(z_ref, y_ref, near_ref, out_ref):
    even = parities()
    out_ref[0:16] = near_ref[16:32]
    out_ref[16:32] = jnp.where(even[0], y_ref[80:96], z_ref[16:32])
    out_ref[32:96] = y_ref[96:160]


def moved(v, axis, sign, halo, k):
    if axis == 0:
        return v[1:] + [halo[k]] if sign > 0 else [halo[k]] + v[:-1]
    nx, (n, lanes) = len(v), v[0].shape
    out = []
    for x in range(nx):
        plane = v[x]
        if axis == 1:
            row = lax.broadcasted_iota(jnp.int32, (n, lanes), 0)
            edge = halo[k * nx + x : k * nx + x + 1]
            rolled = pltpu.roll(plane, n - 1 if sign > 0 else 1, axis=0)
            out.append(jnp.where(row == (n - 1 if sign > 0 else 0), edge, rolled))
        else:
            lane = lax.broadcasted_iota(jnp.int32, (n, lanes), 1)
            parts = []
            for h in range(n // 8):
                j = (k * nx + x) * (n // 8) + h
                shift = (lanes - 1 - j) % lanes if sign > 0 else (lanes - j) % lanes
                parts.append(pltpu.roll(halo, shift, axis=1) if shift else halo)
            edge = jnp.concatenate(parts, axis=0)
            rolled = pltpu.roll(plane, lanes - 1 if sign > 0 else 1, axis=1)
            out.append(jnp.where(lane == (lanes - 1 if sign > 0 else 0), edge, rolled))
    return out


def adjoint(upstream, state, rho, inverse, rate):
    moments = [total([WEIGHTS[q] * upstream[s][q] for q in range(7)]) for s in range(2)]
    contrast = moments[1] - moments[0]
    scaled = rate * contrast
    earlier, relax = [], []
    for s in range(2):
        keep = 1.0 - inverse[s]
        add = moments[s] * inverse[s] + scaled * rho[1 - s]
        earlier.append([keep * upstream[s][q] + add for q in range(7)])
        part = total([upstream[s][q] * (state[s][q] - WEIGHTS[q] * rho[s]) for q in range(7)])
        relax.append(part * inverse[s] * inverse[s])
    return earlier, rho[0] * rho[1] * contrast, relax


def second_kernel(
    f_ref, g_ref, r_ref, t_ref, below_ref, above_ref, z_ref, y_ref, near_ref, back_ref,
    later_ref, rate_ref, relax_ref, deep_ref, up_ref, down_ref, y1_ref, z1_ref, relay_ref,
):
    even = parities()
    nx = r_ref.shape[0]
    c, _, inverse, rate = collided(f_ref, r_ref, t_ref)
    y1 = jnp.where(even[0], near_ref[0:16], back_ref[0:16])
    z1 = jnp.where(even[0], back_ref[0:8], near_ref[0:8])
    y2 = jnp.where(even[0], y_ref[0:80], back_ref[16:96])
    z2 = jnp.where(even[0], back_ref[16:32], z_ref[0:16])
    deep_ref[0:80] = y2
    deep_ref[80:96] = z2
    above = [[above_ref[16 * k : 16 * k + 16] for k in range(4)]]
    below = [[below_ref[16 * k : 16 * k + 16] for k in range(4)]]
    for axis, a, b in ((1, y1, y2[0:16]), (2, z1, z2[0:8])):
        above.append(jnp.where(even[axis], a, b))
        below.append(jnp.where(even[axis], b, a))
    upstream = [[load(g_ref, s, 0)] for s in range(2)]
    middle = [[c[s][0]] for s in range(2)]
    for s in range(2):
        for axis in range(3):
            p, m = 1 + 2 * axis, 2 + 2 * axis
            upstream[s].append(moved(load(g_ref, s, p), axis, 1, above[axis], s))
            upstream[s].append(moved(load(g_ref, s, m), axis, -1, below[axis], s))
            middle[s].append(moved(c[s][p], axis, -1, below[axis], 2 + s))
            middle[s].append(moved(c[s][m], axis, 1, above[axis], 2 + s))
    later = [[[None] * nx for _ in range(7)] for _ in range(2)]
    for x in range(nx):
        up = [[upstream[s][q][x] for q in range(7)] for s in range(2)]
        mid = [[middle[s][q][x] for q in range(7)] for s in range(2)]
        rho = [total(mid[s]) for s in range(2)]
        earlier, rate_part, relax_part = adjoint(up, mid, rho, [inverse[s][x] for s in range(2)], rate[x])
        rate_ref[x] = rate_part
        for s in range(2):
            relax_ref[s, x] = relax_part[s]
            for q in range(7):
                later[s][q][x] = earlier[s][q]
                later_ref[s, q, x] = earlier[s][q]
    for ref, last in ((up_ref, True), (down_ref, False)):
        for s, face in enumerate(pack_x([later[s][2 if last else 1] for s in range(2)], last)):
            ref[16 * s : 16 * s + 16] = face
        ref[32:40] = y2[52:60]
        ref[40:48] = z2[8:16]
    for axis, pack, ref in ((1, pack_y, y1_ref), (2, pack_z, z1_ref)):
        a = pack([later[s][2 + 2 * axis] for s in range(2)], True)
        b = pack([later[s][1 + 2 * axis] for s in range(2)], False)
        ref[0:8] = jnp.where(even[axis], a, b)
    y1_ref[8:16] = z2[8:16]
    z1_ref[8:24] = y2[64:80]
    relay_ref[0:16] = y2[64:80]
    relay_ref[16:24] = z2[8:16]
    relay_ref[24:40] = y2[0:16]
    relay_ref[40:48] = z2[0:8]


def later_beyond(inner, moments, density, inverse, rate):
    scaled = rate * (moments[1] - moments[0])
    return [(1.0 - inverse[s]) * inner[s] + moments[s] * inverse[s] + scaled * density[1 - s] for s in range(2)]


def beyond_y(deep, own, x_above, x_below, z_above, z_below):
    nx = 4
    field = lambda k: deep[16 + nx * k : 16 + nx * k + nx]
    lane = lax.broadcasted_iota(jnp.int32, (nx, 128), 1)
    added = []
    for k in range(4):
        zero = jnp.zeros((nx - 2, 128), jnp.float32)
        x_part = jnp.concatenate([x_below[2 * k + 1 : 2 * k + 2], zero, x_above[2 * k : 2 * k + 1]], axis=0)
        high = pltpu.roll(z_above[nx * k : nx * k + nx], 127, axis=1)
        low = pltpu.roll(z_below[nx * k : nx * k + nx], 1, axis=1)
        z_part = jnp.where(lane == 127, high, jnp.where(lane == 0, low, 0.0))
        added.append(own[nx * k : nx * k + nx] + x_part + z_part)
    moments = [field(2 + s) + WEIGHTS[1] * added[s] for s in range(2)]
    density = [field(4 + s) + added[2 + s] for s in range(2)]
    out = later_beyond([field(0), field(1)], moments, density, [field(6), field(7)], field(8))
    return jnp.concatenate(out, axis=0)


def beyond_z(deep, own, x_above, x_below, y_above, y_below):
    lane = lax.broadcasted_iota(jnp.int32, (8, 128), 1)
    row = lax.broadcasted_iota(jnp.int32, (8, 128), 0)

    def at(v, shift):
        shift = shift % 128
        return pltpu.roll(v, shift, axis=1) if shift else v

    field = lambda k: at(deep, -32 - 8 * k)
    odd = lax.rem(lane, 2) == 1
    y_high, y_low = pltpu.roll(y_above, 7, axis=0), pltpu.roll(y_below, 1, axis=0)
    added = []
    for k in range(4):
        x_part = jnp.where(lane >= 6, at(x_above, 6 - 32 - 8 * k), 0.0)
        x_part = jnp.where(lane < 2, at(x_below, -6 - 32 - 8 * k), x_part)
        y_part = jnp.where((row == 7) & odd, at(y_high, 1 - 8 * k), 0.0)
        y_part = jnp.where((row == 0) & ~odd, at(y_low, -1 - 8 * k), y_part)
        added.append(at(own, -8 * k) + x_part + y_part)
    moments = [field(2 + s) + WEIGHTS[1] * added[s] for s in range(2)]
    density = [field(4 + s) + added[2 + s] for s in range(2)]
    out = later_beyond([field(0), field(1)], moments, density, [field(6), field(7)], field(8))
    return jnp.where(lane < 8, out[0], pltpu.roll(out[1], 8, axis=1))


def z_lines_of(packed, last):
    row, lane = (lax.broadcasted_iota(jnp.int32, (16, 128), d) for d in (0, 1))
    edge = jnp.where(last, packed[7:8], packed[0:1])
    wanted = lane == 2 * row + jnp.where(last, 1, 0)
    return jnp.broadcast_to(jnp.sum(jnp.where(wanted, edge, 0.0), axis=1, keepdims=True), (16, 128))


def y_lines_of(rows, last):
    row, lane = (lax.broadcasted_iota(jnp.int32, (16, 128), d) for d in (0, 1))
    wanted = lane == jnp.where(last, 127, 0)
    edge = jnp.sum(jnp.where(wanted, rows, 0.0), axis=1, keepdims=True)
    return jnp.broadcast_to(jnp.sum(jnp.where(lane // 2 == row, edge, 0.0), axis=0, keepdims=True), (8, 128))


def third_kernel(
    f_ref, r_ref, t_ref, later_ref, rate_late_ref, relax_late_ref, deep_ref, raw_ref, diag_ref,
    below_ref, above_ref, y1_ref, z1_ref, relay_ref, state_ref, rate_ref, relax_ref,
):
    even = parities()
    nx = r_ref.shape[0]
    far_y = far_along_y(lax.axis_index("gy"), lax.axis_size("gy"))
    far_z = far_along_z(lax.axis_index("gz"), lax.axis_size("gz"))
    alike = far_y == far_z
    lines1 = z1_ref[8:24]
    lines2 = jnp.where(far_y, relay_ref[0:16], z_lines_of(relay_ref[40:48], even[1]))
    lines2 = jnp.where(alike, diag_ref[0:16], lines2)
    y2 = beyond_y(
        deep_ref[0:80], raw_ref[0:16], above_ref[32:40], below_ref[32:40],
        jnp.where(even[2], lines1, lines2), jnp.where(even[2], lines2, lines1),
    )
    lines1 = y1_ref[8:16]
    lines2 = jnp.where(far_z, relay_ref[16:24], y_lines_of(relay_ref[24:40], even[2]))
    lines2 = jnp.where(alike, diag_ref[16:24], lines2)
    z2 = beyond_z(
        deep_ref[80:88], raw_ref[16:24], above_ref[40:48], below_ref[40:48],
        jnp.where(even[1], lines1, lines2), jnp.where(even[1], lines2, lines1),
    )
    above = [[above_ref[16 * k : 16 * k + 16] for k in range(2)]]
    below = [[below_ref[16 * k : 16 * k + 16] for k in range(2)]]
    for axis, a, b in ((1, y1_ref[0:8], y2), (2, z1_ref[0:8], z2)):
        above.append(jnp.where(even[axis], a, b))
        below.append(jnp.where(even[axis], b, a))
    upstream = [[load(later_ref, s, 0)] for s in range(2)]
    for s in range(2):
        for axis in range(3):
            upstream[s].append(moved(load(later_ref, s, 1 + 2 * axis), axis, 1, above[axis], s))
            upstream[s].append(moved(load(later_ref, s, 2 + 2 * axis), axis, -1, below[axis], s))
    for x in range(nx):
        up = [[upstream[s][q][x] for q in range(7)] for s in range(2)]
        state = [[f_ref[s, q, x] for q in range(7)] for s in range(2)]
        rho = [total(state[s]) for s in range(2)]
        inverse = [1.0 / t_ref[s, x] for s in range(2)]
        earlier, rate_part, relax_part = adjoint(up, state, rho, inverse, r_ref[x])
        rate_ref[x] = rate_late_ref[x] + rate_part
        for s in range(2):
            relax_ref[s, x] = relax_late_ref[s, x] + relax_part[s]
            for q in range(7):
                state_ref[s, q, x] = earlier[s][q]


def call(kernel, shapes, *args, source=pltpu.VMEM, scratch=()):
    return pl.pallas_call(
        kernel,
        out_shape=[jax.ShapeDtypeStruct(s, jnp.float32) for s in shapes],
        in_specs=[pl.BlockSpec(memory_space=source)] * len(args),
        out_specs=[pl.BlockSpec(memory_space=pltpu.VMEM)] * len(shapes),
        scratch_shapes=list(scratch),
        compiler_params=pltpu.CompilerParams(vmem_limit_bytes=32 * 1024 * 1024),
    )(*args)


def shifts(axis):
    count = lax.axis_size(axis)
    up = [(i, (i + 1) % count) for i in range(count)]
    return up, [(j, i) for i, j in up]


def far_along_y(index, count):
    return (index == 0) | (index == count - 1)


def far_along_z(index, count):
    half = count // 2
    return (index % half == 0) | (index % half == half - 1)


def grid_pairs(move):
    counts = tuple(lax.axis_size(a) for a in AXES)
    nx, ny, nz = counts
    pairs = []
    for x in range(nx):
        for y in range(ny):
            for z in range(nz):
                to = move(x, y, z, counts)
                if to is not None:
                    pairs.append(((x * ny + y) * nz + z, (to[0] * ny + to[1]) * nz + to[2]))
    return pairs


def near_move(x, y, z, counts):
    return (x, partner(y, counts[1], 0), z) if x % 2 == 0 else (x, y, partner(z, counts[2], 0))


def second_y_move(x, y, z, counts):
    return (x, partner(y, counts[1], 1), z) if x % 2 == 0 else None


def second_z_move(x, y, z, counts):
    return (x, y, partner(z, counts[2], 1)) if x % 2 == 1 else None


def diagonal_move(x, y, z, counts):
    if far_along_y(y, counts[1]) == far_along_z(z, counts[2]):
        return (x, partner(y, counts[1], 1), partner(z, counts[2], 1))
    return None


def relay_move(x, y, z, counts):
    far_y, far_z = far_along_y(y, counts[1]), far_along_z(z, counts[2])
    if far_y and not far_z:
        return (x, y, partner(z, counts[2], 1))
    return (x, partner(y, counts[1], 1), z) if far_z and not far_y else None


def first_exchange(up, down, own0, own1, diag):
    to_up, to_down = shifts("gx")
    above = lax.ppermute(down, "gx", to_down)
    below = lax.ppermute(up, "gx", to_up)
    y, near, z = call(forward_kernel, [(160, 128), (40, 128), (32, 128)], own0, own1, above, below)
    z_in = lax.ppermute(z, AXES, grid_pairs(second_z_move))
    y_in = lax.ppermute(y, AXES, grid_pairs(second_y_move))
    diag_in = lax.ppermute(diag, AXES, grid_pairs(diagonal_move))
    near_in = lax.ppermute(near, AXES, grid_pairs(near_move))
    (back,) = call(back_kernel, [(96, 128)], z_in, y_in, near_in)
    back_in = lax.ppermute(back, "gx", axis_pairs("gx", 0))
    return (below, above, z_in, y_in, near_in, back_in), diag_in


def second_exchange(up, down, y1, z1, relay):
    to_up, to_down = shifts("gx")
    return (
        lax.ppermute(up, "gx", to_up),
        lax.ppermute(down, "gx", to_down),
        lax.ppermute(y1, "gy", axis_pairs("gy", 0)),
        lax.ppermute(z1, "gz", axis_pairs("gz", 0)),
        lax.ppermute(relay, AXES, grid_pairs(relay_move)),
    )


def on_device(checkpoint, cotangent, reaction_rate, relax_time):
    inputs = (checkpoint, cotangent, reaction_rate, relax_time)
    messages = [(96, 128), (160, 128), (16, 128), (80, 128), (136, 128), (24, 128)]
    f, g, r, t, *sent, raw = call(
        first_kernel, [a.shape for a in inputs] + messages,
        *(pltpu.with_memory_space_constraint(a, pltpu.HBM) for a in inputs),
        source=pltpu.HBM, scratch=[pltpu.SemaphoreType.DMA((4,))],
    )
    received, diag_in = first_exchange(*sent)
    messages = [(96, 128), (48, 128), (48, 128), (16, 128), (24, 128), (48, 128)]
    later, rate_late, relax_late, deep, *sent = call(
        second_kernel, [f.shape, r.shape, t.shape] + messages, f, g, r, t, *received
    )
    received = second_exchange(*sent)
    return tuple(
        call(
            third_kernel, [f.shape, r.shape, t.shape],
            f, r, t, later, rate_late, relax_late, deep, raw, diag_in, *received,
        )
    )


def solution(mesh):
    placed = (
        P(None, None, "gx", "gy", "gz"),
        P(None, None, "gx", "gy", "gz"),
        P("gx", "gy", "gz"),
        P(None, "gx", "gy", "gz"),
    )
    return jax.shard_map(
        on_device,
        mesh=mesh,
        in_specs=placed,
        out_specs=(P(None, None, "gx", "gy", "gz"), P("gx", "gy", "gz"), P(None, "gx", "gy", "gz")),
        check_vma=False,
    )
```

```python
import jax
import jax.numpy as jnp
from jax import lax
from jax.experimental import pallas as pl
from jax.experimental.pallas import tpu as pltpu
from jax.sharding import PartitionSpec as P

WEIGHTS = (0.25, 0.125, 0.125, 0.125, 0.125, 0.125, 0.125)
AXES = ("gx", "gy", "gz")


def partner(index, count, color):
    if color == 0:
        return index ^ 1
    return (index + 1) % count if index % 2 else (index - 1) % count


def axis_pairs(axis, color):
    count = lax.axis_size(axis)
    return [(i, partner(i, count, color)) for i in range(count)]


def parities():
    return tuple(lax.rem(lax.axis_index(a), 2) == 0 for a in AXES)


def load(ref, *lead):
    return [ref[lead + (x,)] for x in range(ref.shape[len(lead)])]


def total(terms):
    out = terms[0]
    for t in terms[1:]:
        out = out + t
    return out


def collided(f_ref, r_ref, t_ref):
    nx = r_ref.shape[0]
    rate = load(r_ref)
    inverse = [[1.0 / t for t in load(t_ref, s)] for s in range(2)]
    f = [[load(f_ref, s, q) for q in range(7)] for s in range(2)]
    rho = [[total([f[s][q][x] for q in range(7)]) for x in range(nx)] for s in range(2)]
    c = [[[None] * nx for _ in range(7)] for _ in range(2)]
    for x in range(nx):
        reaction = rate[x] * rho[0][x] * rho[1][x]
        for s in range(2):
            source = reaction if s == 1 else -reaction
            for q in range(7):
                w = WEIGHTS[q]
                v = f[s][q][x]
                c[s][q][x] = v - (v - w * rho[s][x]) * inverse[s][x] + w * source
    return c, rho, inverse, rate


def pack_x(fields, last):
    return [v[-1] if last else v[0] for v in fields]


def rows_of(v, i):
    return jnp.concatenate([plane[i : i + 1] for plane in v], axis=0)


def pack_y(fields, last):
    n = fields[0][0].shape[0]
    return jnp.concatenate([rows_of(v, n - 1 if last else 0) for v in fields], axis=0)


def pack_z(fields, last, start=0, out=None):
    lane = lax.broadcasted_iota(jnp.int32, (8, 128), 1)
    out = jnp.zeros((8, 128), jnp.float32) if out is None else out
    j = start
    for v in fields:
        for plane in v:
            for h in range(plane.shape[0] // 8):
                part = plane[8 * h : 8 * h + 8]
                shift = (j + 1) % 128 if last else j
                part = pltpu.roll(part, shift, axis=1) if shift else part
                out = jnp.where(lane == j, part, out)
                j += 1
    return out


def cut(v, axis, sign):
    if axis == 0:
        zero = jnp.zeros_like(v[0])
        return v[1:] + [zero] if sign > 0 else [zero] + v[:-1]
    out = []
    for plane in v:
        n = plane.shape[axis - 1]
        at = lax.broadcasted_iota(jnp.int32, plane.shape, axis - 1)
        rolled = pltpu.roll(plane, n - 1 if sign > 0 else 1, axis=axis - 1)
        out.append(jnp.where(at == (n - 1 if sign > 0 else 0), 0.0, rolled))
    return out


def plus(a, b):
    return [x + y for x, y in zip(a, b)]


def partial_sums(g, c, axes):
    moments, density = [], []
    for s in range(2):
        m = [WEIGHTS[1] * v for v in cut(g[s][1 + 2 * axes[0]], axes[0], 1)]
        d = plus(c[s][0], cut(c[s][1 + 2 * axes[0]], axes[0], -1))
        m = plus(m, [WEIGHTS[1] * v for v in cut(g[s][2 + 2 * axes[0]], axes[0], -1)])
        d = plus(d, cut(c[s][2 + 2 * axes[0]], axes[0], 1))
        m = plus(m, [WEIGHTS[1] * v for v in cut(g[s][1 + 2 * axes[1]], axes[1], 1)])
        d = plus(d, cut(c[s][1 + 2 * axes[1]], axes[1], -1))
        m = plus(m, [WEIGHTS[1] * v for v in cut(g[s][2 + 2 * axes[1]], axes[1], -1)])
        d = plus(d, cut(c[s][2 + 2 * axes[1]], axes[1], 1))
        moments.append(plus(m, [WEIGHTS[0] * v for v in g[s][0]]))
        density.append(d)
    return moments, density


def face_fields(g, c, moments, density, inverse, rate, axis, last):
    out_q, in_q = (1 + 2 * axis, 2 + 2 * axis) if last else (2 + 2 * axis, 1 + 2 * axis)
    sign = -1 if last else 1
    inner = [cut(g[s][in_q], axis, sign) for s in range(2)]
    m = [plus(moments[s], [WEIGHTS[1] * v for v in inner[s]]) for s in range(2)]
    d = [plus(density[s], cut(c[s][out_q], axis, sign)) for s in range(2)]
    return [*inner, *m, *d, *inverse, rate]


def edge_fields(g, c, axis):
    p, m = 1 + 2 * axis, 2 + 2 * axis
    return [(g[0][p], g[0][m]), (g[1][p], g[1][m]), (c[0][m], c[0][p]), (c[1][m], c[1][p])]


def first_kernel(
    f_hbm, g_hbm, r_hbm, t_hbm, f_ref, g_ref, r_ref, t_ref, up_ref, down_ref, own0_ref, own1_ref, diag_ref, raw_ref, sems
):
    copies = [
        pltpu.make_async_copy(a, b, sems.at[i])
        for i, (a, b) in enumerate(((f_hbm, f_ref), (g_hbm, g_ref), (r_hbm, r_ref), (t_hbm, t_ref)))
    ]
    for copy in copies:
        copy.start()
    for copy in copies:
        copy.wait()
    even = parities()
    c, _, inverse, rate = collided(f_ref, r_ref, t_ref)
    g = [[load(g_ref, s, q) for q in range(7)] for s in range(2)]
    up, down = [], []
    for axis in range(3):
        p, m = 1 + 2 * axis, 2 + 2 * axis
        up.append([g[0][m], g[1][m], c[0][p], c[1][p]])
        down.append([g[0][p], g[1][p], c[0][m], c[1][m]])
    for k, (u, d) in enumerate(zip(pack_x(up[0], True), pack_x(down[0], False))):
        up_ref[16 * k : 16 * k + 16] = u
        down_ref[16 * k : 16 * k + 16] = d
    nx, n = len(rate), rate[0].shape[0]
    lane = lax.broadcasted_iota(jnp.int32, (nx, 128), 1)
    row = lax.broadcasted_iota(jnp.int32, (n, 128), 0)
    x_edge, y_edge, z_edge = (edge_fields(g, c, axis) for axis in range(3))
    y_faces, z_faces = [], []
    y_sums, z_sums = partial_sums(g, c, (0, 2)), partial_sums(g, c, (0, 1))
    for last in (False, True):
        i = n - 1 if last else 0
        raw = pack_y((up if last else down)[1], last)
        deep = pack_y(face_fields(g, c, *y_sums, inverse, rate, 1, last), last)
        x_lines = [line for a, b in x_edge for line in (a[0][i : i + 1], b[-1][i : i + 1])]
        x_lines.append(jnp.zeros((28 - 4 * len(rate) - len(x_lines), 128), jnp.float32))
        z_lines = [jnp.where(lane < 64, rows_of(a, i), rows_of(b, i)) for a, b in z_edge]
        y_faces.append((raw, jnp.concatenate([raw, deep, *x_lines], axis=0), jnp.concatenate(z_lines, axis=0)))
        raw = pack_z((up if last else down)[2], last)
        deep = pack_z(face_fields(g, c, *z_sums, inverse, rate, 2, last), last, 32, raw)
        y_lines = [[jnp.where(row < 8, u, v) for u, v in zip(a, b)] for a, b in y_edge]
        x_lines = [a[:-1] + b[-1:] for a, b in x_edge]
        z_faces.append((raw, deep, pack_z(y_lines + x_lines, last)))
    y1, y2 = jnp.where(even[1], y_faces[1][0], y_faces[0][0]), jnp.where(even[1], y_faces[0][0], y_faces[1][0])
    z1, z2 = jnp.where(even[2], z_faces[1][0], z_faces[0][0]), jnp.where(even[2], z_faces[0][0], z_faces[1][0])
    y_deep = jnp.where(even[1], y_faces[0][1], y_faces[1][1])
    y_lines = jnp.where(even[1], y_faces[0][2], y_faces[1][2])
    z_deep = jnp.where(even[2], z_faces[0][1], z_faces[1][1])
    z_lines = jnp.where(even[2], z_faces[0][2], z_faces[1][2])
    raw_ref[0:16] = y2
    raw_ref[16:24] = z2
    diag_ref[0:16] = y_lines
    diag_ref[16:24] = z_lines
    rest = diag_ref.shape[0] - 24
    diag_ref[24:] = jnp.zeros((rest, 128), jnp.float32)
    z1 = jnp.concatenate([z1, jnp.zeros_like(z1)], axis=0)
    y_all = jnp.concatenate([y_deep, y_lines], axis=0)
    z_all = jnp.concatenate([z_deep, z_lines, jnp.zeros((y_all.shape[0] - 16, 128), jnp.float32)], axis=0)
    own0_ref[...] = jnp.where(even[0], y1, z1)
    own1_ref[...] = jnp.where(even[0], y_all, z_all)
    for ref in (up_ref, down_ref):
        ref[64:80] = jnp.where(even[0], z1, y1)
        ref[80:160] = jnp.where(even[0], z_all, y_all)


def forward_kernel(own0_ref, own1_ref, below_ref, above_ref, y_ref, near_ref, z_ref):
    even = parities()
    near_ref[0:16] = own0_ref[...]
    near_ref[16:32] = jnp.where(even[0], above_ref[64:80], below_ref[64:80])
    near_ref[32:40] = jnp.zeros((8, 128), jnp.float32)
    share = jnp.where(even[0], above_ref[80:160], below_ref[80:160])
    y_ref[0:80] = own1_ref[...]
    y_ref[80:160] = share
    z_ref[0:16] = own1_ref[0:16]
    z_ref[16:32] = share[0:16]


def back_kernel(z_ref, y_ref, near_ref, out_ref):
    even = parities()
    out_ref[0:16] = near_ref[16:32]
    out_ref[16:32] = jnp.where(even[0], y_ref[80:96], z_ref[16:32])
    out_ref[32:96] = y_ref[96:160]


def moved(v, axis, sign, halo, k):
    if axis == 0:
        return v[1:] + [halo[k]] if sign > 0 else [halo[k]] + v[:-1]
    nx, (n, lanes) = len(v), v[0].shape
    out = []
    for x in range(nx):
        plane = v[x]
        if axis == 1:
            row = lax.broadcasted_iota(jnp.int32, (n, lanes), 0)
            edge = halo[k * nx + x : k * nx + x + 1]
            rolled = pltpu.roll(plane, n - 1 if sign > 0 else 1, axis=0)
            out.append(jnp.where(row == (n - 1 if sign > 0 else 0), edge, rolled))
        else:
            lane = lax.broadcasted_iota(jnp.int32, (n, lanes), 1)
            parts = []
            for h in range(n // 8):
                j = (k * nx + x) * (n // 8) + h
                shift = (lanes - 1 - j) % lanes if sign > 0 else (lanes - j) % lanes
                parts.append(pltpu.roll(halo, shift, axis=1) if shift else halo)
            edge = jnp.concatenate(parts, axis=0)
            rolled = pltpu.roll(plane, lanes - 1 if sign > 0 else 1, axis=1)
            out.append(jnp.where(lane == (lanes - 1 if sign > 0 else 0), edge, rolled))
    return out


def adjoint(upstream, state, rho, inverse, rate):
    moments = [total([WEIGHTS[q] * upstream[s][q] for q in range(7)]) for s in range(2)]
    contrast = moments[1] - moments[0]
    scaled = rate * contrast
    earlier, relax = [], []
    for s in range(2):
        keep = 1.0 - inverse[s]
        add = moments[s] * inverse[s] + scaled * rho[1 - s]
        earlier.append([keep * upstream[s][q] + add for q in range(7)])
        part = total([upstream[s][q] * (state[s][q] - WEIGHTS[q] * rho[s]) for q in range(7)])
        relax.append(part * inverse[s] * inverse[s])
    return earlier, rho[0] * rho[1] * contrast, relax


def second_kernel(
    f_ref, g_ref, r_ref, t_ref, below_ref, above_ref, z_ref, y_ref, near_ref, back_ref,
    later_ref, rate_ref, relax_ref, deep_ref, up_ref, down_ref, y1_ref, z1_ref, relay_ref,
):
    even = parities()
    nx = r_ref.shape[0]
    c, _, inverse, rate = collided(f_ref, r_ref, t_ref)
    y1 = jnp.where(even[0], near_ref[0:16], back_ref[0:16])
    z1 = jnp.where(even[0], back_ref[0:8], near_ref[0:8])
    y2 = jnp.where(even[0], y_ref[0:80], back_ref[16:96])
    z2 = jnp.where(even[0], back_ref[16:32], z_ref[0:16])
    deep_ref[0:80] = y2
    deep_ref[80:96] = z2
    above = [[above_ref[16 * k : 16 * k + 16] for k in range(4)]]
    below = [[below_ref[16 * k : 16 * k + 16] for k in range(4)]]
    for axis, a, b in ((1, y1, y2[0:16]), (2, z1, z2[0:8])):
        above.append(jnp.where(even[axis], a, b))
        below.append(jnp.where(even[axis], b, a))
    upstream = [[load(g_ref, s, 0)] for s in range(2)]
    middle = [[c[s][0]] for s in range(2)]
    for s in range(2):
        for axis in range(3):
            p, m = 1 + 2 * axis, 2 + 2 * axis
            upstream[s].append(moved(load(g_ref, s, p), axis, 1, above[axis], s))
            upstream[s].append(moved(load(g_ref, s, m), axis, -1, below[axis], s))
            middle[s].append(moved(c[s][p], axis, -1, below[axis], 2 + s))
            middle[s].append(moved(c[s][m], axis, 1, above[axis], 2 + s))
    later = [[[None] * nx for _ in range(7)] for _ in range(2)]
    for x in range(nx):
        up = [[upstream[s][q][x] for q in range(7)] for s in range(2)]
        mid = [[middle[s][q][x] for q in range(7)] for s in range(2)]
        rho = [total(mid[s]) for s in range(2)]
        earlier, rate_part, relax_part = adjoint(up, mid, rho, [inverse[s][x] for s in range(2)], rate[x])
        rate_ref[x] = rate_part
        for s in range(2):
            relax_ref[s, x] = relax_part[s]
            for q in range(7):
                later[s][q][x] = earlier[s][q]
                later_ref[s, q, x] = earlier[s][q]
    for ref, last in ((up_ref, True), (down_ref, False)):
        for s, face in enumerate(pack_x([later[s][2 if last else 1] for s in range(2)], last)):
            ref[16 * s : 16 * s + 16] = face
        ref[32:40] = y2[52:60]
        ref[40:48] = z2[8:16]
    for axis, pack, ref in ((1, pack_y, y1_ref), (2, pack_z, z1_ref)):
        a = pack([later[s][2 + 2 * axis] for s in range(2)], True)
        b = pack([later[s][1 + 2 * axis] for s in range(2)], False)
        ref[0:8] = jnp.where(even[axis], a, b)
    y1_ref[8:16] = z2[8:16]
    z1_ref[8:24] = y2[64:80]
    relay_ref[0:16] = y2[64:80]
    relay_ref[16:24] = z2[8:16]
    relay_ref[24:40] = y2[0:16]
    relay_ref[40:48] = z2[0:8]


def later_beyond(inner, moments, density, inverse, rate):
    scaled = rate * (moments[1] - moments[0])
    return [(1.0 - inverse[s]) * inner[s] + moments[s] * inverse[s] + scaled * density[1 - s] for s in range(2)]


def beyond_y(deep, own, x_above, x_below, z_above, z_below):
    nx = 4
    field = lambda k: deep[16 + nx * k : 16 + nx * k + nx]
    lane = lax.broadcasted_iota(jnp.int32, (nx, 128), 1)
    added = []
    for k in range(4):
        zero = jnp.zeros((nx - 2, 128), jnp.float32)
        x_part = jnp.concatenate([x_below[2 * k + 1 : 2 * k + 2], zero, x_above[2 * k : 2 * k + 1]], axis=0)
        high = pltpu.roll(z_above[nx * k : nx * k + nx], 127, axis=1)
        low = pltpu.roll(z_below[nx * k : nx * k + nx], 1, axis=1)
        z_part = jnp.where(lane == 127, high, jnp.where(lane == 0, low, 0.0))
        added.append(own[nx * k : nx * k + nx] + x_part + z_part)
    moments = [field(2 + s) + WEIGHTS[1] * added[s] for s in range(2)]
    density = [field(4 + s) + added[2 + s] for s in range(2)]
    out = later_beyond([field(0), field(1)], moments, density, [field(6), field(7)], field(8))
    return jnp.concatenate(out, axis=0)


def beyond_z(deep, own, x_above, x_below, y_above, y_below):
    lane = lax.broadcasted_iota(jnp.int32, (8, 128), 1)
    row = lax.broadcasted_iota(jnp.int32, (8, 128), 0)

    def at(v, shift):
        shift = shift % 128
        return pltpu.roll(v, shift, axis=1) if shift else v

    field = lambda k: at(deep, -32 - 8 * k)
    odd = lax.rem(lane, 2) == 1
    y_high, y_low = pltpu.roll(y_above, 7, axis=0), pltpu.roll(y_below, 1, axis=0)
    added = []
    for k in range(4):
        x_part = jnp.where(lane >= 6, at(x_above, 6 - 32 - 8 * k), 0.0)
        x_part = jnp.where(lane < 2, at(x_below, -6 - 32 - 8 * k), x_part)
        y_part = jnp.where((row == 7) & odd, at(y_high, 1 - 8 * k), 0.0)
        y_part = jnp.where((row == 0) & ~odd, at(y_low, -1 - 8 * k), y_part)
        added.append(at(own, -8 * k) + x_part + y_part)
    moments = [field(2 + s) + WEIGHTS[1] * added[s] for s in range(2)]
    density = [field(4 + s) + added[2 + s] for s in range(2)]
    out = later_beyond([field(0), field(1)], moments, density, [field(6), field(7)], field(8))
    return jnp.where(lane < 8, out[0], pltpu.roll(out[1], 8, axis=1))


def z_lines_of(packed, last):
    row, lane = (lax.broadcasted_iota(jnp.int32, (16, 128), d) for d in (0, 1))
    edge = jnp.where(last, packed[7:8], packed[0:1])
    wanted = lane == 2 * row + jnp.where(last, 1, 0)
    return jnp.broadcast_to(jnp.sum(jnp.where(wanted, edge, 0.0), axis=1, keepdims=True), (16, 128))


def y_lines_of(rows, last):
    row, lane = (lax.broadcasted_iota(jnp.int32, (16, 128), d) for d in (0, 1))
    wanted = lane == jnp.where(last, 127, 0)
    edge = jnp.sum(jnp.where(wanted, rows, 0.0), axis=1, keepdims=True)
    return jnp.broadcast_to(jnp.sum(jnp.where(lane // 2 == row, edge, 0.0), axis=0, keepdims=True), (8, 128))


def third_kernel(
    f_ref, r_ref, t_ref, later_ref, rate_late_ref, relax_late_ref, deep_ref, raw_ref, diag_ref,
    below_ref, above_ref, y1_ref, z1_ref, relay_ref, state_ref, rate_ref, relax_ref,
):
    even = parities()
    nx = r_ref.shape[0]
    far_y = far_along_y(lax.axis_index("gy"), lax.axis_size("gy"))
    far_z = far_along_z(lax.axis_index("gz"), lax.axis_size("gz"))
    alike = far_y == far_z
    lines1 = z1_ref[8:24]
    lines2 = jnp.where(far_y, relay_ref[0:16], z_lines_of(relay_ref[40:48], even[1]))
    lines2 = jnp.where(alike, diag_ref[0:16], lines2)
    y2 = beyond_y(
        deep_ref[0:80], raw_ref[0:16], above_ref[32:40], below_ref[32:40],
        jnp.where(even[2], lines1, lines2), jnp.where(even[2], lines2, lines1),
    )
    lines1 = y1_ref[8:16]
    lines2 = jnp.where(far_z, relay_ref[16:24], y_lines_of(relay_ref[24:40], even[2]))
    lines2 = jnp.where(alike, diag_ref[16:24], lines2)
    z2 = beyond_z(
        deep_ref[80:88], raw_ref[16:24], above_ref[40:48], below_ref[40:48],
        jnp.where(even[1], lines1, lines2), jnp.where(even[1], lines2, lines1),
    )
    above = [[above_ref[16 * k : 16 * k + 16] for k in range(2)]]
    below = [[below_ref[16 * k : 16 * k + 16] for k in range(2)]]
    for axis, a, b in ((1, y1_ref[0:8], y2), (2, z1_ref[0:8], z2)):
        above.append(jnp.where(even[axis], a, b))
        below.append(jnp.where(even[axis], b, a))
    upstream = [[load(later_ref, s, 0)] for s in range(2)]
    for s in range(2):
        for axis in range(3):
            upstream[s].append(moved(load(later_ref, s, 1 + 2 * axis), axis, 1, above[axis], s))
            upstream[s].append(moved(load(later_ref, s, 2 + 2 * axis), axis, -1, below[axis], s))
    for x in range(nx):
        up = [[upstream[s][q][x] for q in range(7)] for s in range(2)]
        state = [[f_ref[s, q, x] for q in range(7)] for s in range(2)]
        rho = [total(state[s]) for s in range(2)]
        inverse = [1.0 / t_ref[s, x] for s in range(2)]
        earlier, rate_part, relax_part = adjoint(up, state, rho, inverse, r_ref[x])
        rate_ref[x] = rate_late_ref[x] + rate_part
        for s in range(2):
            relax_ref[s, x] = relax_late_ref[s, x] + relax_part[s]
            for q in range(7):
                state_ref[s, q, x] = earlier[s][q]


def call(kernel, shapes, *args, source=pltpu.VMEM, scratch=()):
    return pl.pallas_call(
        kernel,
        out_shape=[jax.ShapeDtypeStruct(s, jnp.float32) for s in shapes],
        in_specs=[pl.BlockSpec(memory_space=source)] * len(args),
        out_specs=[pl.BlockSpec(memory_space=pltpu.VMEM)] * len(shapes),
        scratch_shapes=list(scratch),
        compiler_params=pltpu.CompilerParams(vmem_limit_bytes=32 * 1024 * 1024),
    )(*args)


def shifts(axis):
    count = lax.axis_size(axis)
    up = [(i, (i + 1) % count) for i in range(count)]
    return up, [(j, i) for i, j in up]


def far_along_y(index, count):
    return (index == 0) | (index == count - 1)


def far_along_z(index, count):
    half = count // 2
    return (index % half == 0) | (index % half == half - 1)


def grid_pairs(move):
    counts = tuple(lax.axis_size(a) for a in AXES)
    nx, ny, nz = counts
    pairs = []
    for x in range(nx):
        for y in range(ny):
            for z in range(nz):
                to = move(x, y, z, counts)
                if to is not None:
                    pairs.append(((x * ny + y) * nz + z, (to[0] * ny + to[1]) * nz + to[2]))
    return pairs


def near_move(x, y, z, counts):
    return (x, partner(y, counts[1], 0), z) if x % 2 == 0 else (x, y, partner(z, counts[2], 0))


def second_y_move(x, y, z, counts):
    return (x, partner(y, counts[1], 1), z) if x % 2 == 0 else None


def second_z_move(x, y, z, counts):
    return (x, y, partner(z, counts[2], 1)) if x % 2 == 1 else None


def diagonal_move(x, y, z, counts):
    if far_along_y(y, counts[1]) == far_along_z(z, counts[2]):
        return (x, partner(y, counts[1], 1), partner(z, counts[2], 1))
    return None


def relay_move(x, y, z, counts):
    far_y, far_z = far_along_y(y, counts[1]), far_along_z(z, counts[2])
    if far_y and not far_z:
        return (x, y, partner(z, counts[2], 1))
    return (x, partner(y, counts[1], 1), z) if far_z and not far_y else None


def first_exchange(up, down, own0, own1, diag):
    to_up, to_down = shifts("gx")
    below = lax.ppermute(up, "gx", to_up)
    above = lax.ppermute(down, "gx", to_down)
    y, near, z = call(forward_kernel, [(160, 128), (40, 128), (32, 128)], own0, own1, below, above)
    z_in = lax.ppermute(z, AXES, grid_pairs(second_z_move))
    y_in = lax.ppermute(y, AXES, grid_pairs(second_y_move))
    diag_in = lax.ppermute(diag, AXES, grid_pairs(diagonal_move))
    near_in = lax.ppermute(near, AXES, grid_pairs(near_move))
    (back,) = call(back_kernel, [(96, 128)], z_in, y_in, near_in)
    back_in = lax.ppermute(back, "gx", axis_pairs("gx", 0))
    return (below, above, z_in, y_in, near_in, back_in), diag_in


def second_exchange(up, down, y1, z1, relay):
    to_up, to_down = shifts("gx")
    return (
        lax.ppermute(up, "gx", to_up),
        lax.ppermute(down, "gx", to_down),
        lax.ppermute(y1, "gy", axis_pairs("gy", 0)),
        lax.ppermute(z1, "gz", axis_pairs("gz", 0)),
        lax.ppermute(relay, AXES, grid_pairs(relay_move)),
    )


def on_device(checkpoint, cotangent, reaction_rate, relax_time):
    inputs = (checkpoint, cotangent, reaction_rate, relax_time)
    messages = [(160, 128), (160, 128), (16, 128), (80, 128), (136, 128), (24, 128)]
    f, g, r, t, *sent, raw = call(
        first_kernel, [a.shape for a in inputs] + messages,
        *(pltpu.with_memory_space_constraint(a, pltpu.HBM) for a in inputs),
        source=pltpu.HBM, scratch=[pltpu.SemaphoreType.DMA((4,))],
    )
    received, diag_in = first_exchange(*sent)
    messages = [(96, 128), (48, 128), (48, 128), (16, 128), (24, 128), (48, 128)]
    later, rate_late, relax_late, deep, *sent = call(
        second_kernel, [f.shape, r.shape, t.shape] + messages, f, g, r, t, *received
    )
    received = second_exchange(*sent)
    return tuple(
        call(
            third_kernel, [f.shape, r.shape, t.shape],
            f, r, t, later, rate_late, relax_late, deep, raw, diag_in, *received,
        )
    )


def solution(mesh):
    placed = (
        P(None, None, "gx", "gy", "gz"),
        P(None, None, "gx", "gy", "gz"),
        P("gx", "gy", "gz"),
        P(None, "gx", "gy", "gz"),
    )
    return jax.shard_map(
        on_device,
        mesh=mesh,
        in_specs=placed,
        out_specs=(P(None, None, "gx", "gy", "gz"), P("gx", "gy", "gz"), P(None, "gx", "gy", "gz")),
        check_vma=False,
    )
```

```python
import jax
import jax.numpy as jnp
from jax import lax
from jax.experimental import pallas as pl
from jax.experimental.pallas import tpu as pltpu
from jax.sharding import PartitionSpec as P

WEIGHTS = (0.25, 0.125, 0.125, 0.125, 0.125, 0.125, 0.125)
AXES = ("gx", "gy", "gz")


def partner(index, count, color):
    if color == 0:
        return index ^ 1
    return (index + 1) % count if index % 2 else (index - 1) % count


def axis_pairs(axis, color):
    count = lax.axis_size(axis)
    return [(i, partner(i, count, color)) for i in range(count)]


def parities():
    return tuple(lax.rem(lax.axis_index(a), 2) == 0 for a in AXES)


def load(ref, *lead):
    return [ref[lead + (x,)] for x in range(ref.shape[len(lead)])]


def total(terms):
    out = terms[0]
    for t in terms[1:]:
        out = out + t
    return out


def collided(f_ref, r_ref, t_ref):
    nx = r_ref.shape[0]
    rate = load(r_ref)
    inverse = [[1.0 / t for t in load(t_ref, s)] for s in range(2)]
    f = [[load(f_ref, s, q) for q in range(7)] for s in range(2)]
    rho = [[total([f[s][q][x] for q in range(7)]) for x in range(nx)] for s in range(2)]
    c = [[[None] * nx for _ in range(7)] for _ in range(2)]
    for x in range(nx):
        reaction = rate[x] * rho[0][x] * rho[1][x]
        for s in range(2):
            source = reaction if s == 1 else -reaction
            for q in range(7):
                w = WEIGHTS[q]
                v = f[s][q][x]
                c[s][q][x] = v - (v - w * rho[s][x]) * inverse[s][x] + w * source
    return c, rho, inverse, rate


def pack_x(fields, last):
    return [v[-1] if last else v[0] for v in fields]


def rows_of(v, i):
    return jnp.concatenate([plane[i : i + 1] for plane in v], axis=0)


def pack_y(fields, last):
    n = fields[0][0].shape[0]
    return jnp.concatenate([rows_of(v, n - 1 if last else 0) for v in fields], axis=0)


def pack_z(fields, last, start=0, out=None):
    lane = lax.broadcasted_iota(jnp.int32, (8, 128), 1)
    out = jnp.zeros((8, 128), jnp.float32) if out is None else out
    j = start
    for v in fields:
        for plane in v:
            for h in range(plane.shape[0] // 8):
                part = plane[8 * h : 8 * h + 8]
                shift = (j + 1) % 128 if last else j
                part = pltpu.roll(part, shift, axis=1) if shift else part
                out = jnp.where(lane == j, part, out)
                j += 1
    return out


def cut(v, axis, sign):
    if axis == 0:
        zero = jnp.zeros_like(v[0])
        return v[1:] + [zero] if sign > 0 else [zero] + v[:-1]
    out = []
    for plane in v:
        n = plane.shape[axis - 1]
        at = lax.broadcasted_iota(jnp.int32, plane.shape, axis - 1)
        rolled = pltpu.roll(plane, n - 1 if sign > 0 else 1, axis=axis - 1)
        out.append(jnp.where(at == (n - 1 if sign > 0 else 0), 0.0, rolled))
    return out


def plus(a, b):
    return [x + y for x, y in zip(a, b)]


def partial_sums(g, c, axes):
    moments, density = [], []
    for s in range(2):
        m = [WEIGHTS[1] * v for v in cut(g[s][1 + 2 * axes[0]], axes[0], 1)]
        d = plus(c[s][0], cut(c[s][1 + 2 * axes[0]], axes[0], -1))
        m = plus(m, [WEIGHTS[1] * v for v in cut(g[s][2 + 2 * axes[0]], axes[0], -1)])
        d = plus(d, cut(c[s][2 + 2 * axes[0]], axes[0], 1))
        m = plus(m, [WEIGHTS[1] * v for v in cut(g[s][1 + 2 * axes[1]], axes[1], 1)])
        d = plus(d, cut(c[s][1 + 2 * axes[1]], axes[1], -1))
        m = plus(m, [WEIGHTS[1] * v for v in cut(g[s][2 + 2 * axes[1]], axes[1], -1)])
        d = plus(d, cut(c[s][2 + 2 * axes[1]], axes[1], 1))
        moments.append(plus(m, [WEIGHTS[0] * v for v in g[s][0]]))
        density.append(d)
    return moments, density


def face_fields(g, c, moments, density, inverse, rate, axis, last):
    out_q, in_q = (1 + 2 * axis, 2 + 2 * axis) if last else (2 + 2 * axis, 1 + 2 * axis)
    sign = -1 if last else 1
    inner = [cut(g[s][in_q], axis, sign) for s in range(2)]
    m = [plus(moments[s], [WEIGHTS[1] * v for v in inner[s]]) for s in range(2)]
    d = [plus(density[s], cut(c[s][out_q], axis, sign)) for s in range(2)]
    return [*inner, *m, *d, *inverse, rate]


def edge_fields(g, c, axis):
    p, m = 1 + 2 * axis, 2 + 2 * axis
    return [(g[0][p], g[0][m]), (g[1][p], g[1][m]), (c[0][m], c[0][p]), (c[1][m], c[1][p])]


def first_kernel(
    f_hbm, g_hbm, r_hbm, t_hbm, f_ref, g_ref, r_ref, t_ref, up_ref, down_ref, own0_ref, own1_ref, diag_ref, raw_ref, sems
):
    copies = [
        pltpu.make_async_copy(a, b, sems.at[i])
        for i, (a, b) in enumerate(((f_hbm, f_ref), (g_hbm, g_ref), (r_hbm, r_ref), (t_hbm, t_ref)))
    ]
    for copy in copies:
        copy.start()
    for i in (0, 2, 3):
        copies[i].wait()
    even = parities()
    c, _, inverse, rate = collided(f_ref, r_ref, t_ref)
    copies[1].wait()
    g = [[load(g_ref, s, q) for q in range(7)] for s in range(2)]
    up, down = [], []
    for axis in range(3):
        p, m = 1 + 2 * axis, 2 + 2 * axis
        up.append([g[0][m], g[1][m], c[0][p], c[1][p]])
        down.append([g[0][p], g[1][p], c[0][m], c[1][m]])
    for k, (u, d) in enumerate(zip(pack_x(up[0], True), pack_x(down[0], False))):
        up_ref[16 * k : 16 * k + 16] = u
        down_ref[16 * k : 16 * k + 16] = d
    nx, n = len(rate), rate[0].shape[0]
    lane = lax.broadcasted_iota(jnp.int32, (nx, 128), 1)
    row = lax.broadcasted_iota(jnp.int32, (n, 128), 0)
    x_edge, y_edge, z_edge = (edge_fields(g, c, axis) for axis in range(3))
    y_faces, z_faces = [], []
    y_sums, z_sums = partial_sums(g, c, (0, 2)), partial_sums(g, c, (0, 1))
    for last in (False, True):
        i = n - 1 if last else 0
        raw = pack_y((up if last else down)[1], last)
        deep = pack_y(face_fields(g, c, *y_sums, inverse, rate, 1, last), last)
        x_lines = [line for a, b in x_edge for line in (a[0][i : i + 1], b[-1][i : i + 1])]
        x_lines.append(jnp.zeros((28 - 4 * len(rate) - len(x_lines), 128), jnp.float32))
        z_lines = [jnp.where(lane < 64, rows_of(a, i), rows_of(b, i)) for a, b in z_edge]
        y_faces.append((raw, jnp.concatenate([raw, deep, *x_lines], axis=0), jnp.concatenate(z_lines, axis=0)))
        raw = pack_z((up if last else down)[2], last)
        deep = pack_z(face_fields(g, c, *z_sums, inverse, rate, 2, last), last, 32, raw)
        y_lines = [[jnp.where(row < 8, u, v) for u, v in zip(a, b)] for a, b in y_edge]
        x_lines = [a[:-1] + b[-1:] for a, b in x_edge]
        z_faces.append((raw, deep, pack_z(y_lines + x_lines, last)))
    y1, y2 = jnp.where(even[1], y_faces[1][0], y_faces[0][0]), jnp.where(even[1], y_faces[0][0], y_faces[1][0])
    z1, z2 = jnp.where(even[2], z_faces[1][0], z_faces[0][0]), jnp.where(even[2], z_faces[0][0], z_faces[1][0])
    y_deep = jnp.where(even[1], y_faces[0][1], y_faces[1][1])
    y_lines = jnp.where(even[1], y_faces[0][2], y_faces[1][2])
    z_deep = jnp.where(even[2], z_faces[0][1], z_faces[1][1])
    z_lines = jnp.where(even[2], z_faces[0][2], z_faces[1][2])
    raw_ref[0:16] = y2
    raw_ref[16:24] = z2
    diag_ref[0:16] = y_lines
    diag_ref[16:24] = z_lines
    rest = diag_ref.shape[0] - 24
    diag_ref[24:] = jnp.zeros((rest, 128), jnp.float32)
    z1 = jnp.concatenate([z1, jnp.zeros_like(z1)], axis=0)
    y_all = jnp.concatenate([y_deep, y_lines], axis=0)
    z_all = jnp.concatenate([z_deep, z_lines, jnp.zeros((y_all.shape[0] - 16, 128), jnp.float32)], axis=0)
    own0_ref[...] = jnp.where(even[0], y1, z1)
    own1_ref[...] = jnp.where(even[0], y_all, z_all)
    for ref in (up_ref, down_ref):
        ref[64:80] = jnp.where(even[0], z1, y1)
        ref[80:160] = jnp.where(even[0], z_all, y_all)


def forward_kernel(own0_ref, own1_ref, below_ref, above_ref, y_ref, z_ref, near_ref):
    even = parities()
    near_ref[0:16] = own0_ref[...]
    near_ref[16:32] = jnp.where(even[0], above_ref[64:80], below_ref[64:80])
    share = jnp.where(even[0], above_ref[80:160], below_ref[80:160])
    y_ref[0:80] = own1_ref[...]
    y_ref[80:160] = share
    z_ref[0:16] = own1_ref[0:16]
    z_ref[16:32] = share[0:16]
    z_ref[32:48] = share[0:16]


def back_kernel(z_ref, y_ref, near_ref, out_ref):
    even = parities()
    out_ref[0:16] = near_ref[16:32]
    out_ref[16:32] = jnp.where(even[0], y_ref[80:96], z_ref[16:32])
    out_ref[32:96] = y_ref[96:160]


def moved(v, axis, sign, halo, k):
    if axis == 0:
        return v[1:] + [halo[k]] if sign > 0 else [halo[k]] + v[:-1]
    nx, (n, lanes) = len(v), v[0].shape
    out = []
    for x in range(nx):
        plane = v[x]
        if axis == 1:
            row = lax.broadcasted_iota(jnp.int32, (n, lanes), 0)
            edge = halo[k * nx + x : k * nx + x + 1]
            rolled = pltpu.roll(plane, n - 1 if sign > 0 else 1, axis=0)
            out.append(jnp.where(row == (n - 1 if sign > 0 else 0), edge, rolled))
        else:
            lane = lax.broadcasted_iota(jnp.int32, (n, lanes), 1)
            parts = []
            for h in range(n // 8):
                j = (k * nx + x) * (n // 8) + h
                shift = (lanes - 1 - j) % lanes if sign > 0 else (lanes - j) % lanes
                parts.append(pltpu.roll(halo, shift, axis=1) if shift else halo)
            edge = jnp.concatenate(parts, axis=0)
            rolled = pltpu.roll(plane, lanes - 1 if sign > 0 else 1, axis=1)
            out.append(jnp.where(lane == (lanes - 1 if sign > 0 else 0), edge, rolled))
    return out


def adjoint(upstream, state, rho, inverse, rate):
    moments = [total([WEIGHTS[q] * upstream[s][q] for q in range(7)]) for s in range(2)]
    contrast = moments[1] - moments[0]
    scaled = rate * contrast
    earlier, relax = [], []
    for s in range(2):
        keep = 1.0 - inverse[s]
        add = moments[s] * inverse[s] + scaled * rho[1 - s]
        earlier.append([keep * upstream[s][q] + add for q in range(7)])
        part = total([upstream[s][q] * (state[s][q] - WEIGHTS[q] * rho[s]) for q in range(7)])
        relax.append(part * inverse[s] * inverse[s])
    return earlier, rho[0] * rho[1] * contrast, relax


def second_kernel(
    f_ref, g_ref, r_ref, t_ref, below_ref, above_ref, z_ref, y_ref, near_ref, back_ref,
    later_ref, rate_ref, relax_ref, deep_ref, up_ref, down_ref, y1_ref, z1_ref, relay_ref,
):
    even = parities()
    nx = r_ref.shape[0]
    c, _, inverse, rate = collided(f_ref, r_ref, t_ref)
    y1 = jnp.where(even[0], near_ref[0:16], back_ref[0:16])
    z1 = jnp.where(even[0], back_ref[0:8], near_ref[0:8])
    y2 = jnp.where(even[0], y_ref[0:80], back_ref[16:96])
    z2 = jnp.where(even[0], back_ref[16:32], z_ref[0:16])
    deep_ref[0:80] = y2
    deep_ref[80:96] = z2
    above = [[above_ref[16 * k : 16 * k + 16] for k in range(4)]]
    below = [[below_ref[16 * k : 16 * k + 16] for k in range(4)]]
    for axis, a, b in ((1, y1, y2[0:16]), (2, z1, z2[0:8])):
        above.append(jnp.where(even[axis], a, b))
        below.append(jnp.where(even[axis], b, a))
    upstream = [[load(g_ref, s, 0)] for s in range(2)]
    middle = [[c[s][0]] for s in range(2)]
    for s in range(2):
        for axis in range(3):
            p, m = 1 + 2 * axis, 2 + 2 * axis
            upstream[s].append(moved(load(g_ref, s, p), axis, 1, above[axis], s))
            upstream[s].append(moved(load(g_ref, s, m), axis, -1, below[axis], s))
            middle[s].append(moved(c[s][p], axis, -1, below[axis], 2 + s))
            middle[s].append(moved(c[s][m], axis, 1, above[axis], 2 + s))
    later = [[[None] * nx for _ in range(7)] for _ in range(2)]
    for x in range(nx):
        up = [[upstream[s][q][x] for q in range(7)] for s in range(2)]
        mid = [[middle[s][q][x] for q in range(7)] for s in range(2)]
        rho = [total(mid[s]) for s in range(2)]
        earlier, rate_part, relax_part = adjoint(up, mid, rho, [inverse[s][x] for s in range(2)], rate[x])
        rate_ref[x] = rate_part
        for s in range(2):
            relax_ref[s, x] = relax_part[s]
            for q in range(7):
                later[s][q][x] = earlier[s][q]
                later_ref[s, q, x] = earlier[s][q]
    for ref, last in ((up_ref, True), (down_ref, False)):
        for s, face in enumerate(pack_x([later[s][2 if last else 1] for s in range(2)], last)):
            ref[16 * s : 16 * s + 16] = face
        ref[32:40] = y2[52:60]
        ref[40:48] = z2[8:16]
    for axis, pack, ref in ((1, pack_y, y1_ref), (2, pack_z, z1_ref)):
        a = pack([later[s][2 + 2 * axis] for s in range(2)], True)
        b = pack([later[s][1 + 2 * axis] for s in range(2)], False)
        ref[0:8] = jnp.where(even[axis], a, b)
    y1_ref[8:16] = z2[8:16]
    z1_ref[8:24] = y2[64:80]
    relay_ref[0:16] = y2[64:80]
    relay_ref[16:24] = z2[8:16]
    relay_ref[24:40] = y2[0:16]
    relay_ref[40:48] = z2[0:8]


def later_beyond(inner, moments, density, inverse, rate):
    scaled = rate * (moments[1] - moments[0])
    return [(1.0 - inverse[s]) * inner[s] + moments[s] * inverse[s] + scaled * density[1 - s] for s in range(2)]


def beyond_y(deep, own, x_above, x_below, z_above, z_below):
    nx = 4
    field = lambda k: deep[16 + nx * k : 16 + nx * k + nx]
    lane = lax.broadcasted_iota(jnp.int32, (nx, 128), 1)
    added = []
    for k in range(4):
        zero = jnp.zeros((nx - 2, 128), jnp.float32)
        x_part = jnp.concatenate([x_below[2 * k + 1 : 2 * k + 2], zero, x_above[2 * k : 2 * k + 1]], axis=0)
        high = pltpu.roll(z_above[nx * k : nx * k + nx], 127, axis=1)
        low = pltpu.roll(z_below[nx * k : nx * k + nx], 1, axis=1)
        z_part = jnp.where(lane == 127, high, jnp.where(lane == 0, low, 0.0))
        added.append(own[nx * k : nx * k + nx] + x_part + z_part)
    moments = [field(2 + s) + WEIGHTS[1] * added[s] for s in range(2)]
    density = [field(4 + s) + added[2 + s] for s in range(2)]
    out = later_beyond([field(0), field(1)], moments, density, [field(6), field(7)], field(8))
    return jnp.concatenate(out, axis=0)


def beyond_z(deep, own, x_above, x_below, y_above, y_below):
    lane = lax.broadcasted_iota(jnp.int32, (8, 128), 1)
    row = lax.broadcasted_iota(jnp.int32, (8, 128), 0)

    def at(v, shift):
        shift = shift % 128
        return pltpu.roll(v, shift, axis=1) if shift else v

    field = lambda k: at(deep, -32 - 8 * k)
    odd = lax.rem(lane, 2) == 1
    y_high, y_low = pltpu.roll(y_above, 7, axis=0), pltpu.roll(y_below, 1, axis=0)
    added = []
    for k in range(4):
        x_part = jnp.where(lane >= 6, at(x_above, 6 - 32 - 8 * k), 0.0)
        x_part = jnp.where(lane < 2, at(x_below, -6 - 32 - 8 * k), x_part)
        y_part = jnp.where((row == 7) & odd, at(y_high, 1 - 8 * k), 0.0)
        y_part = jnp.where((row == 0) & ~odd, at(y_low, -1 - 8 * k), y_part)
        added.append(at(own, -8 * k) + x_part + y_part)
    moments = [field(2 + s) + WEIGHTS[1] * added[s] for s in range(2)]
    density = [field(4 + s) + added[2 + s] for s in range(2)]
    out = later_beyond([field(0), field(1)], moments, density, [field(6), field(7)], field(8))
    return jnp.where(lane < 8, out[0], pltpu.roll(out[1], 8, axis=1))


def z_lines_of(packed, last):
    row, lane = (lax.broadcasted_iota(jnp.int32, (16, 128), d) for d in (0, 1))
    edge = jnp.where(last, packed[7:8], packed[0:1])
    wanted = lane == 2 * row + jnp.where(last, 1, 0)
    return jnp.broadcast_to(jnp.sum(jnp.where(wanted, edge, 0.0), axis=1, keepdims=True), (16, 128))


def y_lines_of(rows, last):
    row, lane = (lax.broadcasted_iota(jnp.int32, (16, 128), d) for d in (0, 1))
    wanted = lane == jnp.where(last, 127, 0)
    edge = jnp.sum(jnp.where(wanted, rows, 0.0), axis=1, keepdims=True)
    return jnp.broadcast_to(jnp.sum(jnp.where(lane // 2 == row, edge, 0.0), axis=0, keepdims=True), (8, 128))


def third_kernel(
    f_ref, r_ref, t_ref, later_ref, rate_late_ref, relax_late_ref, deep_ref, raw_ref, diag_ref,
    below_ref, above_ref, y1_ref, z1_ref, relay_ref, state_hbm, rate_hbm, relax_hbm,
    state_ref, rate_ref, relax_ref, sems,
):
    even = parities()
    nx = r_ref.shape[0]
    far_y = far_along_y(lax.axis_index("gy"), lax.axis_size("gy"))
    far_z = far_along_z(lax.axis_index("gz"), lax.axis_size("gz"))
    alike = far_y == far_z
    lines1 = z1_ref[8:24]
    lines2 = jnp.where(far_y, relay_ref[0:16], z_lines_of(relay_ref[40:48], even[1]))
    lines2 = jnp.where(alike, diag_ref[0:16], lines2)
    y2 = beyond_y(
        deep_ref[0:80], raw_ref[0:16], above_ref[32:40], below_ref[32:40],
        jnp.where(even[2], lines1, lines2), jnp.where(even[2], lines2, lines1),
    )
    lines1 = y1_ref[8:16]
    lines2 = jnp.where(far_z, relay_ref[16:24], y_lines_of(relay_ref[24:40], even[2]))
    lines2 = jnp.where(alike, diag_ref[16:24], lines2)
    z2 = beyond_z(
        deep_ref[80:88], raw_ref[16:24], above_ref[40:48], below_ref[40:48],
        jnp.where(even[1], lines1, lines2), jnp.where(even[1], lines2, lines1),
    )
    above = [[above_ref[16 * k : 16 * k + 16] for k in range(2)]]
    below = [[below_ref[16 * k : 16 * k + 16] for k in range(2)]]
    for axis, a, b in ((1, y1_ref[0:8], y2), (2, z1_ref[0:8], z2)):
        above.append(jnp.where(even[axis], a, b))
        below.append(jnp.where(even[axis], b, a))
    upstream = [[load(later_ref, s, 0)] for s in range(2)]
    for s in range(2):
        for axis in range(3):
            upstream[s].append(moved(load(later_ref, s, 1 + 2 * axis), axis, 1, above[axis], s))
            upstream[s].append(moved(load(later_ref, s, 2 + 2 * axis), axis, -1, below[axis], s))
    copies = []
    for x in range(nx):
        up = [[upstream[s][q][x] for q in range(7)] for s in range(2)]
        state = [[f_ref[s, q, x] for q in range(7)] for s in range(2)]
        rho = [total(state[s]) for s in range(2)]
        inverse = [1.0 / t_ref[s, x] for s in range(2)]
        earlier, rate_part, relax_part = adjoint(up, state, rho, inverse, r_ref[x])
        rate_ref[x] = rate_late_ref[x] + rate_part
        for s in range(2):
            relax_ref[s, x] = relax_late_ref[s, x] + relax_part[s]
            for q in range(7):
                state_ref[s, q, x] = earlier[s][q]
        copies += [
            pltpu.make_async_copy(state_ref.at[:, :, x], state_hbm.at[:, :, x], sems.at[3 * x]),
            pltpu.make_async_copy(rate_ref.at[x], rate_hbm.at[x], sems.at[3 * x + 1]),
            pltpu.make_async_copy(relax_ref.at[:, x], relax_hbm.at[:, x], sems.at[3 * x + 2]),
        ]
        for copy in copies[-3:]:
            copy.start()
    for copy in copies:
        copy.wait()


def call(kernel, shapes, *args, source=pltpu.VMEM, target=pltpu.VMEM, scratch=()):
    return pl.pallas_call(
        kernel,
        out_shape=[jax.ShapeDtypeStruct(s, jnp.float32) for s in shapes],
        in_specs=[pl.BlockSpec(memory_space=source)] * len(args),
        out_specs=[pl.BlockSpec(memory_space=target)] * len(shapes),
        scratch_shapes=list(scratch),
        compiler_params=pltpu.CompilerParams(vmem_limit_bytes=32 * 1024 * 1024),
    )(*args)


def shifts(axis):
    count = lax.axis_size(axis)
    up = [(i, (i + 1) % count) for i in range(count)]
    return up, [(j, i) for i, j in up]


def far_along_y(index, count):
    return (index == 0) | (index == count - 1)


def far_along_z(index, count):
    half = count // 2
    return (index % half == 0) | (index % half == half - 1)


def grid_pairs(move):
    counts = tuple(lax.axis_size(a) for a in AXES)
    nx, ny, nz = counts
    pairs = []
    for x in range(nx):
        for y in range(ny):
            for z in range(nz):
                to = move(x, y, z, counts)
                if to is not None:
                    pairs.append(((x * ny + y) * nz + z, (to[0] * ny + to[1]) * nz + to[2]))
    return pairs


def near_move(x, y, z, counts):
    return (x, partner(y, counts[1], 0), z) if x % 2 == 0 else (x, y, partner(z, counts[2], 0))


def second_y_move(x, y, z, counts):
    return (x, partner(y, counts[1], 1), z) if x % 2 == 0 else None


def second_z_move(x, y, z, counts):
    return (x, y, partner(z, counts[2], 1)) if x % 2 == 1 else None


def diagonal_move(x, y, z, counts):
    if far_along_y(y, counts[1]) == far_along_z(z, counts[2]):
        return (x, partner(y, counts[1], 1), partner(z, counts[2], 1))
    return None


def relay_move(x, y, z, counts):
    far_y, far_z = far_along_y(y, counts[1]), far_along_z(z, counts[2])
    if far_y and not far_z:
        return (x, y, partner(z, counts[2], 1))
    return (x, partner(y, counts[1], 1), z) if far_z and not far_y else None


def first_exchange(up, down, own0, own1, diag):
    to_up, to_down = shifts("gx")
    below = lax.ppermute(up, "gx", to_up)
    above = lax.ppermute(down, "gx", to_down)
    y, z, near = call(forward_kernel, [(160, 128), (48, 128), (32, 128)], own0, own1, below, above)
    z_in = lax.ppermute(z, AXES, grid_pairs(second_z_move))
    y_in = lax.ppermute(y, AXES, grid_pairs(second_y_move))
    diag_in = lax.ppermute(diag, AXES, grid_pairs(diagonal_move))
    near_in = lax.ppermute(near, AXES, grid_pairs(near_move))
    (back,) = call(back_kernel, [(96, 128)], z_in, y_in, near_in)
    back_in = lax.ppermute(back, "gx", axis_pairs("gx", 0))
    return (below, above, z_in, y_in, near_in, back_in), diag_in


def second_exchange(up, down, y1, z1, relay):
    to_up, to_down = shifts("gx")
    return (
        lax.ppermute(up, "gx", to_up),
        lax.ppermute(down, "gx", to_down),
        lax.ppermute(y1, "gy", axis_pairs("gy", 0)),
        lax.ppermute(z1, "gz", axis_pairs("gz", 0)),
        lax.ppermute(relay, AXES, grid_pairs(relay_move)),
    )


def on_device(checkpoint, cotangent, reaction_rate, relax_time):
    inputs = (checkpoint, cotangent, reaction_rate, relax_time)
    messages = [(160, 128), (160, 128), (16, 128), (80, 128), (152, 128), (24, 128)]
    f, g, r, t, *sent, raw = call(
        first_kernel, [a.shape for a in inputs] + messages,
        *(pltpu.with_memory_space_constraint(a, pltpu.HBM) for a in inputs),
        source=pltpu.HBM, scratch=[pltpu.SemaphoreType.DMA((4,))],
    )
    received, diag_in = first_exchange(*sent)
    messages = [(96, 128), (48, 128), (48, 128), (16, 128), (24, 128), (48, 128)]
    later, rate_late, relax_late, deep, *sent = call(
        second_kernel, [f.shape, r.shape, t.shape] + messages, f, g, r, t, *received
    )
    received = second_exchange(*sent)
    return tuple(
        call(
            third_kernel, [f.shape, r.shape, t.shape],
            f, r, t, later, rate_late, relax_late, deep, raw, diag_in, *received, target=pltpu.HBM,
            scratch=[pltpu.VMEM(a.shape, jnp.float32) for a in (f, r, t)] + [pltpu.SemaphoreType.DMA((3 * r.shape[0],))],
        )
    )


def solution(mesh):
    placed = (
        P(None, None, "gx", "gy", "gz"),
        P(None, None, "gx", "gy", "gz"),
        P("gx", "gy", "gz"),
        P(None, "gx", "gy", "gz"),
    )
    return jax.shard_map(
        on_device,
        mesh=mesh,
        in_specs=placed,
        out_specs=(P(None, None, "gx", "gy", "gz"), P("gx", "gy", "gz"), P(None, "gx", "gy", "gz")),
        check_vma=False,
    )
```

```python
import jax
import jax.numpy as jnp
from jax import lax
from jax.experimental import pallas as pl
from jax.experimental.pallas import tpu as pltpu
from jax.sharding import PartitionSpec as P

WEIGHTS = (0.25, 0.125, 0.125, 0.125, 0.125, 0.125, 0.125)
AXES = ("gx", "gy", "gz")


def partner(index, count, color):
    if color == 0:
        return index ^ 1
    return (index + 1) % count if index % 2 else (index - 1) % count


def axis_pairs(axis, color):
    count = lax.axis_size(axis)
    return [(i, partner(i, count, color)) for i in range(count)]


def parities():
    return tuple(lax.rem(lax.axis_index(a), 2) == 0 for a in AXES)


def load(ref, *lead):
    return [ref[lead + (x,)] for x in range(ref.shape[len(lead)])]


def total(terms):
    out = terms[0]
    for t in terms[1:]:
        out = out + t
    return out


def collided(f_ref, r_ref, t_ref):
    nx = r_ref.shape[0]
    rate = load(r_ref)
    inverse = [[1.0 / t for t in load(t_ref, s)] for s in range(2)]
    f = [[load(f_ref, s, q) for q in range(7)] for s in range(2)]
    rho = [[total([f[s][q][x] for q in range(7)]) for x in range(nx)] for s in range(2)]
    c = [[[None] * nx for _ in range(7)] for _ in range(2)]
    for x in range(nx):
        reaction = rate[x] * rho[0][x] * rho[1][x]
        for s in range(2):
            source = reaction if s == 1 else -reaction
            for q in range(7):
                w = WEIGHTS[q]
                v = f[s][q][x]
                c[s][q][x] = v - (v - w * rho[s][x]) * inverse[s][x] + w * source
    return c, rho, inverse, rate


def pack_x(fields, last):
    return [v[-1] if last else v[0] for v in fields]


def rows_of(v, i):
    return jnp.concatenate([plane[i : i + 1] for plane in v], axis=0)


def pack_y(fields, last):
    n = fields[0][0].shape[0]
    return jnp.concatenate([rows_of(v, n - 1 if last else 0) for v in fields], axis=0)


def pack_z(fields, last, start=0, out=None):
    lane = lax.broadcasted_iota(jnp.int32, (8, 128), 1)
    out = jnp.zeros((8, 128), jnp.float32) if out is None else out
    j = start
    for v in fields:
        for plane in v:
            for h in range(plane.shape[0] // 8):
                part = plane[8 * h : 8 * h + 8]
                shift = (j + 1) % 128 if last else j
                part = pltpu.roll(part, shift, axis=1) if shift else part
                out = jnp.where(lane == j, part, out)
                j += 1
    return out


def pack_z_shifted(fields, shift, start=0, out=None):
    lane = lax.broadcasted_iota(jnp.int32, (8, 128), 1)
    out = jnp.zeros((8, 128), jnp.float32) if out is None else out
    j = start
    for v in fields:
        for plane in v:
            for h in range(plane.shape[0] // 8):
                out = jnp.where(lane == j, pltpu.roll(plane[8 * h : 8 * h + 8], shift + j, axis=1), out)
                j += 1
    return out


def choose(flag, a, b):
    return [[jnp.where(flag, x, y) for x, y in zip(u, v)] for u, v in zip(a, b)]


def cut(v, axis, sign):
    if axis == 0:
        zero = jnp.zeros_like(v[0])
        return v[1:] + [zero] if sign > 0 else [zero] + v[:-1]
    out = []
    for plane in v:
        n = plane.shape[axis - 1]
        at = lax.broadcasted_iota(jnp.int32, plane.shape, axis - 1)
        rolled = pltpu.roll(plane, n - 1 if sign > 0 else 1, axis=axis - 1)
        out.append(jnp.where(at == (n - 1 if sign > 0 else 0), 0.0, rolled))
    return out


def plus(a, b):
    return [x + y for x, y in zip(a, b)]


def partial_sums(g, c, axes):
    moments, density = [], []
    for s in range(2):
        m = [WEIGHTS[1] * v for v in cut(g[s][1 + 2 * axes[0]], axes[0], 1)]
        d = plus(c[s][0], cut(c[s][1 + 2 * axes[0]], axes[0], -1))
        m = plus(m, [WEIGHTS[1] * v for v in cut(g[s][2 + 2 * axes[0]], axes[0], -1)])
        d = plus(d, cut(c[s][2 + 2 * axes[0]], axes[0], 1))
        m = plus(m, [WEIGHTS[1] * v for v in cut(g[s][1 + 2 * axes[1]], axes[1], 1)])
        d = plus(d, cut(c[s][1 + 2 * axes[1]], axes[1], -1))
        m = plus(m, [WEIGHTS[1] * v for v in cut(g[s][2 + 2 * axes[1]], axes[1], -1)])
        d = plus(d, cut(c[s][2 + 2 * axes[1]], axes[1], 1))
        moments.append(plus(m, [WEIGHTS[0] * v for v in g[s][0]]))
        density.append(d)
    return moments, density


def face_fields(g, c, moments, density, inverse, rate, axis, last):
    out_q, in_q = (1 + 2 * axis, 2 + 2 * axis) if last else (2 + 2 * axis, 1 + 2 * axis)
    sign = -1 if last else 1
    inner = [cut(g[s][in_q], axis, sign) for s in range(2)]
    m = [plus(moments[s], [WEIGHTS[1] * v for v in inner[s]]) for s in range(2)]
    d = [plus(density[s], cut(c[s][out_q], axis, sign)) for s in range(2)]
    return [*inner, *m, *d, *inverse, rate]


def edge_fields(g, c, axis):
    p, m = 1 + 2 * axis, 2 + 2 * axis
    return [(g[0][p], g[0][m]), (g[1][p], g[1][m]), (c[0][m], c[0][p]), (c[1][m], c[1][p])]


def first_kernel(
    f_hbm, g_hbm, r_hbm, t_hbm, f_ref, g_ref, r_ref, t_ref, up_ref, down_ref, own0_ref, own1_ref, diag_ref, raw_ref, sems
):
    copies = [
        pltpu.make_async_copy(a, b, sems.at[i])
        for i, (a, b) in enumerate(((f_hbm, f_ref), (g_hbm, g_ref), (r_hbm, r_ref), (t_hbm, t_ref)))
    ]
    for copy in copies:
        copy.start()
    for i in (0, 2, 3):
        copies[i].wait()
    even = parities()
    c, _, inverse, rate = collided(f_ref, r_ref, t_ref)
    copies[1].wait()
    g = [[load(g_ref, s, q) for q in range(7)] for s in range(2)]
    up, down = [], []
    for axis in range(3):
        p, m = 1 + 2 * axis, 2 + 2 * axis
        up.append([g[0][m], g[1][m], c[0][p], c[1][p]])
        down.append([g[0][p], g[1][p], c[0][m], c[1][m]])
    for k, (u, d) in enumerate(zip(pack_x(up[0], True), pack_x(down[0], False))):
        up_ref[16 * k : 16 * k + 16] = u
        down_ref[16 * k : 16 * k + 16] = d
    nx, n = len(rate), rate[0].shape[0]
    lane = lax.broadcasted_iota(jnp.int32, (nx, 128), 1)
    row = lax.broadcasted_iota(jnp.int32, (n, 128), 0)
    x_edge, y_edge, z_edge = (edge_fields(g, c, axis) for axis in range(3))
    y_faces, z_faces = [], []
    y_sums, z_sums = partial_sums(g, c, (0, 2)), partial_sums(g, c, (0, 1))
    for last in (False, True):
        i = n - 1 if last else 0
        raw = pack_y((up if last else down)[1], last)
        deep = pack_y(face_fields(g, c, *y_sums, inverse, rate, 1, last), last)
        x_lines = [line for a, b in x_edge for line in (a[0][i : i + 1], b[-1][i : i + 1])]
        x_lines.append(jnp.zeros((28 - 4 * len(rate) - len(x_lines), 128), jnp.float32))
        z_lines = [jnp.where(lane < 64, rows_of(a, i), rows_of(b, i)) for a, b in z_edge]
        y_faces.append((raw, jnp.concatenate([raw, deep, *x_lines], axis=0), jnp.concatenate(z_lines, axis=0)))
        z_faces.append(face_fields(g, c, *z_sums, inverse, rate, 2, last))
    odd = jnp.where(even[2], 0, 1)
    y_lines = [[jnp.where(row < 8, u, v) for u, v in zip(a, b)] for a, b in y_edge]
    x_lines = [a[:-1] + b[-1:] for a, b in x_edge]
    z1 = pack_z_shifted(choose(even[2], up[2], down[2]), 1 - odd)
    z2 = pack_z_shifted(choose(even[2], down[2], up[2]), odd)
    z_deep = pack_z_shifted(choose(even[2], *z_faces), odd, 32, z2)
    z_lines = pack_z_shifted(y_lines + x_lines, odd)
    y1, y2 = jnp.where(even[1], y_faces[1][0], y_faces[0][0]), jnp.where(even[1], y_faces[0][0], y_faces[1][0])
    y_deep = jnp.where(even[1], y_faces[0][1], y_faces[1][1])
    y_lines = jnp.where(even[1], y_faces[0][2], y_faces[1][2])
    raw_ref[0:16] = y2
    raw_ref[16:24] = z2
    diag_ref[0:16] = y_lines
    diag_ref[16:24] = z_lines
    rest = diag_ref.shape[0] - 24
    diag_ref[24:] = jnp.zeros((rest, 128), jnp.float32)
    z1 = jnp.concatenate([z1, jnp.zeros_like(z1)], axis=0)
    y_all = jnp.concatenate([y_deep, y_lines], axis=0)
    z_all = jnp.concatenate([z_deep, z_lines, jnp.zeros((y_all.shape[0] - 16, 128), jnp.float32)], axis=0)
    own0_ref[...] = jnp.where(even[0], y1, z1)
    own1_ref[...] = jnp.where(even[0], y_all, z_all)
    for ref in (up_ref, down_ref):
        ref[64:80] = jnp.where(even[0], z1, y1)
        ref[80:160] = jnp.where(even[0], z_all, y_all)


def forward_kernel(own0_ref, own1_ref, below_ref, above_ref, y_ref, z_ref, near_ref):
    even = parities()
    near_ref[0:16] = own0_ref[...]
    near_ref[16:32] = jnp.where(even[0], above_ref[64:80], below_ref[64:80])
    share = jnp.where(even[0], above_ref[80:160], below_ref[80:160])
    y_ref[0:80] = own1_ref[...]
    y_ref[80:160] = share
    z_ref[0:16] = own1_ref[0:16]
    z_ref[16:32] = share[0:16]
    z_ref[32:48] = share[0:16]


def back_kernel(z_ref, y_ref, near_ref, out_ref):
    even = parities()
    out_ref[0:16] = near_ref[16:32]
    out_ref[16:32] = jnp.where(even[0], y_ref[80:96], z_ref[16:32])
    out_ref[32:96] = y_ref[96:160]


def moved(v, axis, sign, halo, k):
    if axis == 0:
        return v[1:] + [halo[k]] if sign > 0 else [halo[k]] + v[:-1]
    nx, (n, lanes) = len(v), v[0].shape
    out = []
    for x in range(nx):
        plane = v[x]
        if axis == 1:
            row = lax.broadcasted_iota(jnp.int32, (n, lanes), 0)
            edge = halo[k * nx + x : k * nx + x + 1]
            rolled = pltpu.roll(plane, n - 1 if sign > 0 else 1, axis=0)
            out.append(jnp.where(row == (n - 1 if sign > 0 else 0), edge, rolled))
        else:
            lane = lax.broadcasted_iota(jnp.int32, (n, lanes), 1)
            parts = []
            for h in range(n // 8):
                j = (k * nx + x) * (n // 8) + h
                shift = (lanes - 1 - j) % lanes if sign > 0 else (lanes - j) % lanes
                parts.append(pltpu.roll(halo, shift, axis=1) if shift else halo)
            edge = jnp.concatenate(parts, axis=0)
            rolled = pltpu.roll(plane, lanes - 1 if sign > 0 else 1, axis=1)
            out.append(jnp.where(lane == (lanes - 1 if sign > 0 else 0), edge, rolled))
    return out


def adjoint(upstream, state, rho, inverse, rate):
    moments = [total([WEIGHTS[q] * upstream[s][q] for q in range(7)]) for s in range(2)]
    contrast = moments[1] - moments[0]
    scaled = rate * contrast
    earlier, relax = [], []
    for s in range(2):
        keep = 1.0 - inverse[s]
        add = moments[s] * inverse[s] + scaled * rho[1 - s]
        earlier.append([keep * upstream[s][q] + add for q in range(7)])
        part = total([upstream[s][q] * (state[s][q] - WEIGHTS[q] * rho[s]) for q in range(7)])
        relax.append(part * inverse[s] * inverse[s])
    return earlier, rho[0] * rho[1] * contrast, relax


def second_kernel(
    f_ref, g_ref, r_ref, t_ref, below_ref, above_ref, z_ref, y_ref, near_ref, back_ref,
    later_ref, rate_ref, relax_ref, deep_ref, up_ref, down_ref, y1_ref, z1_ref, relay_ref,
):
    even = parities()
    nx = r_ref.shape[0]
    c, _, inverse, rate = collided(f_ref, r_ref, t_ref)
    y1 = jnp.where(even[0], near_ref[0:16], back_ref[0:16])
    z1 = jnp.where(even[0], back_ref[0:8], near_ref[0:8])
    y2 = jnp.where(even[0], y_ref[0:80], back_ref[16:96])
    z2 = jnp.where(even[0], back_ref[16:32], z_ref[0:16])
    deep_ref[0:80] = y2
    deep_ref[80:96] = z2
    above = [[above_ref[16 * k : 16 * k + 16] for k in range(4)]]
    below = [[below_ref[16 * k : 16 * k + 16] for k in range(4)]]
    for axis, a, b in ((1, y1, y2[0:16]), (2, z1, z2[0:8])):
        above.append(jnp.where(even[axis], a, b))
        below.append(jnp.where(even[axis], b, a))
    upstream = [[load(g_ref, s, 0)] for s in range(2)]
    middle = [[c[s][0]] for s in range(2)]
    for s in range(2):
        for axis in range(3):
            p, m = 1 + 2 * axis, 2 + 2 * axis
            upstream[s].append(moved(load(g_ref, s, p), axis, 1, above[axis], s))
            upstream[s].append(moved(load(g_ref, s, m), axis, -1, below[axis], s))
            middle[s].append(moved(c[s][p], axis, -1, below[axis], 2 + s))
            middle[s].append(moved(c[s][m], axis, 1, above[axis], 2 + s))
    later = [[[None] * nx for _ in range(7)] for _ in range(2)]
    for x in range(nx):
        up = [[upstream[s][q][x] for q in range(7)] for s in range(2)]
        mid = [[middle[s][q][x] for q in range(7)] for s in range(2)]
        rho = [total(mid[s]) for s in range(2)]
        earlier, rate_part, relax_part = adjoint(up, mid, rho, [inverse[s][x] for s in range(2)], rate[x])
        rate_ref[x] = rate_part
        for s in range(2):
            relax_ref[s, x] = relax_part[s]
            for q in range(7):
                later[s][q][x] = earlier[s][q]
                later_ref[s, q, x] = earlier[s][q]
    for ref, last in ((up_ref, True), (down_ref, False)):
        for s, face in enumerate(pack_x([later[s][2 if last else 1] for s in range(2)], last)):
            ref[16 * s : 16 * s + 16] = face
        ref[32:40] = y2[52:60]
        ref[40:48] = z2[8:16]
    for axis, pack, ref in ((1, pack_y, y1_ref), (2, pack_z, z1_ref)):
        a = pack([later[s][2 + 2 * axis] for s in range(2)], True)
        b = pack([later[s][1 + 2 * axis] for s in range(2)], False)
        ref[0:8] = jnp.where(even[axis], a, b)
    y1_ref[8:16] = z2[8:16]
    z1_ref[8:24] = y2[64:80]
    relay_ref[0:16] = y2[64:80]
    relay_ref[16:24] = z2[8:16]
    relay_ref[24:40] = y2[0:16]
    relay_ref[40:48] = z2[0:8]


def later_beyond(inner, moments, density, inverse, rate):
    scaled = rate * (moments[1] - moments[0])
    return [(1.0 - inverse[s]) * inner[s] + moments[s] * inverse[s] + scaled * density[1 - s] for s in range(2)]


def beyond_y(deep, own, x_above, x_below, z_above, z_below):
    nx = 4
    field = lambda k: deep[16 + nx * k : 16 + nx * k + nx]
    lane = lax.broadcasted_iota(jnp.int32, (nx, 128), 1)
    added = []
    for k in range(4):
        zero = jnp.zeros((nx - 2, 128), jnp.float32)
        x_part = jnp.concatenate([x_below[2 * k + 1 : 2 * k + 2], zero, x_above[2 * k : 2 * k + 1]], axis=0)
        high = pltpu.roll(z_above[nx * k : nx * k + nx], 127, axis=1)
        low = pltpu.roll(z_below[nx * k : nx * k + nx], 1, axis=1)
        z_part = jnp.where(lane == 127, high, jnp.where(lane == 0, low, 0.0))
        added.append(own[nx * k : nx * k + nx] + x_part + z_part)
    moments = [field(2 + s) + WEIGHTS[1] * added[s] for s in range(2)]
    density = [field(4 + s) + added[2 + s] for s in range(2)]
    out = later_beyond([field(0), field(1)], moments, density, [field(6), field(7)], field(8))
    return jnp.concatenate(out, axis=0)


def beyond_z(deep, own, x_above, x_below, y_above, y_below):
    lane = lax.broadcasted_iota(jnp.int32, (8, 128), 1)
    row = lax.broadcasted_iota(jnp.int32, (8, 128), 0)

    def at(v, shift):
        shift = shift % 128
        return pltpu.roll(v, shift, axis=1) if shift else v

    field = lambda k: at(deep, -32 - 8 * k)
    odd = lax.rem(lane, 2) == 1
    y_high, y_low = pltpu.roll(y_above, 7, axis=0), pltpu.roll(y_below, 1, axis=0)
    added = []
    for k in range(4):
        x_part = jnp.where(lane >= 6, at(x_above, 6 - 32 - 8 * k), 0.0)
        x_part = jnp.where(lane < 2, at(x_below, -6 - 32 - 8 * k), x_part)
        y_part = jnp.where((row == 7) & odd, at(y_high, 1 - 8 * k), 0.0)
        y_part = jnp.where((row == 0) & ~odd, at(y_low, -1 - 8 * k), y_part)
        added.append(at(own, -8 * k) + x_part + y_part)
    moments = [field(2 + s) + WEIGHTS[1] * added[s] for s in range(2)]
    density = [field(4 + s) + added[2 + s] for s in range(2)]
    out = later_beyond([field(0), field(1)], moments, density, [field(6), field(7)], field(8))
    return jnp.where(lane < 8, out[0], pltpu.roll(out[1], 8, axis=1))


def z_lines_of(packed, last):
    row, lane = (lax.broadcasted_iota(jnp.int32, (16, 128), d) for d in (0, 1))
    edge = jnp.where(last, packed[7:8], packed[0:1])
    wanted = lane == 2 * row + jnp.where(last, 1, 0)
    return jnp.broadcast_to(jnp.sum(jnp.where(wanted, edge, 0.0), axis=1, keepdims=True), (16, 128))


def y_lines_of(rows, last):
    row, lane = (lax.broadcasted_iota(jnp.int32, (16, 128), d) for d in (0, 1))
    wanted = lane == jnp.where(last, 127, 0)
    edge = jnp.sum(jnp.where(wanted, rows, 0.0), axis=1, keepdims=True)
    return jnp.broadcast_to(jnp.sum(jnp.where(lane // 2 == row, edge, 0.0), axis=0, keepdims=True), (8, 128))


def third_kernel(
    f_ref, r_ref, t_ref, later_ref, rate_late_ref, relax_late_ref, deep_ref, raw_ref, diag_ref,
    below_ref, above_ref, y1_ref, z1_ref, relay_ref, state_hbm, rate_hbm, relax_hbm,
    state_ref, rate_ref, relax_ref, sems,
):
    even = parities()
    nx = r_ref.shape[0]
    far_y = far_along_y(lax.axis_index("gy"), lax.axis_size("gy"))
    far_z = far_along_z(lax.axis_index("gz"), lax.axis_size("gz"))
    alike = far_y == far_z
    lines1 = z1_ref[8:24]
    lines2 = jnp.where(far_y, relay_ref[0:16], z_lines_of(relay_ref[40:48], even[1]))
    lines2 = jnp.where(alike, diag_ref[0:16], lines2)
    y2 = beyond_y(
        deep_ref[0:80], raw_ref[0:16], above_ref[32:40], below_ref[32:40],
        jnp.where(even[2], lines1, lines2), jnp.where(even[2], lines2, lines1),
    )
    lines1 = y1_ref[8:16]
    lines2 = jnp.where(far_z, relay_ref[16:24], y_lines_of(relay_ref[24:40], even[2]))
    lines2 = jnp.where(alike, diag_ref[16:24], lines2)
    z2 = beyond_z(
        deep_ref[80:88], raw_ref[16:24], above_ref[40:48], below_ref[40:48],
        jnp.where(even[1], lines1, lines2), jnp.where(even[1], lines2, lines1),
    )
    above = [[above_ref[16 * k : 16 * k + 16] for k in range(2)]]
    below = [[below_ref[16 * k : 16 * k + 16] for k in range(2)]]
    for axis, a, b in ((1, y1_ref[0:8], y2), (2, z1_ref[0:8], z2)):
        above.append(jnp.where(even[axis], a, b))
        below.append(jnp.where(even[axis], b, a))
    upstream = [[load(later_ref, s, 0)] for s in range(2)]
    for s in range(2):
        for axis in range(3):
            upstream[s].append(moved(load(later_ref, s, 1 + 2 * axis), axis, 1, above[axis], s))
            upstream[s].append(moved(load(later_ref, s, 2 + 2 * axis), axis, -1, below[axis], s))
    copies = []
    for x in range(nx):
        up = [[upstream[s][q][x] for q in range(7)] for s in range(2)]
        state = [[f_ref[s, q, x] for q in range(7)] for s in range(2)]
        rho = [total(state[s]) for s in range(2)]
        inverse = [1.0 / t_ref[s, x] for s in range(2)]
        earlier, rate_part, relax_part = adjoint(up, state, rho, inverse, r_ref[x])
        rate_ref[x] = rate_late_ref[x] + rate_part
        for s in range(2):
            relax_ref[s, x] = relax_late_ref[s, x] + relax_part[s]
            for q in range(7):
                state_ref[s, q, x] = earlier[s][q]
        copies += [
            pltpu.make_async_copy(state_ref.at[:, :, x], state_hbm.at[:, :, x], sems.at[3 * x]),
            pltpu.make_async_copy(rate_ref.at[x], rate_hbm.at[x], sems.at[3 * x + 1]),
            pltpu.make_async_copy(relax_ref.at[:, x], relax_hbm.at[:, x], sems.at[3 * x + 2]),
        ]
        for copy in copies[-3:]:
            copy.start()
    for copy in copies:
        copy.wait()


def call(kernel, shapes, *args, source=pltpu.VMEM, target=pltpu.VMEM, scratch=()):
    return pl.pallas_call(
        kernel,
        out_shape=[jax.ShapeDtypeStruct(s, jnp.float32) for s in shapes],
        in_specs=[pl.BlockSpec(memory_space=source)] * len(args),
        out_specs=[pl.BlockSpec(memory_space=target)] * len(shapes),
        scratch_shapes=list(scratch),
        compiler_params=pltpu.CompilerParams(vmem_limit_bytes=32 * 1024 * 1024),
    )(*args)


def shifts(axis):
    count = lax.axis_size(axis)
    up = [(i, (i + 1) % count) for i in range(count)]
    return up, [(j, i) for i, j in up]


def far_along_y(index, count):
    return (index == 0) | (index == count - 1)


def far_along_z(index, count):
    half = count // 2
    return (index % half == 0) | (index % half == half - 1)


def grid_pairs(move):
    counts = tuple(lax.axis_size(a) for a in AXES)
    nx, ny, nz = counts
    pairs = []
    for x in range(nx):
        for y in range(ny):
            for z in range(nz):
                to = move(x, y, z, counts)
                if to is not None:
                    pairs.append(((x * ny + y) * nz + z, (to[0] * ny + to[1]) * nz + to[2]))
    return pairs


def near_move(x, y, z, counts):
    return (x, partner(y, counts[1], 0), z) if x % 2 == 0 else (x, y, partner(z, counts[2], 0))


def second_y_move(x, y, z, counts):
    return (x, partner(y, counts[1], 1), z) if x % 2 == 0 else None


def second_z_move(x, y, z, counts):
    return (x, y, partner(z, counts[2], 1)) if x % 2 == 1 else None


def diagonal_move(x, y, z, counts):
    if far_along_y(y, counts[1]) == far_along_z(z, counts[2]):
        return (x, partner(y, counts[1], 1), partner(z, counts[2], 1))
    return None


def relay_move(x, y, z, counts):
    far_y, far_z = far_along_y(y, counts[1]), far_along_z(z, counts[2])
    if far_y and not far_z:
        return (x, y, partner(z, counts[2], 1))
    return (x, partner(y, counts[1], 1), z) if far_z and not far_y else None


def first_exchange(up, down, own0, own1, diag):
    to_up, to_down = shifts("gx")
    below = lax.ppermute(up, "gx", to_up)
    above = lax.ppermute(down, "gx", to_down)
    y, z, near = call(forward_kernel, [(160, 128), (48, 128), (32, 128)], own0, own1, below, above)
    z_in = lax.ppermute(z, AXES, grid_pairs(second_z_move))
    y_in = lax.ppermute(y, AXES, grid_pairs(second_y_move))
    diag_in = lax.ppermute(diag, AXES, grid_pairs(diagonal_move))
    near_in = lax.ppermute(near, AXES, grid_pairs(near_move))
    (back,) = call(back_kernel, [(96, 128)], z_in, y_in, near_in)
    back_in = lax.ppermute(back, "gx", axis_pairs("gx", 0))
    return (below, above, z_in, y_in, near_in, back_in), diag_in


def second_exchange(up, down, y1, z1, relay):
    to_up, to_down = shifts("gx")
    return (
        lax.ppermute(up, "gx", to_up),
        lax.ppermute(down, "gx", to_down),
        lax.ppermute(y1, "gy", axis_pairs("gy", 0)),
        lax.ppermute(z1, "gz", axis_pairs("gz", 0)),
        lax.ppermute(relay, AXES, grid_pairs(relay_move)),
    )


def on_device(checkpoint, cotangent, reaction_rate, relax_time):
    inputs = (checkpoint, cotangent, reaction_rate, relax_time)
    messages = [(160, 128), (160, 128), (16, 128), (80, 128), (152, 128), (24, 128)]
    f, g, r, t, *sent, raw = call(
        first_kernel, [a.shape for a in inputs] + messages,
        *(pltpu.with_memory_space_constraint(a, pltpu.HBM) for a in inputs),
        source=pltpu.HBM, scratch=[pltpu.SemaphoreType.DMA((4,))],
    )
    received, diag_in = first_exchange(*sent)
    messages = [(96, 128), (48, 128), (48, 128), (16, 128), (24, 128), (48, 128)]
    later, rate_late, relax_late, deep, *sent = call(
        second_kernel, [f.shape, r.shape, t.shape] + messages, f, g, r, t, *received
    )
    received = second_exchange(*sent)
    return tuple(
        call(
            third_kernel, [f.shape, r.shape, t.shape],
            f, r, t, later, rate_late, relax_late, deep, raw, diag_in, *received, target=pltpu.HBM,
            scratch=[pltpu.VMEM(a.shape, jnp.float32) for a in (f, r, t)] + [pltpu.SemaphoreType.DMA((3 * r.shape[0],))],
        )
    )


def solution(mesh):
    placed = (
        P(None, None, "gx", "gy", "gz"),
        P(None, None, "gx", "gy", "gz"),
        P("gx", "gy", "gz"),
        P(None, "gx", "gy", "gz"),
    )
    return jax.shard_map(
        on_device,
        mesh=mesh,
        in_specs=placed,
        out_specs=(P(None, None, "gx", "gy", "gz"), P("gx", "gy", "gz"), P(None, "gx", "gy", "gz")),
        check_vma=False,
    )
```
